128 devices in a mesh: grp: 2 (over x_lo), row: 8 (over y, core), col: 8 (over x_hi, z).
Axes of the slice: x: 4 (x_hi: 2, x_lo: 2; x = x_hi * 2 + x_lo), y: 4, z: 4, core: 2. Of those that a mesh axis runs over, the one named last changes fastest.
Arguments:
- pair_state: bfloat16 [768, 768, 128], P(('grp', 'row'), 'col'), may hold values from -6 to 6
- pair_mask: int32 [768], replicated, may hold values 0 or 1
- chain_ids: int32 [768], replicated, may hold values from 0 to 3, never falling along the last dimension, each value on 1 to 384 neighbouring positions
- tokens: bfloat16 [48, 768, 768], P(('grp', 'row')), may hold values from -6 to 6
- grad_attn: bfloat16 [48, 768, 768], P(('grp', 'row')), may hold values from -192 to 192
- norm_pair: bfloat16 [128], replicated, may hold values from 0.099609375 to 1.8984375
- proj_left: bfloat16 [128, 128], replicated, may hold values from -0.5 to 0.5
- gate_left: bfloat16 [128, 128], replicated, may hold values from -0.5 to 0.5
- proj_right: bfloat16 [128, 128], replicated, may hold values from -0.5 to 0.5
- gate_right: bfloat16 [128, 128], replicated, may hold values from -0.5 to 0.5
- gate_out: bfloat16 [128, 128], replicated, may hold values from -0.5 to 0.5
- norm_tri: bfloat16 [128], replicated, may hold values from 0.099609375 to 1.8984375
- tri_out: bfloat16 [128, 128], replicated, may hold values from -1.0546875 to 1.0546875
- norm_bias: bfloat16 [128], replicated, may hold values from 0.099609375 to 1.8984375
- bias_proj: bfloat16 [128, 16], replicated, may hold values from -0.5 to 0.5
- chain_weight: float32 [16], replicated, may hold values from -2 to 2
- norm_tokens: bfloat16 [768], replicated, may hold values from 0.099609375 to 1.8984375
- w_query: bfloat16 [768, 768], P(None, 'col'), may hold values from -0.21875 to 0.21875
- w_key: bfloat16 [768, 768], P(None, 'col'), may hold values from -0.21875 to 0.21875
- w_value: bfloat16 [768, 768], P(None, 'col'), may hold values from -0.21875 to 0.21875
- w_out: bfloat16 [768, 768], P('col'), may hold values from -0.21875 to 0.21875
- norm_ff: bfloat16 [768], replicated, may hold values from 0.099609375 to 1.8984375
- ff_gate: bfloat16 [768, 1536], replicated, may hold values from -0.21875 to 0.21875
- ff_up: bfloat16 [768, 1536], replicated, may hold values from -0.21875 to 0.21875
- ff_down: bfloat16 [1536, 768], replicated, may hold values from -0.15625 to 0.15625
Outputs:
- pair_out: float32 [768, 768, 128], P(('grp', 'row'), 'col')
- refined: float32 [48, 768, 768], P(('grp', 'row'), 'col')
- pair_grad: float32 [768, 768, 128], P(('grp', 'row'), 'col')
The draws below stay inside these ranges and needn't reach their ends.
All inputs are finite; a program needn't handle non-finite values.
Results may differ from the reference program's by a relative error of at most 0.03.
Values may be sent and summed in bfloat16 or wider, within the bound.
No kernel may reach another device: no remote copies, remote signals or barrier semaphores. Data moves between devices by JAX's collectives and lax.ppermute only.
A program may use at most 192 MiB of HBM per device.

```python
import math
import jax
import jax.numpy as jnp
import numpy as np
from jax import lax

C = 128
D = 768
H = 16
HD = 48
FFW = 1536
N = 768
S = 48
N_COL = 8


def place_ends(array, own_key, least, top_value):
    dims = array.shape
    spot = [jax.random.randint(jax.random.fold_in(own_key, axis), (), 0, dims[axis]) for axis in range(len(dims))]
    array = array.at[tuple(spot)].set(least)
    longest = dims.index(max(dims))
    spot[longest] = (spot[longest] + 1) % dims[longest]
    return array.at[tuple(spot)].set(top_value)


def block_scale(rng, extent, split, smallest, top_value):
    def one(position, blocks):
        draws = jax.random.uniform(jax.random.fold_in(jax.random.fold_in(rng, 6), position), (blocks,), jnp.float32, smallest / len(split), top_value / len(split))
        return jnp.repeat(jnp.exp(draws), extent[position] // blocks).reshape((-1,) + (1,) * (len(extent) - position - 1))

    loudness = one(*split[0])
    for cut in split[1:]:
        loudness = loudness * one(*cut)
    return loudness


def length_profile(count, total, limit, slope):
    portions = [(1 << 20) // math.isqrt(grade ** slope) + 1 for grade in range(2, count + 1)]
    rest, given = total - limit - (count - 1), [1] * (count - 1)
    while rest > 0:
        candidates = [i for i in range(count - 1) if given[i] < limit]
        pool, remaining = sum([portions[i] for i in candidates]), rest
        for i in candidates:
            more = min(limit - given[i], max(1, remaining * portions[i] // pool), rest)
            given[i] = given[i] + more
            rest = rest - more
    return np.array([limit] + given)


def ragged_sizes(rng, amount, total, limit, slope):
    if amount == 2:
        one = jax.random.randint(rng, (), max(1, total - limit), min(limit, total - 1) + 1)
        return jnp.stack([one, total - one])
    lengths = jnp.asarray(length_profile(amount, total, limit, slope), jnp.int32)
    couples = (amount - 1) // 2
    giver, taker = lengths[1:1 + 2 * couples:2], lengths[2:2 + 2 * couples:2]
    slack = jnp.minimum(giver - 1, limit - taker)
    moved = jax.random.randint(jax.random.fold_in(rng, 1), (couples,), 0, 1 << 20) % (slack + 1)
    lengths = lengths.at[1:1 + 2 * couples:2].set(giver - moved).at[2:2 + 2 * couples:2].set(taker + moved)
    return lengths[jax.random.permutation(jax.random.fold_in(rng, 2), amount)]


def scatter_about(stream_key, dims, scale, bound, split=(), held_as=jnp.bfloat16):
    loudness = block_scale(stream_key, dims, split, -0.22, 0.18) if split else 1.0
    drawn = jax.random.normal(stream_key, dims, jnp.float32) * scale * loudness
    return jnp.minimum(jnp.maximum(drawn, -bound), bound).astype(held_as)


def setup_inputs(seed: int = 0) -> dict:
    key_list = jax.random.split(jax.random.key(seed), 26)
    return {
        "pair_state": scatter_about(key_list[0], (N, N, C), 1.0, 6.0, ((0, 16), (1, 8))),
        "pair_mask": place_ends((jax.random.randint(key_list[1], (N,), 0, 8) < 7).astype(jnp.int32), jax.random.fold_in(key_list[1], 1), 0, 1),
        "chain_ids": jnp.searchsorted(jnp.cumsum(ragged_sizes(key_list[2], 4, N, N // 2, 0)), jnp.arange(N), side="right").astype(jnp.int32),
        "tokens": scatter_about(key_list[3], (S, N, D), 1.0, 6.0, ((0, 16),)),
        "grad_attn": scatter_about(key_list[4], (S, N, D), 32.0, 192.0, ((0, 16),)),
        "norm_pair": jnp.clip(1.0 + 0.18 * jax.random.normal(key_list[5], (C,), jnp.float32), 0.099609375, 1.8984375).astype(jnp.bfloat16),
        "proj_left": scatter_about(key_list[6], (C, C), C ** -0.5, 0.5),
        "gate_left": scatter_about(key_list[7], (C, C), C ** -0.5, 0.5),
        "proj_right": scatter_about(key_list[8], (C, C), C ** -0.5, 0.5),
        "gate_right": scatter_about(key_list[9], (C, C), C ** -0.5, 0.5),
        "gate_out": scatter_about(key_list[10], (C, C), C ** -0.5, 0.5),
        "norm_tri": jnp.clip(1.0 + 0.18 * jax.random.normal(key_list[11], (C,), jnp.float32), 0.099609375, 1.8984375).astype(jnp.bfloat16),
        "tri_out": scatter_about(key_list[12], (C, C), (2.0 * C ** -0.5), 1.0546875),
        "norm_bias": jnp.clip(1.0 + 0.18 * jax.random.normal(key_list[13], (C,), jnp.float32), 0.099609375, 1.8984375).astype(jnp.bfloat16),
        "bias_proj": scatter_about(key_list[14], (C, H), C ** -0.5, 0.5),
        "chain_weight": jnp.clip(jax.random.uniform(key_list[15], (H,), jnp.float32, -2.0, 2.0), -2.0, 2.0),
        "norm_tokens": jnp.clip(1.0 + 0.18 * jax.random.normal(key_list[16], (D,), jnp.float32), 0.099609375, 1.8984375).astype(jnp.bfloat16),
        "w_query": scatter_about(key_list[17], (D, D), D ** -0.5, 0.21875, ((1, 8),)),
        "w_key": scatter_about(key_list[18], (D, D), D ** -0.5, 0.21875, ((1, 8),)),
        "w_value": scatter_about(key_list[19], (D, D), D ** -0.5, 0.21875, ((1, 8),)),
        "w_out": scatter_about(key_list[20], (D, D), D ** -0.5, 0.21875, ((0, 8),)),
        "norm_ff": jnp.clip(1.0 + 0.18 * jax.random.normal(key_list[21], (D,), jnp.float32), 0.099609375, 1.8984375).astype(jnp.bfloat16),
        "ff_gate": scatter_about(key_list[22], (D, FFW), D ** -0.5, 0.21875),
        "ff_up": scatter_about(key_list[23], (D, FFW), D ** -0.5, 0.21875),
        "ff_down": scatter_about(key_list[24], (FFW, D), FFW ** -0.5, 0.15625),
    }


def layer_norm(value_rows, gain_vec):
    middle = value_rows - lax.optimization_barrier(jnp.mean(value_rows, axis=-1, keepdims=True))
    spread = lax.optimization_barrier(jnp.mean(middle * middle, axis=-1, keepdims=True))
    return middle * lax.rsqrt(spread + 1e-05) * gain_vec.astype(jnp.float32)

def matmul(left_side, right_side):
    return jnp.dot(left_side, right_side, preferred_element_type=jnp.float32)

def rounded_values(value_rows):
    return lax.optimization_barrier(value_rows.astype(jnp.bfloat16)).astype(jnp.float32)

def reference(pair_state, pair_mask, chain_ids, tokens, grad_attn, norm_pair, proj_left, gate_left, proj_right, gate_right, gate_out, norm_tri, tri_out, norm_bias, bias_proj, chain_weight, norm_tokens, w_query, w_key, w_value, w_out, norm_ff, ff_gate, ff_up, ff_down):
    highest_precision = lax.Precision.HIGHEST
    pair_float = pair_state.astype(jnp.float32)
    normed = layer_norm(pair_float, norm_pair).astype(jnp.bfloat16).reshape(N * N, C)
    mask_float = pair_mask.astype(jnp.float32)
    both_mask = (mask_float[:, None] * mask_float[None, :])[:, :, None]
    left_all = (jax.nn.sigmoid(matmul(normed, gate_left)) * matmul(normed, proj_left)).reshape(N, N, C)
    left_all = (left_all * both_mask).astype(jnp.bfloat16)
    right_all = (jax.nn.sigmoid(matmul(normed, gate_right)) * matmul(normed, proj_right)).reshape(N, N, C)
    right_all = (right_all * both_mask).astype(jnp.bfloat16)
    block_size = N // N_COL
    tri_total = jnp.zeros((N, N, C), jnp.float32)
    for piece_index in range(N_COL):
        left_part = left_all[:, piece_index * block_size:(piece_index + 1) * block_size].astype(jnp.float32)
        right_part = right_all[:, piece_index * block_size:(piece_index + 1) * block_size].astype(jnp.float32)
        partial_sum = jnp.einsum('ikc,jkc->ijc', left_part, right_part, precision=highest_precision)
        tri_total = tri_total + rounded_values(partial_sum)
    tri_normed = layer_norm(tri_total, norm_tri).astype(jnp.bfloat16).reshape(N * N, C)
    update = jax.nn.sigmoid(matmul(normed, gate_out)) * matmul(tri_normed, tri_out)
    pair_out = pair_float + update.reshape(N, N, C)
    bias_in = layer_norm(pair_out, norm_bias).astype(jnp.bfloat16).reshape(N * N, C)
    pair_bias = matmul(bias_in, bias_proj).astype(jnp.bfloat16).reshape(N, N, H)
    same_chain = (chain_ids[:, None] == chain_ids[None, :]).astype(jnp.float32)
    extra_terms = jnp.transpose(pair_bias.astype(jnp.float32), (2, 0, 1)) + chain_weight.astype(jnp.float32)[:, None, None] * same_chain[None]
    score_scale = HD ** (-0.5)

    def one_sample(carry, inputs):
        token_row, grad_row = inputs
        token_float = token_row.astype(jnp.float32)
        token_norm = layer_norm(token_float, norm_tokens).astype(jnp.bfloat16)
        query_rows = matmul(token_norm, w_query).astype(jnp.bfloat16).reshape(N, H, HD).astype(jnp.float32)
        key_rows = matmul(token_norm, w_key).astype(jnp.bfloat16).reshape(N, H, HD).astype(jnp.float32)
        value_rows = matmul(token_norm, w_value).astype(jnp.bfloat16).reshape(N, H, HD).astype(jnp.float32)
        logit_scores = jnp.einsum('twi,fwi->wtf', query_rows, key_rows, precision=highest_precision) * score_scale + extra_terms
        weights = jnp.exp(logit_scores)
        probabilities = weights / lax.optimization_barrier(jnp.sum(weights, axis=-1, keepdims=True))
        mixed_output = jnp.einsum('bgy,ybx->gbx', rounded_values(probabilities), value_rows, precision=highest_precision)
        mixed_output = mixed_output.astype(jnp.bfloat16).reshape(N, D)
        state = token_float + matmul(mixed_output, w_out)
        ff_in = layer_norm(state, norm_ff).astype(jnp.bfloat16)
        hidden = (jax.nn.silu(matmul(ff_in, ff_gate)) * matmul(ff_in, ff_up)).astype(jnp.bfloat16)
        refined_row = state + matmul(hidden, ff_down)
        head_gradient = jnp.dot(grad_row, w_out.T, preferred_element_type=jnp.float32)
        head_gradient = head_gradient.astype(jnp.bfloat16).reshape(N, H, HD).astype(jnp.float32)
        probability_gradient = jnp.einsum('twi,fwi->wtf', head_gradient, value_rows, precision=highest_precision)
        score_grad = probabilities * (probability_gradient - lax.optimization_barrier(jnp.sum(probabilities * probability_gradient, axis=-1, keepdims=True)))
        return (carry + score_grad, refined_row)
    bias_grad, refined = lax.scan(one_sample, jnp.zeros((H, N, N), jnp.float32), (tokens, grad_attn))
    flat_grad = jnp.transpose(bias_grad, (1, 2, 0)).reshape(N * N, H)
    pair_grad = jnp.dot(flat_grad, bias_proj.astype(jnp.float32).T, precision=highest_precision).reshape(N, N, C)
    return (pair_out, refined, pair_grad)
```

```python
import functools
import jax
import jax.numpy as jnp
from jax import lax
from jax.experimental import pallas as pl
from jax.experimental.pallas import tpu as pltpu
from jax.sharding import Mesh, PartitionSpec as P

HD = 48
F32 = jnp.float32
BF16 = jnp.bfloat16
ROWS = ("grp", "y", "core")
COLS = ("xh", "z")
ALL = ROWS + COLS
LOG2E = 1.4426950408889634
VMEM_LIMIT = 44 * 1024 * 1024


def layer_norm(value_rows, gain_vec):
    middle = value_rows - jnp.mean(value_rows, axis=-1, keepdims=True)
    spread = jnp.mean(middle * middle, axis=-1, keepdims=True)
    return middle * lax.rsqrt(spread + 1e-05) * gain_vec.astype(F32)


def matmul(left_side, right_side):
    return jnp.dot(left_side, right_side, preferred_element_type=F32)


def dot_nt(a, b):
    return lax.dot_general(a, b, (((1,), (1,)), ((), ())), preferred_element_type=F32)


def dot_tn(a, b):
    return lax.dot_general(a, b, (((0,), (0,)), ((), ())), preferred_element_type=F32)


def lanes_of(rows):
    return lax.broadcasted_iota(jnp.int32, (rows, 128), 1)


def roll(value, shift):
    shift = shift % 128
    return value if shift == 0 else pltpu.roll(value, shift, 1)


def call(kernel, outs, args, scratch, name, flops=0, nbytes=0):
    return pl.pallas_call(
        kernel,
        out_shape=outs,
        in_specs=[pl.BlockSpec(memory_space=pltpu.VMEM)] * len(args),
        out_specs=jax.tree.map(lambda _: pl.BlockSpec(memory_space=pltpu.VMEM), outs),
        scratch_shapes=scratch,
        compiler_params=pltpu.CompilerParams(vmem_limit_bytes=VMEM_LIMIT),
        cost_estimate=pl.CostEstimate(flops=flops, bytes_accessed=nbytes, transcendentals=0),
        name=name,
    )(*args)


def project_kernel(pair_ref, gain_ref, w_ref, mask_ref, out_ref, normed_ref, scr):
    gain = gain_ref[...]

    def norm_block(block, carry):
        rows = pl.ds(pl.multiple_of(block * 512, 512), 512)
        normed_ref[rows, :] = layer_norm(pair_ref[rows, :].astype(F32), gain).astype(BF16)
        return carry

    lax.fori_loop(0, 9, norm_block, 0)
    low = lanes_of(128) < 64
    weights = w_ref[...]

    def rows_at(i, start, size):
        return normed_ref[pl.ds(pl.multiple_of(i * 96 + start, 32), size), :]

    def chunk(i, carry):
        wide = [rows_at(i, 0, 64), rows_at(i + 24, 0, 64)]
        thin = [rows_at(i, 64, 32), rows_at(i + 24, 64, 32)]
        y = dot_nt(weights, jnp.concatenate(wide + thin + thin, axis=0))
        left = y[0:128, 0:128] * jax.nn.sigmoid(y[256:384, 0:128])
        right = y[128:256, 0:128] * jax.nn.sigmoid(y[384:512, 0:128])
        both_p = jnp.where(low, y[0:128, 128:256], y[128:256, 128:256])
        both_g = jnp.where(low, y[256:384, 128:256], y[384:512, 128:256])
        scr[pl.ds(i, 128, stride=72), :] = left
        scr[pl.ds(i + 24, 128, stride=72), :] = right
        scr[pl.ds(i + 48, 128, stride=72), :] = both_p * jax.nn.sigmoid(both_g)
        return carry

    lax.fori_loop(0, 24, chunk, 0)
    mask = mask_ref[...]

    def write(c, carry):
        rows = pl.ds(pl.multiple_of(c * 576, 576), 576)
        out_ref[pl.ds(c * 8, 8)] = (scr[rows, :].reshape(8, 72, 128) * mask[None]).astype(BF16)
        return carry

    lax.fori_loop(0, 16, write, 0)


def unpack_wide(first, second, low):
    top = jnp.where(low, first, roll(second, 64))
    bottom = jnp.where(low, roll(first, 64), second)
    return top, bottom


def product_kernel(in_ref, out_ref, l_scr, r_scr):
    lane = lanes_of(384)
    low = lane < 64

    def put(dst, column, full):
        full = full.reshape(768, 128).astype(BF16)
        if dst is l_scr:
            dst[:, column : column + 128] = full
        else:
            for q in range(8):
                dst[64 * q : 64 * q + 64, column : column + 128] = full[96 * q : 96 * q + 64]
                dst[512 + 32 * q : 544 + 32 * q, column : column + 128] = full[96 * q + 64 : 96 * q + 96]

    def stack(halves):
        return jnp.concatenate([h.reshape(16, 24, 128) for h in halves], axis=1)

    def part(value, start):
        return value[:, start : start + 24].reshape(384, 128)

    for u in range(2):
        blocks = [in_ref[:, 4 * u + v].astype(F32) for v in range(4)]
        for p in range(2):
            for dst, start in ((l_scr, 0), (r_scr, 24)):
                halves = unpack_wide(part(blocks[2 * p], start), part(blocks[2 * p + 1], start), low)
                put(dst, (2 * u + p) * 128, stack(halves))
        thin = [part(b, 48) for b in blocks]
        for dst, base in ((l_scr, 0), (r_scr, 2)):
            halves = []
            for a in range(2):
                parts = [roll(thin[v], 32 * (v - base - a)) for v in range(4)]
                lower = jnp.where(lane < 32, parts[0], parts[1])
                upper = jnp.where(lane < 96, parts[2], parts[3])
                halves.append(jnp.where(low, lower, upper))
            put(dst, 512 + u * 128, stack(halves))
    for b in range(4):
        product = dot_nt(l_scr[192 * b : 192 * b + 192, :], r_scr[...])
        pack_rows(product, out_ref, 4 * b, 4)


def pack_rows(full, out_ref, first, count):
    low = lanes_of(count * 24) < 64
    lane = lanes_of(count * 16)
    for q in range(8):
        tile = full[:, 128 * (q // 2) : 128 * (q // 2) + 128].reshape(count, 48, 128)
        top = tile[:, 0:24].reshape(count * 24, 128)
        bottom = tile[:, 24:48].reshape(count * 24, 128)
        if q % 2 == 0:
            wide = jnp.where(low, top, roll(bottom, 64))
        else:
            wide = jnp.where(low, roll(top, 64), bottom)
        tile = full[:, 512 + 128 * (q // 4) : 640 + 128 * (q // 4)].reshape(count, 48, 128)
        thin = [
            roll(tile[:, 16 * m : 16 * m + 16].reshape(count * 16, 128), 32 * (m - q % 4))
            for m in range(3)
        ]
        thin = jnp.where(lane < 32, thin[0], jnp.where(lane < 64, thin[1], thin[2]))
        piece = jnp.concatenate(
            [wide.reshape(count, 24, 128), thin.reshape(count, 16, 128)], axis=1
        )
        out_ref[pl.ds(first, count), q] = piece.astype(BF16)


def update_kernel(
    t_ref, pair_ref, gate_ref, w_ref, tri_gain_ref, bias_gain_ref, bp_ref, out_ref, bias_ref, scr, b_scr
):
    def spread(c, carry):
        rows = pl.ds(pl.multiple_of(c * 640, 640), 640)
        scr[rows, :] = t_ref[pl.ds(c * 16, 16)].astype(F32).reshape(640, 128)
        return carry

    lax.fori_loop(0, 8, spread, 0)
    weight = w_ref[...]
    tri_gain = tri_gain_ref[...]
    bias_gain = bias_gain_ref[...]
    bias_proj = bp_ref[...]

    def step(position, places):
        tri = scr[pl.ds(position, 128, stride=40), :]
        middle = tri - jnp.mean(tri, axis=0, keepdims=True)
        spread_of = jnp.mean(middle * middle, axis=0, keepdims=True)
        tri_normed = (middle * lax.rsqrt(spread_of + 1e-05) * tri_gain).astype(BF16)
        update = dot_tn(tri_normed, weight)
        fed = []
        at = 0
        for start, size in places:
            rows = pl.ds(pl.multiple_of(start, 32), size)
            new = pair_ref[rows, :].astype(F32) + gate_ref[rows, :] * update[at : at + size]
            out_ref[rows, :] = new
            fed.append(layer_norm(new, bias_gain).astype(BF16))
            at += size
        if at < 128:
            fed.append(fed[-1])
        b_scr[pl.ds(position, 16, stride=40), :] = dot_nt(bias_proj, jnp.concatenate(fed, axis=0))

    def wide(i, carry):
        step(i, [(96 * i, 64), (96 * (i + 24), 64)])
        return carry

    def thin(i, carry):
        step(i + 24, [(96 * (i + 16 * m) + 64, 32) for m in range(3)])
        return carry

    lax.fori_loop(0, 24, wide, 0)
    lax.fori_loop(0, 16, thin, 0)
    bias = b_scr[...].reshape(16, 40, 128).astype(BF16)
    for copy in range(8):
        bias_ref[copy] = bias


def attention_kernel(
    bias_ref, q_ref, k_ref, v_ref, g_ref, chain_row_ref, chain_col_ref, weight_ref,
    mixed_ref, grad_ref, bias_scr, acc,
):
    low = lanes_of(384) < 64
    lane = lanes_of(256)
    head_weight = weight_ref[...] * LOG2E

    def put(column, full):
        same = chain_row_ref[...] == chain_col_ref[:, column : column + 128]
        bias_scr[:, column : column + 128] = full.reshape(768, 128) * LOG2E + jnp.where(
            same, head_weight, 0.0
        )

    for u in range(2):
        blocks = [bias_ref[:, 4 * u + v].astype(F32) for v in range(4)]
        for p in range(2):
            halves = unpack_wide(
                blocks[2 * p][:, 0:24].reshape(384, 128),
                blocks[2 * p + 1][:, 0:24].reshape(384, 128),
                low,
            )
            put((2 * u + p) * 128, jnp.concatenate([h.reshape(16, 24, 128) for h in halves], axis=1))
        thin = [b[:, 24:40].reshape(256, 128) for b in blocks]
        thirds = []
        for m in range(3):
            parts = [roll(thin[v], 32 * (v - m)) for v in range(4)]
            lower = jnp.where(lane < 32, parts[0], parts[1])
            upper = jnp.where(lane < 96, parts[2], parts[3])
            thirds.append(jnp.where(lane < 64, lower, upper).reshape(16, 16, 128))
        put(512 + u * 128, jnp.concatenate(thirds, axis=1))

    scale = HD ** (-0.5) * LOG2E
    block = acc.shape[0]

    def row_block(b, carry):
        rows = pl.ds(pl.multiple_of(b * block, block), block)

        def sample(s, inner):
            values = v_ref[s]
            grads = g_ref[s, rows, :]
            weights = jnp.exp2(dot_nt(q_ref[s, rows, :], k_ref[s]) * scale + bias_scr[rows, :])
            probs = weights * (1.0 / jnp.sum(weights, axis=-1, keepdims=True))
            mixed = matmul(probs.astype(BF16), values)
            mixed_ref[s, rows, :] = mixed.astype(BF16)
            center = jnp.sum(grads.astype(F32) * mixed, axis=-1, keepdims=True)
            score_grad = probs * (dot_nt(grads, values) - center)
            acc[...] = jnp.where(s == 0, score_grad, acc[...] + score_grad)
            return inner

        lax.fori_loop(0, 6, sample, 0)
        pack_rows(acc[...], grad_ref, b * (block // 48), block // 48)
        return carry

    lax.fori_loop(0, 768 // block, row_block, 0)


def pair_grad_kernel(in_ref, w_ref, out_ref, scr):
    total = in_ref[0].astype(F32)
    for part in range(1, 8):
        total = total + in_ref[part].astype(F32)
    scr[...] = total.reshape(640, 128)
    weight = w_ref[...]

    def step(position, places):
        grad = scr[pl.ds(position, 16, stride=40), :]
        high = grad.astype(BF16)
        rest = grad - high.astype(F32)
        middle = rest.astype(BF16)
        least = (rest - middle.astype(F32)).astype(BF16)
        rows = dot_tn(jnp.concatenate([high, middle, least], axis=0), weight)
        at = 0
        for start, size in places:
            out_ref[pl.ds(pl.multiple_of(start, 32), size), :] = rows[at : at + size]
            at += size

    def wide(i, carry):
        step(i, [(96 * i, 64), (96 * (i + 24), 64)])
        return carry

    def thin(i, carry):
        step(i + 24, [(96 * (i + 16 * m) + 64, 32) for m in range(3)])
        return carry

    lax.fori_loop(0, 24, wide, 0)
    lax.fori_loop(0, 16, thin, 0)


def column_order(value, axis):
    shape = value.shape
    split = value.reshape(shape[:axis] + (8, 96) + shape[axis + 1 :])
    wide = lax.slice_in_dim(split, 0, 64, axis=axis + 1).reshape(shape[:axis] + (512,) + shape[axis + 1 :])
    thin = lax.slice_in_dim(split, 64, 96, axis=axis + 1).reshape(shape[:axis] + (256,) + shape[axis + 1 :])
    return jnp.concatenate([wide, thin], axis=axis)


def exchange(value, axes):
    return lax.all_to_all(value, axes, 0, 0, tiled=True)


def body(
    pair_state,
    pair_mask,
    chain_ids,
    tokens,
    grad_attn,
    norm_pair,
    proj_left,
    gate_left,
    proj_right,
    gate_right,
    gate_out,
    norm_tri,
    tri_out,
    norm_bias,
    bias_proj,
    chain_weight,
    norm_tokens,
    w_query,
    w_key,
    w_value,
    w_out,
    norm_ff,
    ff_gate,
    ff_up,
    ff_down,
):
    tile_rows, tile_cols, channels = pair_state.shape
    tile_size = tile_rows * tile_cols
    row_start = lax.axis_index(ROWS) * tile_rows
    col_index = lax.axis_index(COLS)
    col_start = col_index * tile_cols
    pair_flat = pair_state.reshape(tile_size, channels)

    mask_float = pair_mask.astype(F32)
    row_mask = lax.dynamic_slice_in_dim(mask_float, row_start, tile_rows)
    col_mask = lax.dynamic_slice_in_dim(mask_float, col_start, tile_cols)
    tile_mask = row_mask[:, None] * col_mask[None, :]
    wide_mask = jnp.concatenate([tile_mask[:24, :64], tile_mask[24:, :64]], axis=1)
    thin_mask = jnp.concatenate([tile_mask[:24, 64:], tile_mask[24:, 64:]], axis=1)
    packed_mask = jnp.concatenate(
        [wide_mask, wide_mask, jnp.concatenate([thin_mask, thin_mask], axis=1)], axis=0
    )
    pair_weights = jnp.concatenate([proj_left, proj_right, gate_left, gate_right], axis=1).T
    sides, normed = call(
        project_kernel,
        (jax.ShapeDtypeStruct((128, 72, 128), BF16), jax.ShapeDtypeStruct((tile_size, 128), BF16)),
        (pair_flat, norm_pair.astype(F32)[None], pair_weights, packed_mask),
        [pltpu.VMEM((128 * 72, 128), F32)],
        "project",
        flops=2 * 512 * 128 * 6144,
        nbytes=5_000_000,
    )
    sides_in = exchange(sides, ALL).reshape(16, 8, 72, 128)
    products = call(
        product_kernel,
        jax.ShapeDtypeStruct((16, 8, 40, 128), BF16),
        (sides_in,),
        [pltpu.VMEM((768, 768), BF16), pltpu.VMEM((768, 768), BF16)],
        "product",
        flops=2 * 768**3,
        nbytes=4_000_000,
    )
    tri_in = exchange(products.reshape(128, 40, 128), ALL)

    samples, seq_len, model_width = tokens.shape
    token_flat = tokens.reshape(samples * seq_len, model_width)
    token_norm = layer_norm(token_flat.astype(F32), norm_tokens).astype(BF16)

    def heads_of(rows, weight):
        value = matmul(rows, weight).astype(BF16).reshape(samples, seq_len, 2, HD)
        return jnp.transpose(value, (2, 0, 1, 3))

    query = heads_of(token_norm, w_query)
    key = column_order(heads_of(token_norm, w_key), 2)
    value = column_order(heads_of(token_norm, w_value), 2)
    head_grad = heads_of(grad_attn.reshape(samples * seq_len, model_width), w_out.T)
    swapped = exchange(jnp.concatenate([query, key, value, head_grad], axis=3), "core")
    swapped = swapped.reshape(2 * samples, seq_len, 4 * HD)
    query, key, value, head_grad = [swapped[:, :, HD * n : HD * n + HD] for n in range(4)]
    w_out_all = lax.all_gather(w_out, COLS, axis=0, tiled=True)

    gate = jax.nn.sigmoid(matmul(normed, gate_out))
    heads_first = jnp.transpose(bias_proj.T.reshape(8, 2, 128), (1, 0, 2)).reshape(16, 128)
    pair_out, bias = call(
        update_kernel,
        (jax.ShapeDtypeStruct((tile_size, 128), F32), jax.ShapeDtypeStruct((8, 16, 40, 128), BF16)),
        (
            tri_in,
            pair_flat,
            gate,
            tri_out,
            jnp.broadcast_to(norm_tri.astype(F32)[:, None], (128, 128)),
            norm_bias.astype(F32)[None],
            heads_first,
        ),
        [pltpu.VMEM((128 * 40, 128), F32), pltpu.VMEM((16 * 40, 128), F32)],
        "update",
        flops=2 * 128 * 128 * 5120,
        nbytes=9_000_000,
    )
    bias_in = exchange(bias.reshape(128, 40, 128), ALL).reshape(16, 8, 40, 128)

    head_index = 2 * col_index + lax.axis_index("core")
    head_weight = lax.dynamic_slice_in_dim(chain_weight, head_index, 1)[None]
    mixed, bias_grad = call(
        attention_kernel,
        (
            jax.ShapeDtypeStruct((2 * samples, seq_len, HD), BF16),
            jax.ShapeDtypeStruct((16, 8, 40, 128), BF16),
        ),
        (
            bias_in,
            query,
            key,
            value,
            head_grad,
            chain_ids[:, None],
            column_order(chain_ids[None], 1),
            head_weight,
        ),
        [pltpu.VMEM((768, 768), F32), pltpu.VMEM((192, 768), F32)],
        "attention",
        flops=6 * 6 * 768 * 768 * 128,
        nbytes=12_000_000,
    )

    share_len = seq_len // 8
    mixed_out = jnp.transpose(mixed.reshape(2, samples, 8, share_len, HD), (0, 2, 1, 3, 4))
    mixed_in = exchange(mixed_out.reshape(16, samples, share_len, HD), ("core",) + COLS)
    mixed_rows = jnp.transpose(mixed_in.reshape(2, 8, samples, share_len, HD), (2, 3, 1, 0, 4))
    attn = matmul(mixed_rows.reshape(samples * share_len, model_width), w_out_all)
    token_share = lax.dynamic_slice_in_dim(tokens, col_index * share_len, share_len, 1)
    state = token_share.reshape(samples * share_len, model_width).astype(F32) + attn
    ff_in = layer_norm(state, norm_ff).astype(BF16)
    hidden = (jax.nn.silu(matmul(ff_in, ff_gate)) * matmul(ff_in, ff_up)).astype(BF16)
    refined = (state + matmul(hidden, ff_down)).reshape(samples, share_len, model_width)

    grad_in = exchange(bias_grad.reshape(128, 40, 128), ALL).reshape(8, 16, 40, 128)
    pair_grad = call(
        pair_grad_kernel,
        jax.ShapeDtypeStruct((tile_size, 128), F32),
        (grad_in, jnp.concatenate([heads_first] * 3, axis=0)),
        [pltpu.VMEM((16 * 40, 128), F32)],
        "pair_grad",
        flops=2 * 48 * 128 * 5120,
        nbytes=4_000_000,
    )
    return (pair_out.reshape(pair_state.shape), refined, pair_grad.reshape(pair_state.shape))


def solution(mesh):
    fine = Mesh(mesh.devices.reshape(2, 4, 2, 2, 4), ALL)
    pair = P(ROWS, COLS, None)
    sample_rows = P(ROWS, None, None)
    return jax.shard_map(
        body,
        mesh=fine,
        in_specs=(pair, P(), P(), sample_rows, sample_rows)
        + (P(),) * 12
        + (P(None, COLS),) * 3
        + (P(COLS, None),)
        + (P(),) * 4,
        out_specs=(pair, pair, pair),
        check_vma=False,
    )
```

```python
import functools
import jax
import jax.numpy as jnp
from jax import lax
from jax.experimental import pallas as pl
from jax.experimental.pallas import tpu as pltpu
from jax.sharding import Mesh, PartitionSpec as P

HD = 48
F32 = jnp.float32
BF16 = jnp.bfloat16
ROWS = ("grp", "y", "core")
COLS = ("xh", "z")
ALL = ROWS + COLS
LOG2E = 1.4426950408889634
SCALE = HD ** (-0.5) * LOG2E
VMEM_LIMIT = 60 * 1024 * 1024
FORWARD_ROWS = 384
PROJECT_PAR = 2
UPDATE_PAR = 4
BACKWARD_ROWS = 192


def layer_norm(value_rows, gain_vec):
    middle = value_rows - jnp.mean(value_rows, axis=-1, keepdims=True)
    spread = jnp.mean(middle * middle, axis=-1, keepdims=True)
    return middle * lax.rsqrt(spread + 1e-05) * gain_vec.astype(F32)


def matmul(left_side, right_side):
    return jnp.dot(left_side, right_side, preferred_element_type=F32)


def dot_nt(a, b):
    return lax.dot_general(a, b, (((1,), (1,)), ((), ())), preferred_element_type=F32)


def dot_tn(a, b):
    return lax.dot_general(a, b, (((0,), (0,)), ((), ())), preferred_element_type=F32)


def lanes_of(rows):
    return lax.broadcasted_iota(jnp.int32, (rows, 128), 1)


def roll(value, shift):
    shift = shift % 128
    return value if shift == 0 else pltpu.roll(value, shift, 1)


def call(kernel, outs, args, scratch, name, flops=0, nbytes=0, spaces=None, grid=None, out_specs=None):
    vmem = pl.BlockSpec(memory_space=pltpu.VMEM)
    return pl.pallas_call(
        kernel,
        out_shape=outs,
        in_specs=spaces or [vmem] * len(args),
        out_specs=out_specs or jax.tree.map(lambda _: vmem, outs),
        scratch_shapes=scratch,
        compiler_params=pltpu.CompilerParams(vmem_limit_bytes=VMEM_LIMIT),
        cost_estimate=pl.CostEstimate(flops=flops, bytes_accessed=nbytes, transcendentals=0),
        name=name,
        **({} if grid is None else {"grid": grid}),
    )(*args)


def start_all(copies):
    for copy in copies:
        copy.start()
    return copies


def wait_all(copies):
    for copy in copies:
        copy.wait()


def project_kernel(
    pair_hbm, gain_ref, pl_hbm, pr_hbm, gl_hbm, gr_hbm, mask_hbm, place_ref, out_hbm, normed_hbm,
    scr, pair_ref, normed_ref, w_ref, out_ref, mask_ref, pair_sems, w_sems, out_sems,
):
    blocks = [pl.ds(512 * n, 512) for n in range(9)]
    pair_copies = start_all(
        [pltpu.make_async_copy(pair_hbm.at[b], pair_ref.at[b], pair_sems.at[n]) for n, b in enumerate(blocks)]
    )
    w_copies = start_all(
        [
            pltpu.make_async_copy(src, w_ref.at[n], w_sems.at[n])
            for n, src in enumerate((pl_hbm, pr_hbm, gl_hbm, gr_hbm))
        ]
        + [pltpu.make_async_copy(mask_hbm, mask_ref, w_sems.at[4])]
    )
    gain = gain_ref[...]
    normed_copies = []
    for n, block in enumerate(blocks):
        pair_copies[n].wait()
        normed_ref[block, :] = layer_norm(pair_ref[block, :].astype(F32), gain).astype(BF16)
        copy = pltpu.make_async_copy(normed_ref.at[block], normed_hbm.at[block], out_sems.at[n])
        copy.start()
        normed_copies.append(copy)
    wait_all(w_copies)
    lane = lanes_of(1)
    row_start = place_ref[0]
    col_start = place_ref[1]
    wide_cols = jnp.zeros((1, 128), F32)
    thin_cols = jnp.zeros((1, 128), F32)
    for k in range(64):
        wide_cols = jnp.where(lane % 64 == k, mask_ref[col_start + k].astype(F32), wide_cols)
    for k in range(32):
        thin_cols = jnp.where(lane % 32 == k, mask_ref[col_start + 64 + k].astype(F32), thin_cols)
    low = lanes_of(128) < 64
    weights = jnp.concatenate([w_ref[n].astype(F32).T.astype(BF16) for n in range(4)], axis=0)

    def rows_at(i, start, size):
        return normed_ref[pl.ds(pl.multiple_of(i * 96 + start, 32), size), :]

    def one(i):
        wide = [rows_at(i, 0, 64), rows_at(i + 24, 0, 64)]
        thin = [rows_at(i, 64, 32), rows_at(i + 24, 64, 32)]
        y = dot_nt(weights, jnp.concatenate(wide + thin + thin, axis=0))
        first = mask_ref[row_start + i].astype(F32)
        second = mask_ref[row_start + i + 24].astype(F32)
        wide_mask = jnp.where(lane < 64, first, second) * wide_cols
        thin_mask = jnp.where(lane % 64 < 32, first, second) * thin_cols
        left = y[0:128, 0:128] * jax.nn.sigmoid(y[256:384, 0:128])
        right = y[128:256, 0:128] * jax.nn.sigmoid(y[384:512, 0:128])
        both_p = jnp.where(low, y[0:128, 128:256], y[128:256, 128:256])
        both_g = jnp.where(low, y[256:384, 128:256], y[384:512, 128:256])
        scr[pl.ds(i, 128, stride=72), :] = left * wide_mask
        scr[pl.ds(i + 24, 128, stride=72), :] = right * wide_mask
        scr[pl.ds(i + 48, 128, stride=72), :] = both_p * jax.nn.sigmoid(both_g) * thin_mask

    def chunk(i, carry):
        for k in range(PROJECT_PAR):
            one(PROJECT_PAR * i + k)
        return carry

    lax.fori_loop(0, 24 // PROJECT_PAR, chunk, 0)
    out_copies = []
    for n in range(8):
        part = scr[1152 * n : 1152 * n + 1152, :].reshape(16, 72, 128)
        out_ref[16 * n : 16 * n + 16] = part.astype(BF16)
        copy = pltpu.make_async_copy(
            out_ref.at[pl.ds(16 * n, 16)], out_hbm.at[pl.ds(16 * n, 16)], out_sems.at[9 + n]
        )
        copy.start()
        out_copies.append(copy)
    wait_all(normed_copies + out_copies)


def token_kernel(
    tokens_ref, grad_ref, gain_ref, wq_ref, wk_ref, wv_ref, wo_ref, core_ref, keep_ref, send_ref, w_scr, wo_scr, norm_scr
):
    even = core_ref[0] == 0

    @pl.when(pl.program_id(0) == 0)
    def _():
        gap = jnp.zeros((768, 16), F32)
        for n, ref in enumerate((wq_ref, wk_ref, wv_ref)):
            w = ref[...].astype(F32)
            w = jnp.concatenate([w[:, 0:48], gap, w[:, 48:96], gap], axis=1)
            w_scr[:, 128 * n : 128 * n + 128] = jnp.where(even, w, roll(w, 64)).astype(BF16)
        first, second = wo_ref[0:48, :], wo_ref[48:96, :]
        wo_scr[0:48, :] = jnp.where(even, first, second)
        wo_scr[64:112, :] = jnp.where(even, second, first)
        wo_scr[48:64, :] = jnp.zeros((16, 768), BF16)
        wo_scr[112:128, :] = jnp.zeros((16, 768), BF16)

    gain = gain_ref[...]

    def norm_block(block, carry):
        rows = pl.ds(pl.multiple_of(block * 96, 32), 96)
        norm_scr[rows, :] = layer_norm(tokens_ref[0, rows, :].astype(F32), gain).astype(BF16)
        return carry

    lax.fori_loop(0, 8, norm_block, 0)
    low = lanes_of(768) < 64
    query = matmul(norm_scr[...], w_scr[:, 0:128])
    grads = dot_nt(grad_ref[0], wo_scr[...])
    keep_ref[0, 0] = jnp.where(low, query, roll(grads, 64)).astype(BF16)
    send_ref[0, 0] = jnp.where(low, roll(query, 64), grads).astype(BF16)
    key = matmul(norm_scr[...], w_scr[:, 128:256])
    value = matmul(norm_scr[...], w_scr[:, 256:384])
    for ref, full in (
        (keep_ref, jnp.where(low, key, roll(value, 64))),
        (send_ref, jnp.where(low, roll(key, 64), value)),
    ):
        full = full.astype(BF16)
        for q in range(8):
            ref[0, 1, 64 * q : 64 * q + 64] = full[96 * q : 96 * q + 64]
            ref[0, 1, 512 + 32 * q : 544 + 32 * q] = full[96 * q + 64 : 96 * q + 96]


def unpack_wide(first, second, low):
    top = jnp.where(low, first, roll(second, 64))
    bottom = jnp.where(low, roll(first, 64), second)
    return top, bottom


def product_kernel(in_hbm, out_hbm, in_ref, out_ref, l_scr, r_scr, in_sems, out_sems):
    copies = start_all(
        [
            pltpu.make_async_copy(
                in_hbm.at[:, pl.ds(4 * u, 4)], in_ref.at[:, pl.ds(4 * u, 4)], in_sems.at[u]
            )
            for u in range(2)
        ]
    )
    lane = lanes_of(384)
    low = lane < 64

    def put(dst, column, full):
        full = full.reshape(768, 128).astype(BF16)
        if dst is l_scr:
            dst[:, column : column + 128] = full
        else:
            for q in range(8):
                dst[64 * q : 64 * q + 64, column : column + 128] = full[96 * q : 96 * q + 64]
                dst[512 + 32 * q : 544 + 32 * q, column : column + 128] = full[96 * q + 64 : 96 * q + 96]

    def stack(halves):
        return jnp.concatenate([h.reshape(16, 24, 128) for h in halves], axis=1)

    def part(value, start):
        return value[:, start : start + 24].reshape(384, 128)

    for u in range(2):
        copies[u].wait()
        blocks = [in_ref[:, 4 * u + v].astype(F32) for v in range(4)]
        for p in range(2):
            for dst, start in ((l_scr, 0), (r_scr, 24)):
                halves = unpack_wide(part(blocks[2 * p], start), part(blocks[2 * p + 1], start), low)
                put(dst, (2 * u + p) * 128, stack(halves))
        thin = [part(b, 48) for b in blocks]
        for dst, base in ((l_scr, 0), (r_scr, 2)):
            halves = []
            for a in range(2):
                parts = [roll(thin[v], 32 * (v - base - a)) for v in range(4)]
                lower = jnp.where(lane < 32, parts[0], parts[1])
                upper = jnp.where(lane < 96, parts[2], parts[3])
                halves.append(jnp.where(low, lower, upper))
            put(dst, 512 + u * 128, stack(halves))
    out_copies = []
    for b in range(4):
        product = dot_nt(l_scr[192 * b : 192 * b + 192, :], r_scr[...])
        pack_rows(product, out_ref, 4 * b, 4)
        copy = pltpu.make_async_copy(
            out_ref.at[pl.ds(4 * b, 4)], out_hbm.at[pl.ds(4 * b, 4)], out_sems.at[b]
        )
        copy.start()
        out_copies.append(copy)
    wait_all(out_copies)


def pack_rows(full, out_ref, first, count):
    low = lanes_of(count * 24) < 64
    lane = lanes_of(count * 16)
    for q in range(8):
        tile = full[:, 128 * (q // 2) : 128 * (q // 2) + 128].reshape(count, 48, 128)
        top = tile[:, 0:24].reshape(count * 24, 128)
        bottom = tile[:, 24:48].reshape(count * 24, 128)
        if q % 2 == 0:
            wide = jnp.where(low, top, roll(bottom, 64))
        else:
            wide = jnp.where(low, roll(top, 64), bottom)
        tile = full[:, 512 + 128 * (q // 4) : 640 + 128 * (q // 4)].reshape(count, 48, 128)
        thin = [
            roll(tile[:, 16 * m : 16 * m + 16].reshape(count * 16, 128), 32 * (m - q % 4))
            for m in range(3)
        ]
        thin = jnp.where(lane < 32, thin[0], jnp.where(lane < 64, thin[1], thin[2]))
        piece = jnp.concatenate(
            [wide.reshape(count, 24, 128), thin.reshape(count, 16, 128)], axis=1
        )
        out_ref[pl.ds(first, count), q] = piece.astype(BF16)


def wide_places(i):
    return [(i, 0, 64), (i + 24, 0, 64)]


def thin_places(i):
    return [(i + 16 * m, 64, 32) for m in range(3)]


def update_kernel(
    t_hbm, pair_hbm, gate_hbm, w_ref, tri_gain_ref, bias_gain_ref, bp_ref, out_hbm, bias_hbm,
    scr, b_scr, t_ref, pair_ref, gate_ref, out_ref, bias_ref, t_sems, sems, out_sems,
):
    t_copies = start_all(
        [
            pltpu.make_async_copy(t_hbm.at[pl.ds(32 * n, 32)], t_ref.at[pl.ds(32 * n, 32)], t_sems.at[n])
            for n in range(4)
        ]
    )
    copies = start_all(
        [
            pltpu.make_async_copy(pair_hbm, pair_ref, sems.at[0]),
            pltpu.make_async_copy(gate_hbm, gate_ref, sems.at[1]),
        ]
    )
    for n in range(4):
        t_copies[n].wait()
        scr[1280 * n : 1280 * n + 1280, :] = t_ref[32 * n : 32 * n + 32].astype(F32).reshape(1280, 128)
    wait_all(copies)
    weight = w_ref[...]
    tri_gain = tri_gain_ref[...]
    bias_gain = bias_gain_ref[...]
    bias_proj = bp_ref[...]

    def group(positions, places):
        normed = []
        for position in positions:
            tri = scr[pl.ds(position, 128, stride=40), :]
            middle = tri - jnp.mean(tri, axis=0, keepdims=True)
            spread_of = jnp.mean(middle * middle, axis=0, keepdims=True)
            normed.append((middle * lax.rsqrt(spread_of + 1e-05) * tri_gain).astype(BF16))
        update = dot_tn(jnp.concatenate(normed, axis=1), weight)
        fed = []
        for n, spots in enumerate(places):
            at = 128 * n
            for row, start, size in spots:
                cols = pl.ds(start, size)
                new = pair_ref[row, cols, :].astype(F32) + gate_ref[row, cols, :] * update[at : at + size]
                out_ref[row, cols, :] = new
                fed.append(layer_norm(new, bias_gain).astype(BF16))
                at += size
            if len(spots) == 3:
                fed.append(fed[-1])
        bias = dot_nt(bias_proj, jnp.concatenate(fed, axis=0))
        for n, position in enumerate(positions):
            b_scr[pl.ds(position, 16, stride=40), :] = bias[:, 128 * n : 128 * n + 128]

    par = UPDATE_PAR

    def wide(i, carry):
        group([par * i + n for n in range(par)], [wide_places(par * i + n) for n in range(par)])
        return carry

    def thin(i, carry):
        group([24 + par * i + n for n in range(par)], [thin_places(par * i + n) for n in range(par)])
        return carry

    lax.fori_loop(0, 24 // par, wide, 0)
    out_copies = [
        pltpu.make_async_copy(out_ref.at[:, pl.ds(c, n)], out_hbm.at[:, pl.ds(c, n)], out_sems.at[8 + k])
        for k, (c, n) in enumerate(((0, 64), (64, 32)))
    ]
    out_copies[0].start()
    lax.fori_loop(0, 16 // par, thin, 0)
    out_copies[1].start()
    bias_ref[...] = b_scr[...].reshape(16, 40, 128).astype(BF16)
    out_copies += start_all(
        [pltpu.make_async_copy(bias_ref, bias_hbm.at[n], out_sems.at[n]) for n in range(8)]
    )
    wait_all(out_copies)


def unpack_bias(bias_ref, copies, put):
    low = lanes_of(384) < 64
    lane = lanes_of(256)
    for u in range(2):
        copies[u].wait()
        blocks = [bias_ref[:, 4 * u + v].astype(F32) for v in range(4)]
        for p in range(2):
            halves = unpack_wide(
                blocks[2 * p][:, 0:24].reshape(384, 128),
                blocks[2 * p + 1][:, 0:24].reshape(384, 128),
                low,
            )
            put((2 * u + p) * 128, jnp.concatenate([h.reshape(16, 24, 128) for h in halves], axis=1))
        thin = [b[:, 24:40].reshape(256, 128) for b in blocks]
        thirds = []
        for m in range(3):
            parts = [roll(thin[v], 32 * (v - m)) for v in range(4)]
            lower = jnp.where(lane < 32, parts[0], parts[1])
            upper = jnp.where(lane < 96, parts[2], parts[3])
            thirds.append(jnp.where(lane < 64, lower, upper).reshape(16, 16, 128))
        put(512 + u * 128, jnp.concatenate(thirds, axis=1))


def pair_copies(keep_hbm, recv_hbm, pairs, sems):
    return start_all(
        [
            pltpu.make_async_copy(src, pairs.at[pl.ds(3 * n, 3)], sems.at[n])
            for n, src in enumerate((keep_hbm, recv_hbm))
        ]
    )


def forward_kernel(
    bias_hbm, keep_hbm, recv_hbm, chain_row_ref, chain_col_ref, place_ref, weight_ref,
    mixed_hbm, full_hbm, stats_hbm, pairs, bias_ref, mixed_ref, full_ref, stats_ref, sems, in_sems, out_sems,
):
    bias_copies = start_all(
        [
            pltpu.make_async_copy(
                bias_hbm.at[:, pl.ds(4 * u, 4)], bias_ref.at[:, pl.ds(4 * u, 4)], in_sems.at[u]
            )
            for u in range(2)
        ]
    )
    copies = pair_copies(keep_hbm, recv_hbm, pairs, sems)
    core = place_ref[2]
    head_weight = weight_ref[place_ref[3]] * LOG2E

    def put(column, full):
        same = chain_row_ref[...] == chain_col_ref[:, column : column + 128]
        full_ref[:, column : column + 128] = full.reshape(768, 128) * LOG2E + jnp.where(
            same, head_weight, 0.0
        )

    unpack_bias(bias_ref, bias_copies, put)
    full_copy = pltpu.make_async_copy(full_ref, full_hbm, out_sems.at[0])
    full_copy.start()
    stats_ref[...] = jnp.zeros_like(stats_ref)
    wait_all(copies)
    low_all = lanes_of(768) < 64
    lane = lanes_of(FORWARD_ROWS)
    low = lane < 64
    thin_low = lanes_of(48) < 64
    blocks = 768 // FORWARD_ROWS
    shares = FORWARD_ROWS // 96

    def block(s, b, owner, slot):
        both = pairs[s, 1]
        keys = jnp.where(low_all, both, jnp.zeros_like(both))
        rows = pl.ds(pl.multiple_of(b * FORWARD_ROWS, 32), FORWARD_ROWS)
        asked = pairs[s, 0, rows, :]
        weights = jnp.exp2(dot_nt(asked, keys) * SCALE + full_ref[rows, :])
        inverse = 1.0 / jnp.sum(weights, axis=-1, keepdims=True)
        mixed = matmul((weights * inverse).astype(BF16), both)
        center = jnp.sum(jnp.where(low, 0.0, asked.astype(F32) * mixed), axis=-1, keepdims=True)
        stats_ref[rows, :] = jnp.where(
            lane == s, inverse, jnp.where(lane == s + 64, center, stats_ref[rows, :])
        )
        for n in range(shares):
            mixed_ref[owner * 8 + b * shares + n, slot] = jnp.where(
                thin_low, roll(mixed[96 * n : 96 * n + 48], 64), mixed[96 * n + 48 : 96 * n + 96]
            ).astype(BF16)

    def step(i, carry):
        half = i // blocks
        owner = jnp.where(half == 0, core, 1 - core)
        for n in range(3):
            block(3 * half + n, i % blocks, owner, n)
        return carry

    def mixed_copy(owner, sem):
        part = pl.ds(owner * 8, 8)
        return pltpu.make_async_copy(mixed_ref.at[part], mixed_hbm.at[part], out_sems.at[sem])

    lax.fori_loop(0, blocks, step, 0)
    mixed_copy(core, 1).start()
    lax.fori_loop(blocks, 2 * blocks, step, 0)
    mixed_copy(1 - core, 2).start()
    stats_copy = pltpu.make_async_copy(stats_ref, stats_hbm, out_sems.at[3])
    stats_copy.start()
    mixed_copy(core, 1).wait()
    mixed_copy(1 - core, 2).wait()
    full_copy.wait()
    stats_copy.wait()


def backward_kernel(
    full_hbm, stats_hbm, keep_hbm, recv_hbm, grad_hbm, pairs, full_ref, stats_ref, grad_ref, sems, in_sems, out_sems
):
    copies = pair_copies(keep_hbm, recv_hbm, pairs, sems)
    copies += start_all([pltpu.make_async_copy(stats_hbm, stats_ref, in_sems.at[0])])
    copies += start_all([pltpu.make_async_copy(full_hbm, full_ref, in_sems.at[1])])
    wait_all(copies)
    low_all = lanes_of(768) < 64

    def row_block(b, carry):
        rows = pl.ds(pl.multiple_of(b * BACKWARD_ROWS, 32), BACKWARD_ROWS)
        total = None
        for s in range(6):
            both = pairs[s, 1]
            keys = jnp.where(low_all, both, jnp.zeros_like(both))
            values = jnp.where(low_all, jnp.zeros_like(both), both)
            asked = pairs[s, 0, rows, :]
            inverse = stats_ref[rows, s : s + 1]
            center = stats_ref[rows, s + 64 : s + 65]
            probs = jnp.exp2(dot_nt(asked, keys) * SCALE + full_ref[rows, :]) * inverse
            score_grad = probs * (dot_nt(asked, values) - center)
            total = score_grad if total is None else total + score_grad
        pack_rows(total, grad_ref, b * (BACKWARD_ROWS // 48), BACKWARD_ROWS // 48)
        grad_copy(b).start()
        return carry

    def grad_copy(b):
        part = pl.ds(b * (BACKWARD_ROWS // 48), BACKWARD_ROWS // 48)
        return pltpu.make_async_copy(grad_ref.at[part], grad_hbm.at[part], out_sems.at[b])

    lax.fori_loop(0, 768 // BACKWARD_ROWS, row_block, 0)
    wait_all([grad_copy(b) for b in range(768 // BACKWARD_ROWS)])


def pair_grad_kernel(in_hbm, w_ref, out_hbm, scr, in_ref, out_ref, in_sems, out_sems):
    copies = start_all([pltpu.make_async_copy(in_hbm.at[n], in_ref.at[n], in_sems.at[n]) for n in range(8)])
    total = None
    for n in range(8):
        copies[n].wait()
        part = in_ref[n].astype(F32)
        total = part if total is None else total + part
    scr[...] = total.reshape(640, 128)
    weight = w_ref[...]

    def group(positions, places):
        grad = jnp.concatenate([scr[pl.ds(p, 16, stride=40), :] for p in positions], axis=1)
        high = grad.astype(BF16)
        rest = grad - high.astype(F32)
        middle = rest.astype(BF16)
        least = (rest - middle.astype(F32)).astype(BF16)
        rows = dot_tn(jnp.concatenate([high, middle, least], axis=0), weight)
        for n, spots in enumerate(places):
            at = 128 * n
            for row, start, size in spots:
                out_ref[row, pl.ds(start, size), :] = rows[at : at + size]
                at += size

    par = UPDATE_PAR

    def wide(i, carry):
        group([par * i + n for n in range(par)], [wide_places(par * i + n) for n in range(par)])
        return carry

    def thin(i, carry):
        group([24 + par * i + n for n in range(par)], [thin_places(par * i + n) for n in range(par)])
        return carry

    lax.fori_loop(0, 24 // par, wide, 0)
    out_copies = [
        pltpu.make_async_copy(out_ref.at[:, pl.ds(c, n)], out_hbm.at[:, pl.ds(c, n)], out_sems.at[k])
        for k, (c, n) in enumerate(((0, 64), (64, 32)))
    ]
    out_copies[0].start()
    lax.fori_loop(0, 16 // par, thin, 0)
    out_copies[1].start()
    wait_all(out_copies)


def column_order(value, axis):
    shape = value.shape
    split = value.reshape(shape[:axis] + (8, 96) + shape[axis + 1 :])
    wide = lax.slice_in_dim(split, 0, 64, axis=axis + 1).reshape(shape[:axis] + (512,) + shape[axis + 1 :])
    thin = lax.slice_in_dim(split, 64, 96, axis=axis + 1).reshape(shape[:axis] + (256,) + shape[axis + 1 :])
    return jnp.concatenate([wide, thin], axis=axis)


def exchange(value, axes):
    return lax.all_to_all(value, axes, 0, 0, tiled=True)


def body(
    pair_state,
    pair_mask,
    chain_ids,
    tokens,
    grad_attn,
    norm_pair,
    proj_left,
    gate_left,
    proj_right,
    gate_right,
    gate_out,
    norm_tri,
    tri_out,
    norm_bias,
    bias_proj,
    chain_weight,
    norm_tokens,
    w_query,
    w_key,
    w_value,
    w_out,
    norm_ff,
    ff_gate,
    ff_up,
    ff_down,
):
    tile_rows, tile_cols, channels = pair_state.shape
    tile_size = tile_rows * tile_cols
    row_start = lax.axis_index(ROWS) * tile_rows
    col_index = lax.axis_index(COLS)
    col_start = col_index * tile_cols
    pair_flat = pair_state.reshape(tile_size, channels)

    vmem = pl.BlockSpec(memory_space=pltpu.VMEM)
    smem = pl.BlockSpec(memory_space=pltpu.SMEM)
    hbm = pl.BlockSpec(memory_space=pltpu.HBM)
    core_index = lax.axis_index("core")
    place = jnp.stack([row_start, col_start, core_index, 2 * col_index + core_index]).astype(jnp.int32)

    sides, normed = call(
        project_kernel,
        (jax.ShapeDtypeStruct((128, 72, 128), BF16), jax.ShapeDtypeStruct((tile_size, 128), BF16)),
        (
            pair_flat, norm_pair.astype(F32)[None], proj_left, proj_right, gate_left, gate_right,
            pair_mask, place,
        ),
        [
            pltpu.VMEM((128 * 72, 128), F32),
            pltpu.VMEM((tile_size, 128), BF16),
            pltpu.VMEM((tile_size, 128), BF16),
            pltpu.VMEM((4, 128, 128), BF16),
            pltpu.VMEM((128, 72, 128), BF16),
            pltpu.SMEM((768,), jnp.int32),
            pltpu.SemaphoreType.DMA((9,)),
            pltpu.SemaphoreType.DMA((5,)),
            pltpu.SemaphoreType.DMA((17,)),
        ],
        "project",
        flops=2 * 512 * 128 * 6144,
        nbytes=5_000_000,
        spaces=[hbm, vmem] + [hbm] * 5 + [smem],
        out_specs=(hbm, hbm),
    )
    sides_in = exchange(sides, ALL)

    samples, seq_len, model_width = tokens.shape
    part = jax.ShapeDtypeStruct((samples, 2, seq_len, 128), BF16)
    token_block = pl.BlockSpec((1, seq_len, model_width), lambda s: (s, 0, 0))
    part_block = pl.BlockSpec((1, 2, seq_len, 128), lambda s: (s, 0, 0, 0))
    keep, send = call(
        token_kernel,
        (part, part),
        (
            tokens, grad_attn, norm_tokens.astype(F32)[None], w_query, w_key, w_value, w_out, place[2:3],
        ),
        [pltpu.VMEM((768, 384), BF16), pltpu.VMEM((128, 768), BF16), pltpu.VMEM((768, 768), BF16)],
        "tokens",
        flops=2 * 2304 * 768 * 512,
        nbytes=12_000_000,
        spaces=[token_block, token_block] + [vmem] * 5 + [smem],
        grid=(samples,),
        out_specs=(part_block, part_block),
    )
    sides_in, keep, send = lax.optimization_barrier((sides_in, keep, send))
    recv = lax.ppermute(send, "core", [(0, 1), (1, 0)])
    w_out_all = lax.all_gather(w_out, COLS, axis=0, tiled=True)

    products = call(
        product_kernel,
        jax.ShapeDtypeStruct((16, 8, 40, 128), BF16),
        (sides_in.reshape(16, 8, 72, 128),),
        [
            pltpu.VMEM((16, 8, 72, 128), BF16),
            pltpu.VMEM((16, 8, 40, 128), BF16),
            pltpu.VMEM((768, 768), BF16),
            pltpu.VMEM((768, 768), BF16),
            pltpu.SemaphoreType.DMA((2,)),
            pltpu.SemaphoreType.DMA((4,)),
        ],
        "product",
        flops=2 * 768**3,
        nbytes=4_000_000,
        spaces=[hbm],
        out_specs=hbm,
    )
    tri_in = exchange(products.reshape(128, 40, 128), ALL)
    share_len = seq_len // 8
    token_share = lax.dynamic_slice_in_dim(tokens, col_index * share_len, share_len, 1)
    tri_in, recv, token_share = lax.optimization_barrier((tri_in, recv, token_share))

    gate = jax.nn.sigmoid(matmul(normed, gate_out))
    heads_first = jnp.transpose(bias_proj.T.reshape(8, 2, 128), (1, 0, 2)).reshape(16, 128)
    pair_out, bias = call(
        update_kernel,
        (jax.ShapeDtypeStruct(pair_state.shape, F32), jax.ShapeDtypeStruct((8, 16, 40, 128), BF16)),
        (
            tri_in,
            pair_state,
            gate.reshape(pair_state.shape),
            tri_out,
            jnp.broadcast_to(norm_tri.astype(F32)[:, None], (128, 128)),
            norm_bias.astype(F32)[None],
            heads_first,
        ),
        [
            pltpu.VMEM((128 * 40, 128), F32),
            pltpu.VMEM((16 * 40, 128), F32),
            pltpu.VMEM((128, 40, 128), BF16),
            pltpu.VMEM(pair_state.shape, BF16),
            pltpu.VMEM(pair_state.shape, F32),
            pltpu.VMEM(pair_state.shape, F32),
            pltpu.VMEM((16, 40, 128), BF16),
            pltpu.SemaphoreType.DMA((4,)),
            pltpu.SemaphoreType.DMA((2,)),
            pltpu.SemaphoreType.DMA((10,)),
        ],
        "update",
        flops=2 * 128 * 128 * 5120,
        nbytes=9_000_000,
        spaces=[hbm, hbm, hbm] + [vmem] * 4,
        out_specs=(hbm, hbm),
    )
    bias_in = exchange(bias.reshape(128, 40, 128), ALL).reshape(16, 8, 40, 128)

    pair_scratch = pltpu.VMEM((2 * samples, 2, seq_len, 128), BF16)
    mixed, full_bias, stats = call(
        forward_kernel,
        (
            jax.ShapeDtypeStruct((16, samples, 48, 128), BF16),
            jax.ShapeDtypeStruct((seq_len, seq_len), F32),
            jax.ShapeDtypeStruct((seq_len, 128), F32),
        ),
        (
            bias_in, keep, recv, chain_ids[:, None], column_order(chain_ids[None], 1), place, chain_weight,
        ),
        [
            pair_scratch,
            pltpu.VMEM((16, 8, 40, 128), BF16),
            pltpu.VMEM((16, samples, 48, 128), BF16),
            pltpu.VMEM((seq_len, seq_len), F32),
            pltpu.VMEM((seq_len, 128), F32),
            pltpu.SemaphoreType.DMA((2,)),
            pltpu.SemaphoreType.DMA((2,)),
            pltpu.SemaphoreType.DMA((4,)),
        ],
        "forward",
        flops=6 * 4 * 768 * 768 * 128,
        nbytes=12_000_000,
        spaces=[hbm, hbm, hbm, vmem, vmem, smem, smem],
        out_specs=(hbm, hbm, hbm),
    )
    mixed_in = exchange(mixed, ("core",) + COLS)
    bias_grad = call(
        backward_kernel,
        jax.ShapeDtypeStruct((16, 8, 40, 128), BF16),
        (full_bias, stats, keep, recv),
        [
            pair_scratch,
            pltpu.VMEM((seq_len, seq_len), F32),
            pltpu.VMEM((seq_len, 128), F32),
            pltpu.VMEM((16, 8, 40, 128), BF16),
            pltpu.SemaphoreType.DMA((2,)),
            pltpu.SemaphoreType.DMA((2,)),
            pltpu.SemaphoreType.DMA((768 // BACKWARD_ROWS,)),
        ],
        "backward",
        flops=6 * 4 * 768 * 768 * 128,
        nbytes=12_000_000,
        spaces=[hbm] * 4,
        out_specs=hbm,
    )
    grad_in = exchange(bias_grad.reshape(128, 40, 128), ALL).reshape(8, 16, 40, 128)

    mixed_rows = jnp.concatenate([mixed_in[..., 0:HD], mixed_in[..., 64 : 64 + HD]], axis=2)
    mixed_rows = jnp.transpose(mixed_rows.reshape(2, 8, samples, share_len, HD), (2, 3, 1, 0, 4))
    attn = matmul(mixed_rows.reshape(samples * share_len, model_width), w_out_all)
    state = token_share.reshape(samples * share_len, model_width).astype(F32) + attn
    ff_in = layer_norm(state, norm_ff).astype(BF16)
    hidden = (jax.nn.silu(matmul(ff_in, ff_gate)) * matmul(ff_in, ff_up)).astype(BF16)
    refined = (state + matmul(hidden, ff_down)).reshape(samples, share_len, model_width)

    pair_grad = call(
        pair_grad_kernel,
        jax.ShapeDtypeStruct(pair_state.shape, F32),
        (grad_in, jnp.concatenate([heads_first] * 3, axis=0)),
        [
            pltpu.VMEM((16 * 40, 128), F32),
            pltpu.VMEM((8, 16, 40, 128), BF16),
            pltpu.VMEM(pair_state.shape, F32),
            pltpu.SemaphoreType.DMA((8,)),
            pltpu.SemaphoreType.DMA((2,)),
        ],
        "pair_grad",
        flops=2 * 48 * 128 * 5120,
        nbytes=4_000_000,
        spaces=[hbm, vmem],
        out_specs=hbm,
    )
    return (pair_out, refined, pair_grad)


def solution(mesh):
    fine = Mesh(mesh.devices.reshape(2, 4, 2, 2, 4), ALL)
    pair = P(ROWS, COLS, None)
    sample_rows = P(ROWS, None, None)
    return jax.shard_map(
        body,
        mesh=fine,
        in_specs=(pair, P(), P(), sample_rows, sample_rows)
        + (P(),) * 12
        + (P(None, COLS),) * 3
        + (P(COLS, None),)
        + (P(),) * 4,
        out_specs=(pair, pair, pair),
        check_vma=False,
    )
```

```python
import functools
import jax
import jax.numpy as jnp
from jax import lax
from jax.experimental import pallas as pl
from jax.experimental.pallas import tpu as pltpu
from jax.sharding import Mesh, PartitionSpec as P

HD = 48
F32 = jnp.float32
BF16 = jnp.bfloat16
ROWS = ("grp", "y", "core")
COLS = ("xh", "z")
ALL = ROWS + COLS
LOG2E = 1.4426950408889634
SCALE = HD ** (-0.5) * LOG2E
FORWARD_ROWS = 768
PROJECT_PAR = 12
UPDATE_PAR = 12
THIN_PAR = 16
BACKWARD_ROWS = 192


def layer_norm(value_rows, gain_vec):
    middle = value_rows - jnp.mean(value_rows, axis=-1, keepdims=True)
    spread = jnp.mean(middle * middle, axis=-1, keepdims=True)
    return middle * lax.rsqrt(spread + 1e-05) * gain_vec.astype(F32)


def matmul(left_side, right_side):
    return jnp.dot(left_side, right_side, preferred_element_type=F32)


def dot_nt(a, b):
    return lax.dot_general(a, b, (((1,), (1,)), ((), ())), preferred_element_type=F32)


def dot_tn(a, b):
    return lax.dot_general(a, b, (((0,), (0,)), ((), ())), preferred_element_type=F32)


def lanes_of(rows):
    return lax.broadcasted_iota(jnp.int32, (rows, 128), 1)


def roll(value, shift):
    shift = shift % 128
    return value if shift == 0 else pltpu.roll(value, shift, 1)


def call(kernel, outs, args, scratch, name, flops=0, nbytes=0, spaces=None, grid=None, out_specs=None, mib=60):
    vmem = pl.BlockSpec(memory_space=pltpu.VMEM)
    return pl.pallas_call(
        kernel,
        out_shape=outs,
        in_specs=spaces or [vmem] * len(args),
        out_specs=out_specs or jax.tree.map(lambda _: vmem, outs),
        scratch_shapes=scratch,
        compiler_params=pltpu.CompilerParams(vmem_limit_bytes=mib * 1024 * 1024),
        cost_estimate=pl.CostEstimate(flops=flops, bytes_accessed=nbytes, transcendentals=0),
        name=name,
        **({} if grid is None else {"grid": grid}),
    )(*args)


def start_all(copies):
    for copy in copies:
        copy.start()
    return copies


def wait_all(copies):
    for copy in copies:
        copy.wait()


def project_kernel(
    pair_hbm, gain_ref, pl_hbm, pr_hbm, gl_hbm, gr_hbm, mask_hbm, place_ref, out_hbm, normed_hbm,
    scr, pair_ref, normed_ref, w_ref, out_ref, mask_ref, pair_sems, w_sems, out_sems,
):
    blocks = [pl.ds(512 * n, 512) for n in range(9)]
    pair_copies = start_all(
        [pltpu.make_async_copy(pair_hbm.at[b], pair_ref.at[b], pair_sems.at[n]) for n, b in enumerate(blocks)]
    )
    w_copies = start_all(
        [
            pltpu.make_async_copy(src, w_ref.at[n], w_sems.at[n])
            for n, src in enumerate((pl_hbm, pr_hbm, gl_hbm, gr_hbm))
        ]
        + [pltpu.make_async_copy(mask_hbm, mask_ref, w_sems.at[4])]
    )
    gain = gain_ref[...]
    normed_copies = []
    for n, block in enumerate(blocks):
        pair_copies[n].wait()
        normed_ref[block, :] = layer_norm(pair_ref[block, :].astype(F32), gain).astype(BF16)
        copy = pltpu.make_async_copy(normed_ref.at[block], normed_hbm.at[block], out_sems.at[n])
        copy.start()
        normed_copies.append(copy)
    wait_all(w_copies)
    lane = lanes_of(1)
    row_start = place_ref[0]
    col_start = place_ref[1]
    wide_cols = jnp.zeros((1, 128), F32)
    thin_cols = jnp.zeros((1, 128), F32)
    for k in range(64):
        wide_cols = jnp.where(lane % 64 == k, mask_ref[col_start + k].astype(F32), wide_cols)
    for k in range(32):
        thin_cols = jnp.where(lane % 32 == k, mask_ref[col_start + 64 + k].astype(F32), thin_cols)
    low = lanes_of(128) < 64
    weights = jnp.concatenate([w_ref[n].astype(F32).T.astype(BF16) for n in range(4)], axis=0)

    def rows_at(i, start, size):
        return normed_ref[pl.ds(pl.multiple_of(i * 96 + start, 32), size), :]

    def one(i):
        wide = [rows_at(i, 0, 64), rows_at(i + 24, 0, 64)]
        thin = [rows_at(i, 64, 32), rows_at(i + 24, 64, 32)]
        y = dot_nt(weights, jnp.concatenate(wide + thin + thin, axis=0))
        first = mask_ref[row_start + i].astype(F32)
        second = mask_ref[row_start + i + 24].astype(F32)
        wide_mask = jnp.where(lane < 64, first, second) * wide_cols
        thin_mask = jnp.where(lane % 64 < 32, first, second) * thin_cols
        left = y[0:128, 0:128] * jax.nn.sigmoid(y[256:384, 0:128])
        right = y[128:256, 0:128] * jax.nn.sigmoid(y[384:512, 0:128])
        both_p = jnp.where(low, y[0:128, 128:256], y[128:256, 128:256])
        both_g = jnp.where(low, y[256:384, 128:256], y[384:512, 128:256])
        scr[pl.ds(i, 128, stride=72), :] = left * wide_mask
        scr[pl.ds(i + 24, 128, stride=72), :] = right * wide_mask
        scr[pl.ds(i + 48, 128, stride=72), :] = both_p * jax.nn.sigmoid(both_g) * thin_mask

    def chunk(i, carry):
        for k in range(PROJECT_PAR):
            one(PROJECT_PAR * i + k)
        return carry

    lax.fori_loop(0, 24 // PROJECT_PAR, chunk, 0)
    out_copies = []
    for n in range(8):
        part = scr[1152 * n : 1152 * n + 1152, :].reshape(16, 72, 128)
        out_ref[16 * n : 16 * n + 16] = part.astype(BF16)
        copy = pltpu.make_async_copy(
            out_ref.at[pl.ds(16 * n, 16)], out_hbm.at[pl.ds(16 * n, 16)], out_sems.at[9 + n]
        )
        copy.start()
        out_copies.append(copy)
    wait_all(normed_copies + out_copies)


def token_kernel(
    tokens_ref, grad_ref, gain_ref, wq_ref, wk_ref, wv_ref, wo_ref, core_ref, keep_ref, send_ref, w_scr, wo_scr, norm_scr
):
    even = core_ref[0] == 0

    @pl.when(pl.program_id(0) == 0)
    def _():
        gap = jnp.zeros((768, 16), F32)
        for n, ref in enumerate((wq_ref, wk_ref, wv_ref)):
            w = ref[...].astype(F32)
            w = jnp.concatenate([w[:, 0:48], gap, w[:, 48:96], gap], axis=1)
            w_scr[:, 128 * n : 128 * n + 128] = jnp.where(even, w, roll(w, 64)).astype(BF16)
        first, second = wo_ref[0:48, :], wo_ref[48:96, :]
        wo_scr[0:48, :] = jnp.where(even, first, second)
        wo_scr[64:112, :] = jnp.where(even, second, first)
        wo_scr[48:64, :] = jnp.zeros((16, 768), BF16)
        wo_scr[112:128, :] = jnp.zeros((16, 768), BF16)

    gain = gain_ref[...]

    def norm_block(block, carry):
        rows = pl.ds(pl.multiple_of(block * 96, 32), 96)
        norm_scr[rows, :] = layer_norm(tokens_ref[0, rows, :].astype(F32), gain).astype(BF16)
        return carry

    lax.fori_loop(0, 8, norm_block, 0)
    low = lanes_of(768) < 64
    query = matmul(norm_scr[...], w_scr[:, 0:128])
    grads = dot_nt(grad_ref[0], wo_scr[...])
    keep_ref[0, 0] = jnp.where(low, query, roll(grads, 64)).astype(BF16)
    send_ref[0, 0] = jnp.where(low, roll(query, 64), grads).astype(BF16)
    key = matmul(norm_scr[...], w_scr[:, 128:256])
    value = matmul(norm_scr[...], w_scr[:, 256:384])
    for ref, full in (
        (keep_ref, jnp.where(low, key, roll(value, 64))),
        (send_ref, jnp.where(low, roll(key, 64), value)),
    ):
        full = full.astype(BF16)
        for q in range(8):
            ref[0, 1, 64 * q : 64 * q + 64] = full[96 * q : 96 * q + 64]
            ref[0, 1, 512 + 32 * q : 544 + 32 * q] = full[96 * q + 64 : 96 * q + 96]


def unpack_wide(first, second, low):
    top = jnp.where(low, first, roll(second, 64))
    bottom = jnp.where(low, roll(first, 64), second)
    return top, bottom


def product_kernel(in_hbm, out_hbm, in_ref, out_ref, l_scr, r_scr, in_sems, out_sems):
    copies = start_all(
        [
            pltpu.make_async_copy(
                in_hbm.at[:, pl.ds(4 * u, 4)], in_ref.at[:, pl.ds(4 * u, 4)], in_sems.at[u]
            )
            for u in range(2)
        ]
    )
    lane = lanes_of(384)
    low = lane < 64

    def put(dst, column, full):
        full = full.reshape(768, 128).astype(BF16)
        if dst is l_scr:
            dst[:, column : column + 128] = full
        else:
            for q in range(8):
                dst[64 * q : 64 * q + 64, column : column + 128] = full[96 * q : 96 * q + 64]
                dst[512 + 32 * q : 544 + 32 * q, column : column + 128] = full[96 * q + 64 : 96 * q + 96]

    def stack(halves):
        return jnp.concatenate([h.reshape(16, 24, 128) for h in halves], axis=1)

    def part(value, start):
        return value[:, start : start + 24].reshape(384, 128)

    for u in range(2):
        copies[u].wait()
        blocks = [in_ref[:, 4 * u + v].astype(F32) for v in range(4)]
        for p in range(2):
            for dst, start in ((l_scr, 0), (r_scr, 24)):
                halves = unpack_wide(part(blocks[2 * p], start), part(blocks[2 * p + 1], start), low)
                put(dst, (2 * u + p) * 128, stack(halves))
        thin = [part(b, 48) for b in blocks]
        for dst, base in ((l_scr, 0), (r_scr, 2)):
            halves = []
            for a in range(2):
                parts = [roll(thin[v], 32 * (v - base - a)) for v in range(4)]
                lower = jnp.where(lane < 32, parts[0], parts[1])
                upper = jnp.where(lane < 96, parts[2], parts[3])
                halves.append(jnp.where(low, lower, upper))
            put(dst, 512 + u * 128, stack(halves))
    out_copies = []
    for b in range(4):
        product = dot_nt(l_scr[192 * b : 192 * b + 192, :], r_scr[...])
        pack_rows(product, out_ref, 4 * b, 4)
        copy = pltpu.make_async_copy(
            out_ref.at[pl.ds(4 * b, 4)], out_hbm.at[pl.ds(4 * b, 4)], out_sems.at[b]
        )
        copy.start()
        out_copies.append(copy)
    wait_all(out_copies)


def pack_rows(full, out_ref, first, count):
    low = lanes_of(count * 24) < 64
    lane = lanes_of(count * 16)
    for q in range(8):
        tile = full[:, 128 * (q // 2) : 128 * (q // 2) + 128].reshape(count, 48, 128)
        top = tile[:, 0:24].reshape(count * 24, 128)
        bottom = tile[:, 24:48].reshape(count * 24, 128)
        if q % 2 == 0:
            wide = jnp.where(low, top, roll(bottom, 64))
        else:
            wide = jnp.where(low, roll(top, 64), bottom)
        tile = full[:, 512 + 128 * (q // 4) : 640 + 128 * (q // 4)].reshape(count, 48, 128)
        thin = [
            roll(tile[:, 16 * m : 16 * m + 16].reshape(count * 16, 128), 32 * (m - q % 4))
            for m in range(3)
        ]
        thin = jnp.where(lane < 32, thin[0], jnp.where(lane < 64, thin[1], thin[2]))
        piece = jnp.concatenate(
            [wide.reshape(count, 24, 128), thin.reshape(count, 16, 128)], axis=1
        )
        out_ref[pl.ds(first, count), q] = piece.astype(BF16)


def transition_kernel(
    mixed_hbm, ring_hbm, far_hbm, place_ref, token_hbm, gain_ref, gate_hbm, up_hbm, down_hbm, out_hbm,
    mixed_ref, wo_ref, token_ref, gate_ref, up_ref, down_ref, x_ref, out_ref, sems, wo_sems, out_sems,
):
    pairs = ((mixed_hbm, mixed_ref), (token_hbm, token_ref), (gate_hbm, gate_ref), (up_hbm, up_ref), (down_hbm, down_ref))
    wo_copies = []
    for far, src in ((0, ring_hbm), (1, far_hbm)):
        for n in range(8):
            core = lax.rem(place_ref[2] + far, 2)
            high = lax.rem(place_ref[4] + n // 4, 2)
            block = core * 8 + high * 4 + lax.rem(place_ref[5] + n, 4)
            wo_copies.append(
                pltpu.make_async_copy(src.at[n], wo_ref.at[block, pl.ds(0, 48)], wo_sems.at[8 * far + n])
            )
    start_all(wo_copies)
    copies = start_all([pltpu.make_async_copy(src, dst, sems.at[n]) for n, (src, dst) in enumerate(pairs)])
    wo_ref[:, 48:64, :] = jnp.zeros((16, 16, 768), BF16)
    copies[0].wait()
    low = lanes_of(144) < 64
    for n in range(8):
        first = mixed_ref[2 * n].reshape(144, 128).astype(F32)
        second = mixed_ref[2 * n + 1].reshape(144, 128).astype(F32)
        top, bottom = unpack_wide(first, second, low)
        x_ref[0:144, 128 * n : 128 * n + 128] = top.astype(BF16)
        x_ref[144:288, 128 * n : 128 * n + 128] = bottom.astype(BF16)
    wait_all(wo_copies)
    attn = matmul(x_ref[...], wo_ref[...].reshape(1024, 768))
    copies[1].wait()
    token = jnp.concatenate([token_ref[s, 48 * half : 48 * half + 48] for half in range(2) for s in range(3)], axis=0)
    state = token.astype(F32) + attn
    fed = layer_norm(state, gain_ref[...]).astype(BF16)
    wait_all(copies[2:])
    refined = state
    for n in range(3):
        cols = slice(512 * n, 512 * n + 512)
        hidden = jax.nn.silu(matmul(fed, gate_ref[:, cols])) * matmul(fed, up_ref[:, cols])
        refined = refined + matmul(hidden.astype(BF16), down_ref[cols, :])
    for half in range(2):
        for s in range(3):
            at = 144 * half + 48 * s
            out_ref[s, 48 * half : 48 * half + 48] = refined[at : at + 48]
    copy = pltpu.make_async_copy(out_ref, out_hbm, out_sems.at[0])
    copy.start()
    copy.wait()


def wide_places(i):
    return [(i, 0, 64), (i + 24, 0, 64)]


def thin_places(i):
    return [(i + 16 * m, 64, 32) for m in range(3)]


def update_kernel(
    t_hbm, pair_hbm, gate_hbm, w_ref, tri_gain_ref, bias_gain_ref, bp_ref, out_hbm, bias_hbm,
    scr, b_scr, t_ref, pair_ref, gate_ref, out_ref, bias_ref, t_sems, sems, out_sems,
):
    t_copies = start_all(
        [
            pltpu.make_async_copy(t_hbm.at[pl.ds(32 * n, 32)], t_ref.at[pl.ds(32 * n, 32)], t_sems.at[n])
            for n in range(4)
        ]
    )
    copies = start_all(
        [
            pltpu.make_async_copy(pair_hbm, pair_ref, sems.at[0]),
            pltpu.make_async_copy(gate_hbm, gate_ref, sems.at[1]),
        ]
    )
    for n in range(4):
        t_copies[n].wait()
        scr[1280 * n : 1280 * n + 1280, :] = t_ref[32 * n : 32 * n + 32].astype(F32).reshape(1280, 128)
    wait_all(copies)
    weight = w_ref[...]
    tri_gain = tri_gain_ref[...]
    bias_gain = bias_gain_ref[...]
    bias_proj = bp_ref[...]

    def group(positions, places):
        normed = []
        for position in positions:
            tri = scr[pl.ds(position, 128, stride=40), :]
            middle = tri - jnp.mean(tri, axis=0, keepdims=True)
            spread_of = jnp.mean(middle * middle, axis=0, keepdims=True)
            normed.append((middle * lax.rsqrt(spread_of + 1e-05) * tri_gain).astype(BF16))
        update = dot_tn(jnp.concatenate(normed, axis=1), weight)
        fed = []
        for n, spots in enumerate(places):
            at = 128 * n
            for row, start, size in spots:
                cols = pl.ds(start, size)
                new = pair_ref[row, cols, :].astype(F32) + gate_ref[row, cols, :] * update[at : at + size]
                out_ref[row, cols, :] = new
                fed.append(layer_norm(new, bias_gain).astype(BF16))
                at += size
            if len(spots) == 3:
                fed.append(fed[-1])
        bias = dot_nt(bias_proj, jnp.concatenate(fed, axis=0))
        for n, position in enumerate(positions):
            b_scr[pl.ds(position, 16, stride=40), :] = bias[:, 128 * n : 128 * n + 128]

    par, par2 = UPDATE_PAR, THIN_PAR

    def wide(i, carry):
        group([par * i + n for n in range(par)], [wide_places(par * i + n) for n in range(par)])
        return carry

    def thin(i, carry):
        group([24 + par2 * i + n for n in range(par2)], [thin_places(par2 * i + n) for n in range(par2)])
        return carry

    lax.fori_loop(0, 24 // par, wide, 0)
    out_copies = [
        pltpu.make_async_copy(out_ref.at[:, pl.ds(c, n)], out_hbm.at[:, pl.ds(c, n)], out_sems.at[8 + k])
        for k, (c, n) in enumerate(((0, 64), (64, 32)))
    ]
    out_copies[0].start()
    lax.fori_loop(0, 16 // par2, thin, 0)
    out_copies[1].start()
    bias_ref[...] = b_scr[...].reshape(16, 40, 128).astype(BF16)
    out_copies += start_all(
        [pltpu.make_async_copy(bias_ref, bias_hbm.at[n], out_sems.at[n]) for n in range(8)]
    )
    wait_all(out_copies)


def unpack_bias(bias_ref, copies, put):
    low = lanes_of(384) < 64
    lane = lanes_of(256)
    for u in range(2):
        copies[u].wait()
        blocks = [bias_ref[:, 4 * u + v].astype(F32) for v in range(4)]
        for p in range(2):
            halves = unpack_wide(
                blocks[2 * p][:, 0:24].reshape(384, 128),
                blocks[2 * p + 1][:, 0:24].reshape(384, 128),
                low,
            )
            put((2 * u + p) * 128, jnp.concatenate([h.reshape(16, 24, 128) for h in halves], axis=1))
        thin = [b[:, 24:40].reshape(256, 128) for b in blocks]
        thirds = []
        for m in range(3):
            parts = [roll(thin[v], 32 * (v - m)) for v in range(4)]
            lower = jnp.where(lane < 32, parts[0], parts[1])
            upper = jnp.where(lane < 96, parts[2], parts[3])
            thirds.append(jnp.where(lane < 64, lower, upper).reshape(16, 16, 128))
        put(512 + u * 128, jnp.concatenate(thirds, axis=1))


def pair_copies(keep_hbm, recv_hbm, pairs, sems):
    return start_all(
        [
            pltpu.make_async_copy(src, pairs.at[pl.ds(3 * n, 3)], sems.at[n])
            for n, src in enumerate((keep_hbm, recv_hbm))
        ]
    )


def forward_kernel(
    bias_hbm, keep_hbm, recv_hbm, chain_row_ref, chain_col_ref, place_ref, weight_ref,
    mixed_hbm, full_hbm, stats_hbm, pairs, bias_ref, mixed_ref, full_ref, stats_ref, sems, in_sems, out_sems,
):
    bias_copies = start_all(
        [
            pltpu.make_async_copy(
                bias_hbm.at[:, pl.ds(4 * u, 4)], bias_ref.at[:, pl.ds(4 * u, 4)], in_sems.at[u]
            )
            for u in range(2)
        ]
    )
    copies = pair_copies(keep_hbm, recv_hbm, pairs, sems)
    core = place_ref[2]
    head_weight = weight_ref[place_ref[3]] * LOG2E

    def put(column, full):
        same = chain_row_ref[...] == chain_col_ref[:, column : column + 128]
        full_ref[:, column : column + 128] = full.reshape(768, 128) * LOG2E + jnp.where(
            same, head_weight, 0.0
        )

    unpack_bias(bias_ref, bias_copies, put)
    full_copy = pltpu.make_async_copy(full_ref, full_hbm, out_sems.at[0])
    full_copy.start()
    stats_ref[...] = jnp.zeros_like(stats_ref)
    wait_all(copies)
    low_all = lanes_of(768) < 64
    lane = lanes_of(FORWARD_ROWS)
    low = lane < 64
    thin_low = lanes_of(48) < 64
    blocks = 768 // FORWARD_ROWS
    shares = FORWARD_ROWS // 96

    def block(s, b, owner, slot):
        both = pairs[s, 1]
        keys = jnp.where(low_all, both, jnp.zeros_like(both))
        rows = pl.ds(pl.multiple_of(b * FORWARD_ROWS, 32), FORWARD_ROWS)
        asked = pairs[s, 0, rows, :]
        weights = jnp.exp2(dot_nt(asked, keys) * SCALE + full_ref[rows, :])
        inverse = 1.0 / jnp.sum(weights, axis=-1, keepdims=True)
        mixed = matmul((weights * inverse).astype(BF16), both)
        center = jnp.sum(jnp.where(low, 0.0, asked.astype(F32) * mixed), axis=-1, keepdims=True)
        stats_ref[rows, :] = jnp.where(
            lane == s, inverse, jnp.where(lane == s + 64, center, stats_ref[rows, :])
        )
        for n in range(shares):
            mixed_ref[owner * 8 + b * shares + n, slot] = jnp.where(
                thin_low, roll(mixed[96 * n : 96 * n + 48], 64), mixed[96 * n + 48 : 96 * n + 96]
            ).astype(BF16)

    def step(i, carry):
        half = i // blocks
        owner = jnp.where(half == 0, core, 1 - core)
        for n in range(3):
            block(3 * half + n, i % blocks, owner, n)
        return carry

    def mixed_copy(owner, sem):
        part = pl.ds(owner * 8, 8)
        return pltpu.make_async_copy(mixed_ref.at[part], mixed_hbm.at[part], out_sems.at[sem])

    lax.fori_loop(0, blocks, step, 0)
    mixed_copy(core, 1).start()
    lax.fori_loop(blocks, 2 * blocks, step, 0)
    mixed_copy(1 - core, 2).start()
    stats_copy = pltpu.make_async_copy(stats_ref, stats_hbm, out_sems.at[3])
    stats_copy.start()
    mixed_copy(core, 1).wait()
    mixed_copy(1 - core, 2).wait()
    full_copy.wait()
    stats_copy.wait()


def backward_kernel(
    full_hbm, stats_hbm, keep_hbm, recv_hbm, grad_hbm, pairs, full_ref, stats_ref, grad_ref, sems, in_sems, out_sems
):
    copies = pair_copies(keep_hbm, recv_hbm, pairs, sems)
    copies += start_all([pltpu.make_async_copy(stats_hbm, stats_ref, in_sems.at[0])])
    copies += start_all([pltpu.make_async_copy(full_hbm, full_ref, in_sems.at[1])])
    wait_all(copies)
    low_all = lanes_of(768) < 64

    def row_block(b, carry):
        rows = pl.ds(pl.multiple_of(b * BACKWARD_ROWS, 32), BACKWARD_ROWS)
        total = None
        for s in range(6):
            both = pairs[s, 1]
            keys = jnp.where(low_all, both, jnp.zeros_like(both))
            values = jnp.where(low_all, jnp.zeros_like(both), both)
            asked = pairs[s, 0, rows, :]
            inverse = stats_ref[rows, s : s + 1]
            center = stats_ref[rows, s + 64 : s + 65]
            probs = jnp.exp2(dot_nt(asked, keys) * SCALE + full_ref[rows, :]) * inverse
            score_grad = probs * (dot_nt(asked, values) - center)
            total = score_grad if total is None else total + score_grad
        pack_rows(total, grad_ref, b * (BACKWARD_ROWS // 48), BACKWARD_ROWS // 48)
        grad_copy(b).start()
        return carry

    def grad_copy(b):
        part = pl.ds(b * (BACKWARD_ROWS // 48), BACKWARD_ROWS // 48)
        return pltpu.make_async_copy(grad_ref.at[part], grad_hbm.at[part], out_sems.at[b])

    lax.fori_loop(0, 768 // BACKWARD_ROWS, row_block, 0)
    wait_all([grad_copy(b) for b in range(768 // BACKWARD_ROWS)])


def pair_grad_kernel(in_hbm, w_ref, out_hbm, scr, in_ref, out_ref, in_sems, out_sems):
    copies = start_all([pltpu.make_async_copy(in_hbm.at[n], in_ref.at[n], in_sems.at[n]) for n in range(8)])
    total = None
    for n in range(8):
        copies[n].wait()
        part = in_ref[n].astype(F32)
        total = part if total is None else total + part
    scr[...] = total.reshape(640, 128)
    weight = w_ref[...]

    def group(positions, places):
        grad = jnp.concatenate([scr[pl.ds(p, 16, stride=40), :] for p in positions], axis=1)
        high = grad.astype(BF16)
        rest = grad - high.astype(F32)
        middle = rest.astype(BF16)
        least = (rest - middle.astype(F32)).astype(BF16)
        rows = dot_tn(jnp.concatenate([high, middle, least], axis=0), weight)
        for n, spots in enumerate(places):
            at = 128 * n
            for row, start, size in spots:
                out_ref[row, pl.ds(start, size), :] = rows[at : at + size]
                at += size

    par, par2 = UPDATE_PAR, THIN_PAR

    def wide(i, carry):
        group([par * i + n for n in range(par)], [wide_places(par * i + n) for n in range(par)])
        return carry

    def thin(i, carry):
        group([24 + par2 * i + n for n in range(par2)], [thin_places(par2 * i + n) for n in range(par2)])
        return carry

    lax.fori_loop(0, 24 // par, wide, 0)
    out_copies = [
        pltpu.make_async_copy(out_ref.at[:, pl.ds(c, n)], out_hbm.at[:, pl.ds(c, n)], out_sems.at[k])
        for k, (c, n) in enumerate(((0, 64), (64, 32)))
    ]
    out_copies[0].start()
    lax.fori_loop(0, 16 // par2, thin, 0)
    out_copies[1].start()
    wait_all(out_copies)


def column_order(value, axis):
    shape = value.shape
    split = value.reshape(shape[:axis] + (8, 96) + shape[axis + 1 :])
    wide = lax.slice_in_dim(split, 0, 64, axis=axis + 1).reshape(shape[:axis] + (512,) + shape[axis + 1 :])
    thin = lax.slice_in_dim(split, 64, 96, axis=axis + 1).reshape(shape[:axis] + (256,) + shape[axis + 1 :])
    return jnp.concatenate([wide, thin], axis=axis)


def memory(space):
    return pl.BlockSpec(memory_space=space)


VMEM, SMEM, HBM = memory(pltpu.VMEM), memory(pltpu.SMEM), memory(pltpu.HBM)
TILE = (48, 96, 128)
PACKED = (16, 8, 40, 128)


def shape(dims, dtype=BF16):
    return jax.ShapeDtypeStruct(dims, dtype)


def dma(count):
    return pltpu.SemaphoreType.DMA((count,))


def run_project(*args):
    return call(
        project_kernel,
        (shape((128, 72, 128)), shape((4608, 128))),
        args,
        [
            pltpu.VMEM((128 * 72, 128), F32),
            pltpu.VMEM((4608, 128), BF16),
            pltpu.VMEM((4608, 128), BF16),
            pltpu.VMEM((4, 128, 128), BF16),
            pltpu.VMEM((128, 72, 128), BF16),
            pltpu.SMEM((768,), jnp.int32),
            dma(9),
            dma(5),
            dma(17),
        ],
        "project",
        flops=2 * 512 * 128 * 6144,
        nbytes=5_000_000,
        spaces=[HBM, VMEM] + [HBM] * 5 + [SMEM],
        out_specs=(HBM, HBM),
    )


def run_tokens(samples, *args):
    part = shape((samples, 2, 768, 128))
    token_block = pl.BlockSpec((1, 768, 768), lambda s: (s, 0, 0))
    part_block = pl.BlockSpec((1, 2, 768, 128), lambda s: (s, 0, 0, 0))
    return call(
        token_kernel,
        (part, part),
        args,
        [pltpu.VMEM((768, 384), BF16), pltpu.VMEM((128, 768), BF16), pltpu.VMEM((768, 768), BF16)],
        "tokens",
        flops=2 * 2304 * 768 * 512,
        nbytes=12_000_000,
        spaces=[token_block, token_block] + [VMEM] * 5 + [SMEM],
        grid=(samples,),
        out_specs=(part_block, part_block),
    )


def run_product(*args):
    return call(
        product_kernel,
        shape(PACKED),
        args,
        [
            pltpu.VMEM((16, 8, 72, 128), BF16),
            pltpu.VMEM(PACKED, BF16),
            pltpu.VMEM((768, 768), BF16),
            pltpu.VMEM((768, 768), BF16),
            dma(2),
            dma(4),
        ],
        "product",
        flops=2 * 768**3,
        nbytes=4_000_000,
        spaces=[HBM],
        out_specs=HBM,
        mib=50,
    )


def run_update(*args):
    return call(
        update_kernel,
        (shape(TILE, F32), shape((8, 16, 40, 128))),
        args,
        [
            pltpu.VMEM((128 * 40, 128), F32),
            pltpu.VMEM((16 * 40, 128), F32),
            pltpu.VMEM((128, 40, 128), BF16),
            pltpu.VMEM(TILE, BF16),
            pltpu.VMEM(TILE, F32),
            pltpu.VMEM(TILE, F32),
            pltpu.VMEM((16, 40, 128), BF16),
            dma(4),
            dma(2),
            dma(10),
        ],
        "update",
        flops=2 * 128 * 128 * 5120,
        nbytes=9_000_000,
        spaces=[HBM, HBM, HBM] + [VMEM] * 4,
        out_specs=(HBM, HBM),
        mib=52,
    )


def run_forward(*args):
    return call(
        forward_kernel,
        (shape((16, 3, 48, 128)), shape((768, 768), F32), shape((768, 128), F32)),
        args,
        [
            pltpu.VMEM((6, 2, 768, 128), BF16),
            pltpu.VMEM(PACKED, BF16),
            pltpu.VMEM((16, 3, 48, 128), BF16),
            pltpu.VMEM((768, 768), F32),
            pltpu.VMEM((768, 128), F32),
            dma(2),
            dma(2),
            dma(4),
        ],
        "forward",
        flops=6 * 4 * 768 * 768 * 128,
        nbytes=12_000_000,
        spaces=[HBM, HBM, HBM, VMEM, VMEM, SMEM, SMEM],
        out_specs=(HBM, HBM, HBM),
        mib=51,
    )


def run_backward(*args):
    return call(
        backward_kernel,
        shape(PACKED),
        args,
        [
            pltpu.VMEM((6, 2, 768, 128), BF16),
            pltpu.VMEM((768, 768), F32),
            pltpu.VMEM((768, 128), F32),
            pltpu.VMEM(PACKED, BF16),
            dma(2),
            dma(2),
            dma(768 // BACKWARD_ROWS),
        ],
        "backward",
        flops=6 * 4 * 768 * 768 * 128,
        nbytes=12_000_000,
        spaces=[HBM] * 4,
        out_specs=HBM,
    )


def run_pair_grad(*args):
    return call(
        pair_grad_kernel,
        shape(TILE, F32),
        args,
        [
            pltpu.VMEM((16 * 40, 128), F32),
            pltpu.VMEM((8, 16, 40, 128), BF16),
            pltpu.VMEM(TILE, F32),
            dma(8),
            dma(2),
        ],
        "pair_grad",
        flops=2 * 48 * 128 * 5120,
        nbytes=4_000_000,
        spaces=[HBM, VMEM],
        out_specs=HBM,
        mib=52,
    )


def run_transition(*args):
    return call(
        transition_kernel,
        shape((3, 96, 768), F32),
        args,
        [
            pltpu.VMEM((16, 3, 48, 128), BF16),
            pltpu.VMEM((16, 64, 768), BF16),
            pltpu.VMEM((3, 96, 768), BF16),
            pltpu.VMEM((768, 1536), BF16),
            pltpu.VMEM((768, 1536), BF16),
            pltpu.VMEM((1536, 768), BF16),
            pltpu.VMEM((288, 1024), BF16),
            pltpu.VMEM((3, 96, 768), F32),
            dma(5),
            dma(16),
            dma(1),
        ],
        "transition",
        flops=2 * 288 * 768 * (1024 + 3 * 1536),
        nbytes=12_000_000,
        spaces=[HBM] * 3 + [SMEM, HBM, VMEM] + [HBM] * 3,
        out_specs=HBM,
        mib=51,
    )


def exchange(value, axes):
    return lax.all_to_all(value, axes, 0, 0, tiled=True)


SWAP = [(0, 1), (1, 0)]


def gather_ring(half):
    ring = [half] + [lax.ppermute(half, "z", [(i, (i - k) % 4) for i in range(4)]) for k in range(1, 4)]
    return jnp.stack(ring)


def body(
    pair_state,
    pair_mask,
    chain_ids,
    tokens,
    grad_attn,
    norm_pair,
    proj_left,
    gate_left,
    proj_right,
    gate_right,
    gate_out,
    norm_tri,
    tri_out,
    norm_bias,
    bias_proj,
    chain_weight,
    norm_tokens,
    w_query,
    w_key,
    w_value,
    w_out,
    norm_ff,
    ff_gate,
    ff_up,
    ff_down,
):
    tile_rows, tile_cols, channels = pair_state.shape
    tile_size = tile_rows * tile_cols
    row_start = lax.axis_index(ROWS) * tile_rows
    col_index = lax.axis_index(COLS)
    col_start = col_index * tile_cols
    pair_flat = pair_state.reshape(tile_size, channels)

    core_index = lax.axis_index("core")
    place = jnp.stack(
        [row_start, col_start, core_index, 2 * col_index + core_index, lax.axis_index("xh"), lax.axis_index("z")]
    ).astype(jnp.int32)

    sides, normed = run_project(
        pair_flat, norm_pair.astype(F32)[None], proj_left, proj_right, gate_left, gate_right, pair_mask, place
    )
    sides_in = exchange(sides, ALL)

    samples, seq_len, model_width = tokens.shape
    keep, send = run_tokens(
        samples, tokens, grad_attn, norm_tokens.astype(F32)[None], w_query, w_key, w_value, w_out, place[2:3]
    )
    keep, send, w_out_late = lax.optimization_barrier((keep, send, w_out))
    ring = gather_ring(lax.dynamic_slice_in_dim(w_out_late, core_index * HD, HD, 0))
    sides_in, keep, send, ring = lax.optimization_barrier((sides_in, keep, send, ring))
    recv = lax.ppermute(send, "core", SWAP)
    products = run_product(sides_in.reshape(16, 8, 72, 128))
    rings = jnp.concatenate([ring, lax.ppermute(ring, "xh", SWAP)], axis=0)
    products, rings = lax.optimization_barrier((products, rings))
    tri_in = exchange(products.reshape(128, 40, 128), ALL)
    share_len = seq_len // 8
    token_share = lax.dynamic_slice_in_dim(tokens, col_index * share_len, share_len, 1)
    gate = jax.nn.sigmoid(matmul(normed, gate_out)).reshape(pair_state.shape)
    heads_first = jnp.transpose(bias_proj.T.reshape(8, 2, 128), (1, 0, 2)).reshape(16, 128)
    tri_gain = jnp.broadcast_to(norm_tri.astype(F32)[:, None], (128, 128))
    bias_gain = norm_bias.astype(F32)[None]
    ff_gain = norm_ff.astype(F32)[None]
    triple = jnp.concatenate([heads_first] * 3, axis=0)
    chain_row, chain_col = chain_ids[:, None], column_order(chain_ids[None], 1)
    (
        tri_in, recv, token_share, gate, heads_first, tri_gain, bias_gain, ff_gain, triple, chain_row, chain_col
    ) = lax.optimization_barrier(
        (
            tri_in, recv, token_share, gate, heads_first, tri_gain, bias_gain, ff_gain, triple, chain_row, chain_col
        )
    )

    pair_out, bias = run_update(
        tri_in,
        pair_state,
        gate,
        tri_out,
        tri_gain,
        bias_gain,
        heads_first,
    )
    bias_in = exchange(bias.reshape(128, 40, 128), ALL).reshape(PACKED)

    bias_in, rings = lax.optimization_barrier((bias_in, rings))
    far_rings = lax.ppermute(rings, "core", SWAP)

    mixed, full_bias, stats = run_forward(
        bias_in, keep, recv, chain_row, chain_col, place, chain_weight
    )
    mixed_in = exchange(mixed, ("core",) + COLS)
    bias_grad = run_backward(full_bias, stats, keep, recv)
    grad_in = exchange(bias_grad.reshape(128, 40, 128), ALL).reshape(8, 16, 40, 128)

    refined = run_transition(
        mixed_in, rings, far_rings, place, token_share, ff_gain, ff_gate, ff_up, ff_down
    )

    pair_grad = run_pair_grad(grad_in, triple)
    return (pair_out, refined, pair_grad)


def solution(mesh):
    fine = Mesh(mesh.devices.reshape(2, 4, 2, 2, 4), ALL)
    pair = P(ROWS, COLS, None)
    sample_rows = P(ROWS, None, None)
    return jax.shard_map(
        body,
        mesh=fine,
        in_specs=(pair, P(), P(), sample_rows, sample_rows)
        + (P(),) * 12
        + (P(None, COLS),) * 3
        + (P(COLS, None),)
        + (P(),) * 4,
        out_specs=(pair, pair, pair),
        check_vma=False,
    )
```

```python
import functools
import jax
import jax.numpy as jnp
from jax import lax
from jax.experimental import pallas as pl
from jax.experimental.pallas import tpu as pltpu
from jax.sharding import Mesh, PartitionSpec as P

HD = 48
F32 = jnp.float32
BF16 = jnp.bfloat16
ROWS = ("grp", "y", "core")
COLS = ("xh", "z")
ALL = ROWS + COLS
LOG2E = 1.4426950408889634
SCALE = HD ** (-0.5) * LOG2E
FORWARD_ROWS = 768
UPDATE_PAR = 12
THIN_PAR = 16
BACKWARD_ROWS = 384


def layer_norm(value_rows, gain_vec):
    middle = value_rows - jnp.mean(value_rows, axis=-1, keepdims=True)
    spread = jnp.mean(middle * middle, axis=-1, keepdims=True)
    return middle * lax.rsqrt(spread + 1e-05) * gain_vec.astype(F32)


def matmul(left_side, right_side):
    return jnp.dot(left_side, right_side, preferred_element_type=F32)


def dot_nt(a, b):
    return lax.dot_general(a, b, (((1,), (1,)), ((), ())), preferred_element_type=F32)


def dot_tn(a, b):
    return lax.dot_general(a, b, (((0,), (0,)), ((), ())), preferred_element_type=F32)


def lanes_of(rows):
    return lax.broadcasted_iota(jnp.int32, (rows, 128), 1)


def roll(value, shift):
    shift = shift % 128
    return value if shift == 0 else pltpu.roll(value, shift, 1)


def call(kernel, outs, args, scratch, name, flops=0, nbytes=0, spaces=None, grid=None, out_specs=None, mib=60):
    vmem = pl.BlockSpec(memory_space=pltpu.VMEM)
    return pl.pallas_call(
        kernel,
        out_shape=outs,
        in_specs=spaces or [vmem] * len(args),
        out_specs=out_specs or jax.tree.map(lambda _: vmem, outs),
        scratch_shapes=scratch,
        compiler_params=pltpu.CompilerParams(vmem_limit_bytes=int(mib * 1024 * 1024)),
        cost_estimate=pl.CostEstimate(flops=flops, bytes_accessed=nbytes, transcendentals=0),
        name=name,
        **({} if grid is None else {"grid": grid}),
    )(*args)


def start_all(copies):
    for copy in copies:
        copy.start()
    return copies


def wait_all(copies):
    for copy in copies:
        copy.wait()


def project_kernel(
    pair_hbm, gain_ref, pl_hbm, pr_hbm, gl_hbm, gr_hbm, mask_hbm, out_hbm, normed_hbm,
    scr, pair_ref, normed_ref, w_ref, out_ref, mask_ref, pair_sems, w_sems, out_sems,
):
    blocks = [pl.ds(2304 * (n % 2) + 576 * (n // 2), 576) for n in range(8)]
    pair_copies = start_all(
        [pltpu.make_async_copy(pair_hbm.at[b], pair_ref.at[b], pair_sems.at[n]) for n, b in enumerate(blocks)]
    )
    w_copies = start_all(
        [
            pltpu.make_async_copy(src, w_ref.at[n], w_sems.at[n])
            for n, src in enumerate((pl_hbm, pr_hbm, gl_hbm, gr_hbm))
        ]
        + [pltpu.make_async_copy(mask_hbm, mask_ref, w_sems.at[4])]
    )
    gain = gain_ref[...].astype(F32).reshape(1, 128)
    normed_copies = []

    def norm_block(n):
        block = blocks[n]
        pair_copies[n].wait()
        normed_ref[block, :] = layer_norm(pair_ref[block, :].astype(F32), gain).astype(BF16)
        copy = pltpu.make_async_copy(normed_ref.at[block], normed_hbm.at[block], out_sems.at[n])
        copy.start()
        normed_copies.append(copy)

    norm_block(0)
    norm_block(1)
    wait_all(w_copies)
    lane = lanes_of(1)
    row_start = lax.axis_index(ROWS) * 48
    col_start = lax.axis_index(COLS) * 96
    wide_cols = jnp.zeros((1, 128), F32)
    thin_cols = jnp.zeros((1, 128), F32)
    for k in range(64):
        wide_cols = jnp.where(lane % 64 == k, mask_ref[col_start + k].astype(F32), wide_cols)
    for k in range(32):
        thin_cols = jnp.where(lane % 32 == k, mask_ref[col_start + 64 + k].astype(F32), thin_cols)
    low = lanes_of(128) < 64
    weights = jnp.concatenate([w_ref[n].astype(F32).T.astype(BF16) for n in range(4)], axis=0)

    def rows_at(i, start, size):
        return normed_ref[pl.ds(pl.multiple_of(i * 96 + start, 32), size), :]

    def one(i):
        wide = [rows_at(i, 0, 64), rows_at(i + 24, 0, 64)]
        thin = [rows_at(i, 64, 32), rows_at(i + 24, 64, 32)]
        y = dot_nt(weights, jnp.concatenate(wide + thin + thin, axis=0))
        first = mask_ref[row_start + i].astype(F32)
        second = mask_ref[row_start + i + 24].astype(F32)
        wide_mask = jnp.where(lane < 64, first, second) * wide_cols
        thin_mask = jnp.where(lane % 64 < 32, first, second) * thin_cols
        left = y[0:128, 0:128] * jax.nn.sigmoid(y[256:384, 0:128])
        right = y[128:256, 0:128] * jax.nn.sigmoid(y[384:512, 0:128])
        both_p = jnp.where(low, y[0:128, 128:256], y[128:256, 128:256])
        both_g = jnp.where(low, y[256:384, 128:256], y[384:512, 128:256])
        scr[pl.ds(i, 128, stride=72), :] = left * wide_mask
        scr[pl.ds(i + 24, 128, stride=72), :] = right * wide_mask
        scr[pl.ds(i + 48, 128, stride=72), :] = both_p * jax.nn.sigmoid(both_g) * thin_mask

    for m in range(4):
        if m < 3:
            norm_block(2 * m + 2)
            norm_block(2 * m + 3)
        for k in range(6):
            one(6 * m + k)
    out_copies = []
    for n in range(8):
        part = scr[1152 * n : 1152 * n + 1152, :].reshape(16, 72, 128)
        out_ref[16 * n : 16 * n + 16] = part.astype(BF16)
        copy = pltpu.make_async_copy(
            out_ref.at[pl.ds(16 * n, 16)], out_hbm.at[pl.ds(16 * n, 16)], out_sems.at[9 + n]
        )
        copy.start()
        out_copies.append(copy)
    wait_all(normed_copies + out_copies)


def token_kernel(
    tokens_ref, grad_ref, gain_ref, wq_ref, wk_ref, wv_ref, wo_ref, core_ref, keep_ref, send_ref, w_scr, wo_scr, norm_scr
):
    even = core_ref[0] == 0

    @pl.when(pl.program_id(0) == 0)
    def _():
        gap = jnp.zeros((768, 16), F32)
        for n, ref in enumerate((wq_ref, wk_ref, wv_ref)):
            w = ref[...].astype(F32)
            w = jnp.concatenate([w[:, 0:48], gap, w[:, 48:96], gap], axis=1)
            w_scr[:, 128 * n : 128 * n + 128] = jnp.where(even, w, roll(w, 64)).astype(BF16)
        first, second = wo_ref[0:48, :], wo_ref[48:96, :]
        wo_scr[0:48, :] = jnp.where(even, first, second)
        wo_scr[64:112, :] = jnp.where(even, second, first)
        wo_scr[48:64, :] = jnp.zeros((16, 768), BF16)
        wo_scr[112:128, :] = jnp.zeros((16, 768), BF16)

    gain = gain_ref[...]

    def norm_block(block, carry):
        rows = pl.ds(pl.multiple_of(block * 96, 32), 96)
        norm_scr[rows, :] = layer_norm(tokens_ref[0, rows, :].astype(F32), gain).astype(BF16)
        return carry

    lax.fori_loop(0, 8, norm_block, 0)
    low = lanes_of(768) < 64
    query = matmul(norm_scr[...], w_scr[:, 0:128])
    grads = dot_nt(grad_ref[0], wo_scr[...])
    keep_ref[0, 0] = jnp.where(low, query, roll(grads, 64)).astype(BF16)
    send_ref[0, 0] = jnp.where(low, roll(query, 64), grads).astype(BF16)
    key = matmul(norm_scr[...], w_scr[:, 128:256])
    value = matmul(norm_scr[...], w_scr[:, 256:384])
    for ref, full in (
        (keep_ref, jnp.where(low, key, roll(value, 64))),
        (send_ref, jnp.where(low, roll(key, 64), value)),
    ):
        full = full.astype(BF16)
        for q in range(8):
            ref[0, 1, 64 * q : 64 * q + 64] = full[96 * q : 96 * q + 64]
            ref[0, 1, 512 + 32 * q : 544 + 32 * q] = full[96 * q + 64 : 96 * q + 96]


def unpack_wide(first, second, low):
    top = jnp.where(low, first, roll(second, 64))
    bottom = jnp.where(low, roll(first, 64), second)
    return top, bottom


def product_kernel(in_hbm, out_hbm, in_ref, out_ref, l_scr, r_scr, in_sems, out_sems):
    copies = start_all(
        [
            pltpu.make_async_copy(
                in_hbm.at[:, pl.ds(4 * u, 4)], in_ref.at[:, pl.ds(4 * u, 4)], in_sems.at[u]
            )
            for u in range(2)
        ]
    )
    lane = lanes_of(384)
    low = lane < 64

    def put(dst, column, full):
        full = full.reshape(768, 128).astype(BF16)
        if dst is l_scr:
            dst[:, column : column + 128] = full
        else:
            for q in range(8):
                dst[64 * q : 64 * q + 64, column : column + 128] = full[96 * q : 96 * q + 64]
                dst[512 + 32 * q : 544 + 32 * q, column : column + 128] = full[96 * q + 64 : 96 * q + 96]

    def stack(halves):
        return jnp.concatenate([h.reshape(16, 24, 128) for h in halves], axis=1)

    def part(value, start):
        return value[:, start : start + 24].reshape(384, 128)

    for u in range(2):
        copies[u].wait()
        blocks = [in_ref[:, 4 * u + v].astype(F32) for v in range(4)]
        for p in range(2):
            for dst, start in ((l_scr, 0), (r_scr, 24)):
                halves = unpack_wide(part(blocks[2 * p], start), part(blocks[2 * p + 1], start), low)
                put(dst, (2 * u + p) * 128, stack(halves))
        thin = [part(b, 48) for b in blocks]
        for dst, base in ((l_scr, 0), (r_scr, 2)):
            halves = []
            for a in range(2):
                parts = [roll(thin[v], 32 * (v - base - a)) for v in range(4)]
                lower = jnp.where(lane < 32, parts[0], parts[1])
                upper = jnp.where(lane < 96, parts[2], parts[3])
                halves.append(jnp.where(low, lower, upper))
            put(dst, 512 + u * 128, stack(halves))
    out_copies = []
    for b in range(4):
        product = dot_nt(l_scr[192 * b : 192 * b + 192, :], r_scr[...])
        pack_rows(product, out_ref, 4 * b, 4)
        copy = pltpu.make_async_copy(
            out_ref.at[pl.ds(4 * b, 4)], out_hbm.at[pl.ds(4 * b, 4)], out_sems.at[b]
        )
        copy.start()
        out_copies.append(copy)
    wait_all(out_copies)


def pack_rows(full, out_ref, first, count):
    low = lanes_of(count * 24) < 64
    lane = lanes_of(count * 16)
    for q in range(8):
        tile = full[:, 128 * (q // 2) : 128 * (q // 2) + 128].reshape(count, 48, 128)
        top = tile[:, 0:24].reshape(count * 24, 128)
        bottom = tile[:, 24:48].reshape(count * 24, 128)
        if q % 2 == 0:
            wide = jnp.where(low, top, roll(bottom, 64))
        else:
            wide = jnp.where(low, roll(top, 64), bottom)
        tile = full[:, 512 + 128 * (q // 4) : 640 + 128 * (q // 4)].reshape(count, 48, 128)
        thin = [
            roll(tile[:, 16 * m : 16 * m + 16].reshape(count * 16, 128), 32 * (m - q % 4))
            for m in range(3)
        ]
        thin = jnp.where(lane < 32, thin[0], jnp.where(lane < 64, thin[1], thin[2]))
        piece = jnp.concatenate(
            [wide.reshape(count, 24, 128), thin.reshape(count, 16, 128)], axis=1
        )
        out_ref[pl.ds(first, count), q] = piece.astype(BF16)


def transition_kernel(
    mixed_hbm, ring_hbm, far_hbm, place_ref, token_hbm, gain_ref, gate_hbm, up_hbm, down_hbm, out_hbm,
    mixed_ref, wo_ref, token_ref, gate_ref, up_ref, down_ref, x_ref, out_ref, sems, wo_sems, out_sems,
):
    pairs = ((mixed_hbm, mixed_ref), (token_hbm, token_ref), (gate_hbm, gate_ref), (up_hbm, up_ref), (down_hbm, down_ref))
    wo_copies = []
    for far, src in ((0, ring_hbm), (1, far_hbm)):
        for n in range(8):
            core = lax.rem(place_ref[2] + far, 2)
            high = lax.rem(place_ref[4] + n // 4, 2)
            block = core * 8 + high * 4 + lax.rem(place_ref[5] + n, 4)
            wo_copies.append(
                pltpu.make_async_copy(src.at[n], wo_ref.at[block, pl.ds(0, 48)], wo_sems.at[8 * far + n])
            )
    start_all(wo_copies)
    copies = start_all([pltpu.make_async_copy(src, dst, sems.at[n]) for n, (src, dst) in enumerate(pairs)])
    wo_ref[:, 48:64, :] = jnp.zeros((16, 16, 768), BF16)
    copies[0].wait()
    low = lanes_of(144) < 64
    for n in range(8):
        first = mixed_ref[2 * n].reshape(144, 128).astype(F32)
        second = mixed_ref[2 * n + 1].reshape(144, 128).astype(F32)
        top, bottom = unpack_wide(first, second, low)
        x_ref[0:144, 128 * n : 128 * n + 128] = top.astype(BF16)
        x_ref[144:288, 128 * n : 128 * n + 128] = bottom.astype(BF16)
    wait_all(wo_copies)
    attn = matmul(x_ref[...], wo_ref[...].reshape(1024, 768))
    copies[1].wait()
    token = jnp.concatenate([token_ref[s, 48 * half : 48 * half + 48] for half in range(2) for s in range(3)], axis=0)
    state = token.astype(F32) + attn
    fed = layer_norm(state, gain_ref[...]).astype(BF16)
    wait_all(copies[2:])
    refined = state
    for n in range(3):
        cols = slice(512 * n, 512 * n + 512)
        hidden = jax.nn.silu(matmul(fed, gate_ref[:, cols])) * matmul(fed, up_ref[:, cols])
        refined = refined + matmul(hidden.astype(BF16), down_ref[cols, :])
    for half in range(2):
        for s in range(3):
            at = 144 * half + 48 * s
            out_ref[s, 48 * half : 48 * half + 48] = refined[at : at + 48]
    copy = pltpu.make_async_copy(out_ref, out_hbm, out_sems.at[0])
    copy.start()
    copy.wait()


def wide_places(i):
    return [(i, 0, 64), (i + 24, 0, 64)]


def thin_places(i):
    return [(i + 16 * m, 64, 32) for m in range(3)]


def update_kernel(
    t_hbm, pair_hbm, gate_hbm, w_ref, tri_gain_ref, bias_gain_ref, bp_ref, out_hbm, bias_hbm,
    scr, b_scr, t_ref, pair_ref, gate_ref, out_ref, bias_ref, t_sems, sems, out_sems,
):
    t_copies = start_all(
        [
            pltpu.make_async_copy(t_hbm.at[pl.ds(32 * n, 32)], t_ref.at[pl.ds(32 * n, 32)], t_sems.at[n])
            for n in range(4)
        ]
    )
    copies = start_all(
        [
            pltpu.make_async_copy(pair_hbm, pair_ref, sems.at[0]),
            pltpu.make_async_copy(gate_hbm, gate_ref, sems.at[1]),
        ]
    )
    for n in range(4):
        t_copies[n].wait()
        scr[1280 * n : 1280 * n + 1280, :] = t_ref[32 * n : 32 * n + 32].astype(F32).reshape(1280, 128)
    wait_all(copies)
    weight = w_ref[...]
    tri_gain = tri_gain_ref[...]
    bias_gain = bias_gain_ref[...]
    bias_proj = bp_ref[...]

    def group(positions, places):
        normed = []
        for position in positions:
            tri = scr[pl.ds(position, 128, stride=40), :]
            middle = tri - jnp.mean(tri, axis=0, keepdims=True)
            spread_of = jnp.mean(middle * middle, axis=0, keepdims=True)
            normed.append((middle * lax.rsqrt(spread_of + 1e-05) * tri_gain).astype(BF16))
        update = dot_tn(jnp.concatenate(normed, axis=1), weight)
        fed = []
        for n, spots in enumerate(places):
            at = 128 * n
            for row, start, size in spots:
                cols = pl.ds(start, size)
                new = pair_ref[row, cols, :].astype(F32) + gate_ref[row, cols, :] * update[at : at + size]
                out_ref[row, cols, :] = new
                fed.append(layer_norm(new, bias_gain).astype(BF16))
                at += size
            if len(spots) == 3:
                fed.append(fed[-1])
        bias = dot_nt(bias_proj, jnp.concatenate(fed, axis=0))
        for n, position in enumerate(positions):
            b_scr[pl.ds(position, 16, stride=40), :] = bias[:, 128 * n : 128 * n + 128]

    par, par2 = UPDATE_PAR, THIN_PAR

    def wide(i, carry):
        group([par * i + n for n in range(par)], [wide_places(par * i + n) for n in range(par)])
        return carry

    def thin(i, carry):
        group([24 + par2 * i + n for n in range(par2)], [thin_places(par2 * i + n) for n in range(par2)])
        return carry

    lax.fori_loop(0, 24 // par, wide, 0)
    out_copies = [
        pltpu.make_async_copy(out_ref.at[:, pl.ds(c, n)], out_hbm.at[:, pl.ds(c, n)], out_sems.at[8 + k])
        for k, (c, n) in enumerate(((0, 64), (64, 32)))
    ]
    out_copies[0].start()
    lax.fori_loop(0, 16 // par2, thin, 0)
    out_copies[1].start()
    bias_ref[...] = b_scr[...].reshape(16, 40, 128).astype(BF16)
    out_copies += start_all(
        [pltpu.make_async_copy(bias_ref, bias_hbm.at[n], out_sems.at[n]) for n in range(8)]
    )
    wait_all(out_copies)


def unpack_bias(bias_ref, copies, put):
    low = lanes_of(384) < 64
    lane = lanes_of(256)
    for u in range(2):
        copies[u].wait()
        blocks = [bias_ref[:, 4 * u + v].astype(F32) for v in range(4)]
        for p in range(2):
            halves = unpack_wide(
                blocks[2 * p][:, 0:24].reshape(384, 128),
                blocks[2 * p + 1][:, 0:24].reshape(384, 128),
                low,
            )
            put((2 * u + p) * 128, jnp.concatenate([h.reshape(16, 24, 128) for h in halves], axis=1))
        thin = [b[:, 24:40].reshape(256, 128) for b in blocks]
        thirds = []
        for m in range(3):
            parts = [roll(thin[v], 32 * (v - m)) for v in range(4)]
            lower = jnp.where(lane < 32, parts[0], parts[1])
            upper = jnp.where(lane < 96, parts[2], parts[3])
            thirds.append(jnp.where(lane < 64, lower, upper).reshape(16, 16, 128))
        put(512 + u * 128, jnp.concatenate(thirds, axis=1))


def pair_copies(keep_hbm, recv_hbm, pairs, sems):
    return start_all(
        [
            pltpu.make_async_copy(src, pairs.at[pl.ds(3 * n, 3)], sems.at[n])
            for n, src in enumerate((keep_hbm, recv_hbm))
        ]
    )


def forward_kernel(
    bias_hbm, keep_hbm, recv_hbm, chain_row_ref, chain_col_ref, place_ref, weight_ref,
    mixed_hbm, full_hbm, pairs, bias_ref, mixed_ref, full_ref, sems, in_sems, out_sems,
):
    bias_copies = start_all(
        [
            pltpu.make_async_copy(
                bias_hbm.at[:, pl.ds(4 * u, 4)], bias_ref.at[:, pl.ds(4 * u, 4)], in_sems.at[u]
            )
            for u in range(2)
        ]
    )
    copies = pair_copies(keep_hbm, recv_hbm, pairs, sems)
    core = place_ref[2]
    head_weight = weight_ref[place_ref[3]] * LOG2E

    def put(column, full):
        same = chain_row_ref[...] == chain_col_ref[:, column : column + 128]
        full_ref[:, column : column + 128] = full.reshape(768, 128) * LOG2E + jnp.where(
            same, head_weight, 0.0
        )

    unpack_bias(bias_ref, bias_copies, put)
    stats = slice(768, 896)
    full_copy = pltpu.make_async_copy(full_ref.at[:, 0:768], full_hbm.at[:, 0:768], out_sems.at[0])
    full_copy.start()
    full_ref[:, stats] = jnp.zeros((768, 128), F32)
    wait_all(copies)
    low_all = lanes_of(768) < 64
    lane = lanes_of(FORWARD_ROWS)
    low = lane < 64
    thin_low = lanes_of(48) < 64
    blocks = 768 // FORWARD_ROWS
    shares = FORWARD_ROWS // 96

    def block(s, b, owner, slot):
        both = pairs[s, 1]
        keys = jnp.where(low_all, both, jnp.zeros_like(both))
        rows = pl.ds(pl.multiple_of(b * FORWARD_ROWS, 32), FORWARD_ROWS)
        asked = pairs[s, 0, rows, :]
        weights = jnp.exp2(dot_nt(asked, keys) * SCALE + full_ref[rows, 0:768])
        inverse = 1.0 / jnp.sum(weights, axis=-1, keepdims=True)
        mixed = matmul((weights * inverse).astype(BF16), both)
        center = jnp.sum(jnp.where(low, 0.0, asked.astype(F32) * mixed), axis=-1, keepdims=True)
        full_ref[rows, stats] = jnp.where(
            lane == s, inverse, jnp.where(lane == s + 64, center, full_ref[rows, stats])
        )
        for n in range(shares):
            mixed_ref[owner * 8 + b * shares + n, slot] = jnp.where(
                thin_low, roll(mixed[96 * n : 96 * n + 48], 64), mixed[96 * n + 48 : 96 * n + 96]
            ).astype(BF16)

    def step(i, carry):
        half = i // blocks
        owner = jnp.where(half == 0, core, 1 - core)
        for n in range(3):
            block(3 * half + n, i % blocks, owner, n)
        return carry

    def mixed_copy(owner, sem):
        part = pl.ds(owner * 8, 8)
        return pltpu.make_async_copy(mixed_ref.at[part], mixed_hbm.at[part], out_sems.at[sem])

    lax.fori_loop(0, blocks, step, 0)
    mixed_copy(core, 1).start()
    lax.fori_loop(blocks, 2 * blocks, step, 0)
    mixed_copy(1 - core, 2).start()
    stats_copy = pltpu.make_async_copy(full_ref.at[:, stats], full_hbm.at[:, stats], out_sems.at[3])
    stats_copy.start()
    mixed_copy(core, 1).wait()
    mixed_copy(1 - core, 2).wait()
    full_copy.wait()
    stats_copy.wait()


def backward_kernel(full_hbm, keep_hbm, recv_hbm, grad_hbm, pairs, full_ref, grad_ref, sems, in_sems, out_sems):
    copies = pair_copies(keep_hbm, recv_hbm, pairs, sems)
    blocks = 768 // BACKWARD_ROWS

    def full_copy(b):
        rows = pl.ds(pl.multiple_of(b * BACKWARD_ROWS, 32), BACKWARD_ROWS)
        return pltpu.make_async_copy(full_hbm.at[rows], full_ref.at[rows], in_sems.at[b])

    start_all([full_copy(b) for b in range(blocks)])
    wait_all(copies)
    low_all = lanes_of(768) < 64

    def row_block(b, carry):
        full_copy(b).wait()
        rows = pl.ds(pl.multiple_of(b * BACKWARD_ROWS, 32), BACKWARD_ROWS)
        total = None
        for s in range(6):
            both = pairs[s, 1]
            keys = jnp.where(low_all, both, jnp.zeros_like(both))
            values = jnp.where(low_all, jnp.zeros_like(both), both)
            asked = pairs[s, 0, rows, :]
            inverse = full_ref[rows, 768 + s : 769 + s]
            center = full_ref[rows, 832 + s : 833 + s]
            probs = jnp.exp2(dot_nt(asked, keys) * SCALE + full_ref[rows, 0:768]) * inverse
            score_grad = probs * (dot_nt(asked, values) - center)
            total = score_grad if total is None else total + score_grad
        pack_rows(total, grad_ref, b * (BACKWARD_ROWS // 48), BACKWARD_ROWS // 48)
        grad_copy(b).start()
        return carry

    def grad_copy(b):
        part = pl.ds(b * (BACKWARD_ROWS // 48), BACKWARD_ROWS // 48)
        return pltpu.make_async_copy(grad_ref.at[part], grad_hbm.at[part], out_sems.at[b])

    lax.fori_loop(0, blocks, row_block, 0)
    wait_all([grad_copy(b) for b in range(blocks)])


def pair_grad_kernel(in_hbm, w_ref, out_hbm, scr, in_ref, out_ref, in_sems, out_sems):
    copies = start_all([pltpu.make_async_copy(in_hbm.at[n], in_ref.at[n], in_sems.at[n]) for n in range(8)])
    total = None
    for n in range(8):
        copies[n].wait()
        part = in_ref[n].astype(F32)
        total = part if total is None else total + part
    scr[...] = total.reshape(640, 128)
    weight = w_ref[...]

    def group(positions, places):
        grad = jnp.concatenate([scr[pl.ds(p, 16, stride=40), :] for p in positions], axis=1)
        high = grad.astype(BF16)
        rest = grad - high.astype(F32)
        middle = rest.astype(BF16)
        least = (rest - middle.astype(F32)).astype(BF16)
        rows = dot_tn(jnp.concatenate([high, middle, least], axis=0), weight)
        for n, spots in enumerate(places):
            at = 128 * n
            for row, start, size in spots:
                out_ref[row, pl.ds(start, size), :] = rows[at : at + size]
                at += size

    par, par2 = UPDATE_PAR, THIN_PAR

    def wide(i, carry):
        group([par * i + n for n in range(par)], [wide_places(par * i + n) for n in range(par)])
        return carry

    def thin(i, carry):
        group([24 + par2 * i + n for n in range(par2)], [thin_places(par2 * i + n) for n in range(par2)])
        return carry

    lax.fori_loop(0, 24 // par, wide, 0)
    out_copies = [
        pltpu.make_async_copy(out_ref.at[:, pl.ds(c, n)], out_hbm.at[:, pl.ds(c, n)], out_sems.at[k])
        for k, (c, n) in enumerate(((0, 64), (64, 32)))
    ]
    out_copies[0].start()
    lax.fori_loop(0, 16 // par2, thin, 0)
    out_copies[1].start()
    wait_all(out_copies)


def column_order(value, axis):
    shape = value.shape
    split = value.reshape(shape[:axis] + (8, 96) + shape[axis + 1 :])
    wide = lax.slice_in_dim(split, 0, 64, axis=axis + 1).reshape(shape[:axis] + (512,) + shape[axis + 1 :])
    thin = lax.slice_in_dim(split, 64, 96, axis=axis + 1).reshape(shape[:axis] + (256,) + shape[axis + 1 :])
    return jnp.concatenate([wide, thin], axis=axis)


def memory(space):
    return pl.BlockSpec(memory_space=space)


VMEM, SMEM, HBM = memory(pltpu.VMEM), memory(pltpu.SMEM), memory(pltpu.HBM)
TILE = (48, 96, 128)
PACKED = (16, 8, 40, 128)


def shape(dims, dtype=BF16):
    return jax.ShapeDtypeStruct(dims, dtype)


def dma(count):
    return pltpu.SemaphoreType.DMA((count,))


def run_project(*args):
    return call(
        project_kernel,
        (shape((128, 72, 128)), shape((4608, 128))),
        args,
        [
            pltpu.VMEM((128 * 72, 128), F32),
            pltpu.VMEM((4608, 128), BF16),
            pltpu.VMEM((4608, 128), BF16),
            pltpu.VMEM((4, 128, 128), BF16),
            pltpu.VMEM((128, 72, 128), BF16),
            pltpu.SMEM((768,), jnp.int32),
            dma(9),
            dma(5),
            dma(17),
        ],
        "project",
        flops=2 * 512 * 128 * 6144,
        nbytes=5_000_000,
        spaces=[HBM, VMEM] + [HBM] * 5,
        out_specs=(HBM, HBM),
    )


def run_tokens(samples, *args):
    part = shape((samples, 2, 768, 128))
    token_block = pl.BlockSpec((1, 768, 768), lambda s: (s, 0, 0))
    part_block = pl.BlockSpec((1, 2, 768, 128), lambda s: (s, 0, 0, 0))
    return call(
        token_kernel,
        (part, part),
        args,
        [pltpu.VMEM((768, 384), BF16), pltpu.VMEM((128, 768), BF16), pltpu.VMEM((768, 768), BF16)],
        "tokens",
        flops=2 * 2304 * 768 * 512,
        nbytes=12_000_000,
        spaces=[token_block, token_block] + [VMEM] * 5 + [SMEM],
        grid=(samples,),
        out_specs=(part_block, part_block),
    )


def run_product(*args):
    return call(
        product_kernel,
        shape(PACKED),
        args,
        [
            pltpu.VMEM((16, 8, 72, 128), BF16),
            pltpu.VMEM(PACKED, BF16),
            pltpu.VMEM((768, 768), BF16),
            pltpu.VMEM((768, 768), BF16),
            dma(2),
            dma(4),
        ],
        "product",
        flops=2 * 768**3,
        nbytes=4_000_000,
        spaces=[HBM],
        out_specs=HBM,
        mib=50.5,
    )


def run_update(*args):
    return call(
        update_kernel,
        (shape(TILE, F32), shape((8, 16, 40, 128))),
        args,
        [
            pltpu.VMEM((128 * 40, 128), F32),
            pltpu.VMEM((16 * 40, 128), F32),
            pltpu.VMEM((128, 40, 128), BF16),
            pltpu.VMEM(TILE, BF16),
            pltpu.VMEM(TILE, F32),
            pltpu.VMEM(TILE, F32),
            pltpu.VMEM((16, 40, 128), BF16),
            dma(4),
            dma(2),
            dma(10),
        ],
        "update",
        flops=2 * 128 * 128 * 5120,
        nbytes=9_000_000,
        spaces=[HBM, HBM, HBM] + [VMEM] * 4,
        out_specs=(HBM, HBM),
        mib=52,
    )


def run_forward(*args):
    return call(
        forward_kernel,
        (shape((16, 3, 48, 128)), shape((768, 896), F32)),
        args,
        [
            pltpu.VMEM((6, 2, 768, 128), BF16),
            pltpu.VMEM(PACKED, BF16),
            pltpu.VMEM((16, 3, 48, 128), BF16),
            pltpu.VMEM((768, 896), F32),
            dma(2),
            dma(2),
            dma(4),
        ],
        "forward",
        flops=6 * 4 * 768 * 768 * 128,
        nbytes=12_000_000,
        spaces=[HBM, HBM, HBM, VMEM, VMEM, SMEM, SMEM],
        out_specs=(HBM, HBM),
        mib=51,
    )


def run_backward(*args):
    return call(
        backward_kernel,
        shape(PACKED),
        args,
        [
            pltpu.VMEM((6, 2, 768, 128), BF16),
            pltpu.VMEM((768, 896), F32),
            pltpu.VMEM(PACKED, BF16),
            dma(2),
            dma(768 // BACKWARD_ROWS),
            dma(768 // BACKWARD_ROWS),
        ],
        "backward",
        flops=6 * 4 * 768 * 768 * 128,
        nbytes=12_000_000,
        spaces=[HBM] * 3,
        out_specs=HBM,
    )


def run_pair_grad(*args):
    return call(
        pair_grad_kernel,
        shape(TILE, F32),
        args,
        [
            pltpu.VMEM((16 * 40, 128), F32),
            pltpu.VMEM((8, 16, 40, 128), BF16),
            pltpu.VMEM(TILE, F32),
            dma(8),
            dma(2),
        ],
        "pair_grad",
        flops=2 * 48 * 128 * 5120,
        nbytes=4_000_000,
        spaces=[HBM, VMEM],
        out_specs=HBM,
        mib=52,
    )


def run_transition(*args):
    return call(
        transition_kernel,
        shape((3, 96, 768), F32),
        args,
        [
            pltpu.VMEM((16, 3, 48, 128), BF16),
            pltpu.VMEM((16, 64, 768), BF16),
            pltpu.VMEM((3, 96, 768), BF16),
            pltpu.VMEM((768, 1536), BF16),
            pltpu.VMEM((768, 1536), BF16),
            pltpu.VMEM((1536, 768), BF16),
            pltpu.VMEM((288, 1024), BF16),
            pltpu.VMEM((3, 96, 768), F32),
            dma(5),
            dma(16),
            dma(1),
        ],
        "transition",
        flops=2 * 288 * 768 * (1024 + 3 * 1536),
        nbytes=12_000_000,
        spaces=[HBM] * 3 + [SMEM, HBM, VMEM] + [HBM] * 3,
        out_specs=HBM,
        mib=51,
    )


def exchange(value, axes):
    return lax.all_to_all(value, axes, 0, 0, tiled=True)


SWAP = [(0, 1), (1, 0)]


def gather_ring(half):
    ring = [half] + [lax.ppermute(half, "z", [(i, (i - k) % 4) for i in range(4)]) for k in range(1, 4)]
    return jnp.stack(ring)


def body(
    pair_state,
    pair_mask,
    chain_ids,
    tokens,
    grad_attn,
    norm_pair,
    proj_left,
    gate_left,
    proj_right,
    gate_right,
    gate_out,
    norm_tri,
    tri_out,
    norm_bias,
    bias_proj,
    chain_weight,
    norm_tokens,
    w_query,
    w_key,
    w_value,
    w_out,
    norm_ff,
    ff_gate,
    ff_up,
    ff_down,
):
    tile_rows, tile_cols, channels = pair_state.shape
    tile_size = tile_rows * tile_cols
    row_start = lax.axis_index(ROWS) * tile_rows
    col_index = lax.axis_index(COLS)
    col_start = col_index * tile_cols
    pair_flat = pair_state.reshape(tile_size, channels)

    core_index = lax.axis_index("core")
    place = jnp.stack(
        [row_start, col_start, core_index, 2 * col_index + core_index, lax.axis_index("xh"), lax.axis_index("z")]
    ).astype(jnp.int32)

    sides, normed = run_project(
        pair_flat, norm_pair, proj_left, proj_right, gate_left, gate_right, pair_mask
    )
    sides_in = exchange(sides, ALL)

    samples, seq_len, model_width = tokens.shape
    keep, send = run_tokens(
        samples, tokens, grad_attn, norm_tokens.astype(F32)[None], w_query, w_key, w_value, w_out, place[2:3]
    )
    keep, send, w_out_late = lax.optimization_barrier((keep, send, w_out))
    ring = gather_ring(lax.dynamic_slice_in_dim(w_out_late, core_index * HD, HD, 0))
    sides_in, keep, send, ring = lax.optimization_barrier((sides_in, keep, send, ring))
    recv = lax.ppermute(send, "core", SWAP)
    products = run_product(sides_in.reshape(16, 8, 72, 128))
    rings = jnp.concatenate([ring, lax.ppermute(ring, "xh", SWAP)], axis=0)
    products, rings = lax.optimization_barrier((products, rings))
    tri_in = exchange(products.reshape(128, 40, 128), ALL)
    share_len = seq_len // 8
    token_share = lax.dynamic_slice_in_dim(tokens, col_index * share_len, share_len, 1)
    gate = jax.nn.sigmoid(matmul(normed, gate_out)).reshape(pair_state.shape)
    heads_first = jnp.transpose(bias_proj.T.reshape(8, 2, 128), (1, 0, 2)).reshape(16, 128)
    tri_gain = jnp.broadcast_to(norm_tri.astype(F32)[:, None], (128, 128))
    bias_gain = norm_bias.astype(F32)[None]
    ff_gain = norm_ff.astype(F32)[None]
    triple = jnp.concatenate([heads_first] * 3, axis=0)
    chain_row, chain_col = chain_ids[:, None], column_order(chain_ids[None], 1)
    (
        tri_in, recv, token_share, gate, heads_first, tri_gain, bias_gain, ff_gain, triple, chain_row, chain_col
    ) = lax.optimization_barrier(
        (
            tri_in, recv, token_share, gate, heads_first, tri_gain, bias_gain, ff_gain, triple, chain_row, chain_col
        )
    )

    pair_out, bias = run_update(
        tri_in,
        pair_state,
        gate,
        tri_out,
        tri_gain,
        bias_gain,
        heads_first,
    )
    bias_in = exchange(bias.reshape(128, 40, 128), ALL).reshape(PACKED)

    bias_in, rings = lax.optimization_barrier((bias_in, rings))
    far_rings = lax.ppermute(rings, "core", SWAP)

    mixed, full_bias = run_forward(
        bias_in, keep, recv, chain_row, chain_col, place, chain_weight
    )
    mixed_in = exchange(mixed, ("core",) + COLS)
    bias_grad = run_backward(full_bias, keep, recv)
    grad_in = exchange(bias_grad.reshape(128, 40, 128), ALL).reshape(8, 16, 40, 128)

    refined = run_transition(
        mixed_in, rings, far_rings, place, token_share, ff_gain, ff_gate, ff_up, ff_down
    )

    pair_grad = run_pair_grad(grad_in, triple)
    return (pair_out, refined, pair_grad)


def solution(mesh):
    fine = Mesh(mesh.devices.reshape(2, 4, 2, 2, 4), ALL)
    pair = P(ROWS, COLS, None)
    sample_rows = P(ROWS, None, None)
    return jax.shard_map(
        body,
        mesh=fine,
        in_specs=(pair, P(), P(), sample_rows, sample_rows)
        + (P(),) * 12
        + (P(None, COLS),) * 3
        + (P(COLS, None),)
        + (P(),) * 4,
        out_specs=(pair, pair, pair),
        check_vma=False,
    )
```

```python
import functools
import jax
import jax.numpy as jnp
from jax import lax
from jax.experimental import pallas as pl
from jax.experimental.pallas import tpu as pltpu
from jax.sharding import Mesh, PartitionSpec as P

HD = 48
F32 = jnp.float32
BF16 = jnp.bfloat16
ROWS = ("grp", "y", "core")
COLS = ("xh", "z")
ALL = ROWS + COLS
LOG2E = 1.4426950408889634
SCALE = HD ** (-0.5) * LOG2E
FORWARD_ROWS = 768
UPDATE_PAR = 12
THIN_PAR = 16
BACKWARD_ROWS = 384


def layer_norm(value_rows, gain_vec):
    middle = value_rows - jnp.mean(value_rows, axis=-1, keepdims=True)
    spread = jnp.mean(middle * middle, axis=-1, keepdims=True)
    return middle * lax.rsqrt(spread + 1e-05) * gain_vec.astype(F32)


def matmul(left_side, right_side):
    return jnp.dot(left_side, right_side, preferred_element_type=F32)


def dot_nt(a, b):
    return lax.dot_general(a, b, (((1,), (1,)), ((), ())), preferred_element_type=F32)


def dot_tn(a, b):
    return lax.dot_general(a, b, (((0,), (0,)), ((), ())), preferred_element_type=F32)


def lanes_of(rows):
    return lax.broadcasted_iota(jnp.int32, (rows, 128), 1)


def roll(value, shift):
    shift = shift % 128
    return value if shift == 0 else pltpu.roll(value, shift, 1)


def call(kernel, outs, args, scratch, name, flops=0, nbytes=0, spaces=None, grid=None, out_specs=None, mib=60):
    vmem = pl.BlockSpec(memory_space=pltpu.VMEM)
    return pl.pallas_call(
        kernel,
        out_shape=outs,
        in_specs=spaces or [vmem] * len(args),
        out_specs=out_specs or jax.tree.map(lambda _: vmem, outs),
        scratch_shapes=scratch,
        compiler_params=pltpu.CompilerParams(vmem_limit_bytes=int(mib * 1024 * 1024)),
        cost_estimate=pl.CostEstimate(flops=flops, bytes_accessed=nbytes, transcendentals=0),
        name=name,
        **({} if grid is None else {"grid": grid}),
    )(*args)


def start_all(copies):
    for copy in copies:
        copy.start()
    return copies


def wait_all(copies):
    for copy in copies:
        copy.wait()


def project_kernel(
    pair_hbm, gain_ref, pl_hbm, pr_hbm, gl_hbm, gr_hbm, mask_hbm, out_hbm, normed_hbm,
    scr, pair_ref, normed_ref, w_ref, out_ref, mask_ref, pair_sems, w_sems, out_sems,
):
    blocks = [pl.ds(2304 * (n % 2) + 576 * (n // 2), 576) for n in range(8)]
    pair_copies = start_all(
        [pltpu.make_async_copy(pair_hbm.at[b], pair_ref.at[b], pair_sems.at[n]) for n, b in enumerate(blocks)]
    )
    w_copies = start_all(
        [
            pltpu.make_async_copy(src, w_ref.at[n], w_sems.at[n])
            for n, src in enumerate((pl_hbm, pr_hbm, gl_hbm, gr_hbm))
        ]
        + [pltpu.make_async_copy(mask_hbm, mask_ref, w_sems.at[4])]
    )
    gain = gain_ref[...].astype(F32).reshape(1, 128)
    normed_copies = []

    def norm_block(n):
        block = blocks[n]
        pair_copies[n].wait()
        normed_ref[block, :] = layer_norm(pair_ref[block, :].astype(F32), gain).astype(BF16)
        copy = pltpu.make_async_copy(normed_ref.at[block], normed_hbm.at[block], out_sems.at[n])
        copy.start()
        normed_copies.append(copy)

    norm_block(0)
    norm_block(1)
    wait_all(w_copies)
    lane = lanes_of(1)
    row_start = lax.axis_index(ROWS) * 48
    col_start = lax.axis_index(COLS) * 96
    wide_cols = jnp.zeros((1, 128), F32)
    thin_cols = jnp.zeros((1, 128), F32)
    for k in range(64):
        wide_cols = jnp.where(lane % 64 == k, mask_ref[col_start + k].astype(F32), wide_cols)
    for k in range(32):
        thin_cols = jnp.where(lane % 32 == k, mask_ref[col_start + 64 + k].astype(F32), thin_cols)
    low = lanes_of(128) < 64
    weights = jnp.concatenate([w_ref[n].astype(F32).T.astype(BF16) for n in range(4)], axis=0)

    def rows_at(i, start, size):
        return normed_ref[pl.ds(pl.multiple_of(i * 96 + start, 32), size), :]

    def one(i):
        wide = [rows_at(i, 0, 64), rows_at(i + 24, 0, 64)]
        thin = [rows_at(i, 64, 32), rows_at(i + 24, 64, 32)]
        y = dot_nt(weights, jnp.concatenate(wide + thin + thin, axis=0))
        first = mask_ref[row_start + i].astype(F32)
        second = mask_ref[row_start + i + 24].astype(F32)
        wide_mask = jnp.where(lane < 64, first, second) * wide_cols
        thin_mask = jnp.where(lane % 64 < 32, first, second) * thin_cols
        left = y[0:128, 0:128] * jax.nn.sigmoid(y[256:384, 0:128])
        right = y[128:256, 0:128] * jax.nn.sigmoid(y[384:512, 0:128])
        both_p = jnp.where(low, y[0:128, 128:256], y[128:256, 128:256])
        both_g = jnp.where(low, y[256:384, 128:256], y[384:512, 128:256])
        scr[pl.ds(i, 128, stride=72), :] = left * wide_mask
        scr[pl.ds(i + 24, 128, stride=72), :] = right * wide_mask
        scr[pl.ds(i + 48, 128, stride=72), :] = both_p * jax.nn.sigmoid(both_g) * thin_mask

    for m in range(4):
        if m < 3:
            norm_block(2 * m + 2)
            norm_block(2 * m + 3)
        for k in range(6):
            one(6 * m + k)
    out_copies = []
    for n in range(8):
        part = scr[1152 * n : 1152 * n + 1152, :].reshape(16, 72, 128)
        out_ref[16 * n : 16 * n + 16] = part.astype(BF16)
        copy = pltpu.make_async_copy(
            out_ref.at[pl.ds(16 * n, 16)], out_hbm.at[pl.ds(16 * n, 16)], out_sems.at[9 + n]
        )
        copy.start()
        out_copies.append(copy)
    wait_all(normed_copies + out_copies)


def token_kernel(
    tokens_ref, grad_ref, gain_ref, wq_ref, wk_ref, wv_ref, wo_ref, core_ref, keep_ref, send_ref, w_scr, wo_scr, norm_scr
):
    even = core_ref[0] == 0

    @pl.when(pl.program_id(0) == 0)
    def _():
        gap = jnp.zeros((768, 16), F32)
        for n, ref in enumerate((wq_ref, wk_ref, wv_ref)):
            w = ref[...].astype(F32)
            w = jnp.concatenate([w[:, 0:48], gap, w[:, 48:96], gap], axis=1)
            w_scr[:, 128 * n : 128 * n + 128] = jnp.where(even, w, roll(w, 64)).astype(BF16)
        first, second = wo_ref[0:48, :], wo_ref[48:96, :]
        wo_scr[0:48, :] = jnp.where(even, first, second)
        wo_scr[64:112, :] = jnp.where(even, second, first)
        wo_scr[48:64, :] = jnp.zeros((16, 768), BF16)
        wo_scr[112:128, :] = jnp.zeros((16, 768), BF16)

    gain = gain_ref[...]

    def norm_block(block, carry):
        rows = pl.ds(pl.multiple_of(block * 96, 32), 96)
        norm_scr[rows, :] = layer_norm(tokens_ref[0, rows, :].astype(F32), gain).astype(BF16)
        return carry

    lax.fori_loop(0, 8, norm_block, 0)
    low = lanes_of(768) < 64
    query = matmul(norm_scr[...], w_scr[:, 0:128])
    grads = dot_nt(grad_ref[0], wo_scr[...])
    keep_ref[0, 0] = jnp.where(low, query, roll(grads, 64)).astype(BF16)
    send_ref[0, 0] = jnp.where(low, roll(query, 64), grads).astype(BF16)
    key = matmul(norm_scr[...], w_scr[:, 128:256])
    value = matmul(norm_scr[...], w_scr[:, 256:384])
    for ref, full in (
        (keep_ref, jnp.where(low, key, roll(value, 64))),
        (send_ref, jnp.where(low, roll(key, 64), value)),
    ):
        full = full.astype(BF16)
        for q in range(8):
            ref[0, 1, 64 * q : 64 * q + 64] = full[96 * q : 96 * q + 64]
            ref[0, 1, 512 + 32 * q : 544 + 32 * q] = full[96 * q + 64 : 96 * q + 96]


def unpack_wide(first, second, low):
    top = jnp.where(low, first, roll(second, 64))
    bottom = jnp.where(low, roll(first, 64), second)
    return top, bottom


def product_kernel(in_hbm, out_hbm, in_ref, out_ref, l_scr, r_scr, in_sems, out_sems):
    copies = start_all(
        [
            pltpu.make_async_copy(
                in_hbm.at[:, pl.ds(4 * u, 4)], in_ref.at[:, pl.ds(4 * u, 4)], in_sems.at[u]
            )
            for u in range(2)
        ]
    )
    lane = lanes_of(384)
    low = lane < 64

    def put(dst, column, full):
        full = full.reshape(768, 128).astype(BF16)
        if dst is l_scr:
            dst[:, column : column + 128] = full
        else:
            for q in range(8):
                dst[64 * q : 64 * q + 64, column : column + 128] = full[96 * q : 96 * q + 64]
                dst[512 + 32 * q : 544 + 32 * q, column : column + 128] = full[96 * q + 64 : 96 * q + 96]

    def stack(halves):
        return jnp.concatenate([h.reshape(16, 24, 128) for h in halves], axis=1)

    def part(value, start):
        return value[:, start : start + 24].reshape(384, 128)

    for u in range(2):
        copies[u].wait()
        blocks = [in_ref[:, 4 * u + v].astype(F32) for v in range(4)]
        for p in range(2):
            for dst, start in ((l_scr, 0), (r_scr, 24)):
                halves = unpack_wide(part(blocks[2 * p], start), part(blocks[2 * p + 1], start), low)
                put(dst, (2 * u + p) * 128, stack(halves))
        thin = [part(b, 48) for b in blocks]
        for dst, base in ((l_scr, 0), (r_scr, 2)):
            halves = []
            for a in range(2):
                parts = [roll(thin[v], 32 * (v - base - a)) for v in range(4)]
                lower = jnp.where(lane < 32, parts[0], parts[1])
                upper = jnp.where(lane < 96, parts[2], parts[3])
                halves.append(jnp.where(low, lower, upper))
            put(dst, 512 + u * 128, stack(halves))
    out_copies = []
    for b in range(4):
        product = dot_nt(l_scr[192 * b : 192 * b + 192, :], r_scr[...])
        pack_rows(product, out_ref, 4 * b, 4)
        copy = pltpu.make_async_copy(
            out_ref.at[pl.ds(4 * b, 4)], out_hbm.at[pl.ds(4 * b, 4)], out_sems.at[b]
        )
        copy.start()
        out_copies.append(copy)
    wait_all(out_copies)


def pack_rows(full, out_ref, first, count):
    low = lanes_of(count * 24) < 64
    lane = lanes_of(count * 16)
    for q in range(8):
        tile = full[:, 128 * (q // 2) : 128 * (q // 2) + 128].reshape(count, 48, 128)
        top = tile[:, 0:24].reshape(count * 24, 128)
        bottom = tile[:, 24:48].reshape(count * 24, 128)
        if q % 2 == 0:
            wide = jnp.where(low, top, roll(bottom, 64))
        else:
            wide = jnp.where(low, roll(top, 64), bottom)
        tile = full[:, 512 + 128 * (q // 4) : 640 + 128 * (q // 4)].reshape(count, 48, 128)
        thin = [
            roll(tile[:, 16 * m : 16 * m + 16].reshape(count * 16, 128), 32 * (m - q % 4))
            for m in range(3)
        ]
        thin = jnp.where(lane < 32, thin[0], jnp.where(lane < 64, thin[1], thin[2]))
        piece = jnp.concatenate(
            [wide.reshape(count, 24, 128), thin.reshape(count, 16, 128)], axis=1
        )
        out_ref[pl.ds(first, count), q] = piece.astype(BF16)


def transition_kernel(
    mixed_hbm, ring_hbm, far_hbm, place_ref, token_hbm, gain_ref, gate_hbm, up_hbm, down_hbm, out_hbm,
    mixed_ref, wo_ref, token_ref, gate_ref, up_ref, down_ref, x_ref, out_ref, sems, wo_sems, out_sems,
):
    pairs = ((mixed_hbm, mixed_ref), (token_hbm, token_ref), (gate_hbm, gate_ref), (up_hbm, up_ref), (down_hbm, down_ref))
    wo_copies = []
    for far, src in ((0, ring_hbm), (1, far_hbm)):
        for n in range(8):
            core = lax.rem(place_ref[2] + far, 2)
            high = lax.rem(place_ref[4] + n // 4, 2)
            block = core * 8 + high * 4 + lax.rem(place_ref[5] + n, 4)
            wo_copies.append(
                pltpu.make_async_copy(src.at[n], wo_ref.at[block, pl.ds(0, 48)], wo_sems.at[8 * far + n])
            )
    start_all(wo_copies)
    copies = start_all([pltpu.make_async_copy(src, dst, sems.at[n]) for n, (src, dst) in enumerate(pairs)])
    wo_ref[:, 48:64, :] = jnp.zeros((16, 16, 768), BF16)
    copies[0].wait()
    low = lanes_of(144) < 64
    for n in range(8):
        first = mixed_ref[2 * n].reshape(144, 128).astype(F32)
        second = mixed_ref[2 * n + 1].reshape(144, 128).astype(F32)
        top, bottom = unpack_wide(first, second, low)
        x_ref[0:144, 128 * n : 128 * n + 128] = top.astype(BF16)
        x_ref[144:288, 128 * n : 128 * n + 128] = bottom.astype(BF16)
    wait_all(wo_copies)
    attn = matmul(x_ref[...], wo_ref[...].reshape(1024, 768))
    copies[1].wait()
    token = jnp.concatenate([token_ref[s, 48 * half : 48 * half + 48] for half in range(2) for s in range(3)], axis=0)
    state = token.astype(F32) + attn
    fed = layer_norm(state, gain_ref[...]).astype(BF16)
    wait_all(copies[2:])
    refined = state
    for n in range(3):
        cols = slice(512 * n, 512 * n + 512)
        hidden = jax.nn.silu(matmul(fed, gate_ref[:, cols])) * matmul(fed, up_ref[:, cols])
        refined = refined + matmul(hidden.astype(BF16), down_ref[cols, :])
    for half in range(2):
        for s in range(3):
            at = 144 * half + 48 * s
            out_ref[s, 48 * half : 48 * half + 48] = refined[at : at + 48]
    copy = pltpu.make_async_copy(out_ref, out_hbm, out_sems.at[0])
    copy.start()
    copy.wait()


def wide_places(i):
    return [(i, 0, 64), (i + 24, 0, 64)]


def thin_places(i):
    return [(i + 16 * m, 64, 32) for m in range(3)]


def update_kernel(
    t_hbm, pair_hbm, gate_hbm, w_ref, tri_gain_ref, bias_gain_ref, bp_ref, out_hbm, bias_hbm,
    scr, b_scr, t_ref, pair_ref, gate_ref, out_ref, bias_ref, t_sems, sems, out_sems,
):
    t_copies = start_all(
        [
            pltpu.make_async_copy(t_hbm.at[pl.ds(32 * n, 32)], t_ref.at[pl.ds(32 * n, 32)], t_sems.at[n])
            for n in range(4)
        ]
    )
    copies = start_all(
        [
            pltpu.make_async_copy(pair_hbm, pair_ref, sems.at[0]),
            pltpu.make_async_copy(gate_hbm, gate_ref, sems.at[1]),
        ]
    )
    for n in range(4):
        t_copies[n].wait()
        scr[1280 * n : 1280 * n + 1280, :] = t_ref[32 * n : 32 * n + 32].astype(F32).reshape(1280, 128)
    wait_all(copies)
    weight = w_ref[...]
    tri_gain = tri_gain_ref[...]
    bias_gain = bias_gain_ref[...]
    bias_proj = bp_ref[...]

    def group(positions, places):
        normed = []
        for position in positions:
            tri = scr[pl.ds(position, 128, stride=40), :]
            middle = tri - jnp.mean(tri, axis=0, keepdims=True)
            spread_of = jnp.mean(middle * middle, axis=0, keepdims=True)
            normed.append((middle * lax.rsqrt(spread_of + 1e-05) * tri_gain).astype(BF16))
        update = dot_tn(jnp.concatenate(normed, axis=1), weight)
        fed = []
        for n, spots in enumerate(places):
            at = 128 * n
            for row, start, size in spots:
                cols = pl.ds(start, size)
                new = pair_ref[row, cols, :].astype(F32) + gate_ref[row, cols, :] * update[at : at + size]
                out_ref[row, cols, :] = new
                fed.append(layer_norm(new, bias_gain).astype(BF16))
                at += size
            if len(spots) == 3:
                fed.append(fed[-1])
        bias = dot_nt(bias_proj, jnp.concatenate(fed, axis=0))
        for n, position in enumerate(positions):
            b_scr[pl.ds(position, 16, stride=40), :] = bias[:, 128 * n : 128 * n + 128]

    par, par2 = UPDATE_PAR, THIN_PAR

    def wide(i, carry):
        group([par * i + n for n in range(par)], [wide_places(par * i + n) for n in range(par)])
        return carry

    def thin(i, carry):
        group([24 + par2 * i + n for n in range(par2)], [thin_places(par2 * i + n) for n in range(par2)])
        return carry

    lax.fori_loop(0, 24 // par, wide, 0)
    out_copies = [
        pltpu.make_async_copy(out_ref.at[:, pl.ds(c, n)], out_hbm.at[:, pl.ds(c, n)], out_sems.at[8 + k])
        for k, (c, n) in enumerate(((0, 64), (64, 32)))
    ]
    out_copies[0].start()
    lax.fori_loop(0, 16 // par2, thin, 0)
    out_copies[1].start()
    bias_ref[...] = b_scr[...].reshape(16, 40, 128).astype(BF16)
    out_copies += start_all(
        [pltpu.make_async_copy(bias_ref, bias_hbm.at[n], out_sems.at[n]) for n in range(8)]
    )
    wait_all(out_copies)


def unpack_bias(bias_ref, copies, put):
    low = lanes_of(384) < 64
    lane = lanes_of(256)
    for u in range(2):
        copies[u].wait()
        blocks = [bias_ref[:, 4 * u + v].astype(F32) for v in range(4)]
        for p in range(2):
            halves = unpack_wide(
                blocks[2 * p][:, 0:24].reshape(384, 128),
                blocks[2 * p + 1][:, 0:24].reshape(384, 128),
                low,
            )
            put((2 * u + p) * 128, jnp.concatenate([h.reshape(16, 24, 128) for h in halves], axis=1))
        thin = [b[:, 24:40].reshape(256, 128) for b in blocks]
        thirds = []
        for m in range(3):
            parts = [roll(thin[v], 32 * (v - m)) for v in range(4)]
            lower = jnp.where(lane < 32, parts[0], parts[1])
            upper = jnp.where(lane < 96, parts[2], parts[3])
            thirds.append(jnp.where(lane < 64, lower, upper).reshape(16, 16, 128))
        put(512 + u * 128, jnp.concatenate(thirds, axis=1))


def pair_copies(keep_hbm, recv_hbm, pairs, sems):
    return start_all(
        [
            pltpu.make_async_copy(src, pairs.at[pl.ds(3 * n, 3)], sems.at[n])
            for n, src in enumerate((keep_hbm, recv_hbm))
        ]
    )


def forward_kernel(
    bias_hbm, keep_hbm, recv_hbm, chain_row_ref, chain_col_ref, place_ref, weight_ref,
    mixed_hbm, full_hbm, pairs, bias_ref, mixed_ref, full_ref, sems, in_sems, out_sems,
):
    bias_copies = start_all(
        [
            pltpu.make_async_copy(
                bias_hbm.at[:, pl.ds(4 * u, 4)], bias_ref.at[:, pl.ds(4 * u, 4)], in_sems.at[u]
            )
            for u in range(2)
        ]
    )
    copies = pair_copies(keep_hbm, recv_hbm, pairs, sems)
    core = place_ref[2]
    head_weight = weight_ref[place_ref[3]] * LOG2E

    def put(column, full):
        same = chain_row_ref[...] == chain_col_ref[:, column : column + 128]
        full_ref[:, column : column + 128] = full.reshape(768, 128) * LOG2E + jnp.where(
            same, head_weight, 0.0
        )

    unpack_bias(bias_ref, bias_copies, put)
    stats = slice(768, 896)
    full_copy = pltpu.make_async_copy(full_ref.at[:, 0:768], full_hbm.at[:, 0:768], out_sems.at[0])
    full_copy.start()
    full_ref[:, stats] = jnp.zeros((768, 128), F32)
    wait_all(copies)
    low_all = lanes_of(768) < 64
    lane = lanes_of(FORWARD_ROWS)
    low = lane < 64
    thin_low = lanes_of(48) < 64
    blocks = 768 // FORWARD_ROWS
    shares = FORWARD_ROWS // 96

    def block(s, b, owner, slot):
        both = pairs[s, 1]
        keys = jnp.where(low_all, both, jnp.zeros_like(both))
        rows = pl.ds(pl.multiple_of(b * FORWARD_ROWS, 32), FORWARD_ROWS)
        asked = pairs[s, 0, rows, :]
        weights = jnp.exp2(dot_nt(asked, keys) * SCALE + full_ref[rows, 0:768])
        inverse = 1.0 / jnp.sum(weights, axis=-1, keepdims=True)
        mixed = matmul((weights * inverse).astype(BF16), both)
        center = jnp.sum(jnp.where(low, 0.0, asked.astype(F32) * mixed), axis=-1, keepdims=True)
        full_ref[rows, stats] = jnp.where(
            lane == s, inverse, jnp.where(lane == s + 64, center, full_ref[rows, stats])
        )
        for n in range(shares):
            mixed_ref[owner * 8 + b * shares + n, slot] = jnp.where(
                thin_low, roll(mixed[96 * n : 96 * n + 48], 64), mixed[96 * n + 48 : 96 * n + 96]
            ).astype(BF16)

    def step(i, carry):
        half = i // blocks
        owner = jnp.where(half == 0, core, 1 - core)
        for n in range(3):
            block(3 * half + n, i % blocks, owner, n)
        return carry

    def mixed_copy(owner, sem):
        part = pl.ds(owner * 8, 8)
        return pltpu.make_async_copy(mixed_ref.at[part], mixed_hbm.at[part], out_sems.at[sem])

    lax.fori_loop(0, blocks, step, 0)
    mixed_copy(core, 1).start()
    lax.fori_loop(blocks, 2 * blocks, step, 0)
    mixed_copy(1 - core, 2).start()
    stats_copy = pltpu.make_async_copy(full_ref.at[:, stats], full_hbm.at[:, stats], out_sems.at[3])
    stats_copy.start()
    mixed_copy(core, 1).wait()
    mixed_copy(1 - core, 2).wait()
    full_copy.wait()
    stats_copy.wait()


def backward_kernel(full_hbm, keep_hbm, recv_hbm, grad_hbm, pairs, full_ref, grad_ref, sems, in_sems, out_sems):
    copies = pair_copies(keep_hbm, recv_hbm, pairs, sems)
    blocks = 768 // BACKWARD_ROWS

    def full_copy(b):
        rows = pl.ds(pl.multiple_of(b * BACKWARD_ROWS, 32), BACKWARD_ROWS)
        return pltpu.make_async_copy(full_hbm.at[rows], full_ref.at[rows], in_sems.at[b])

    start_all([full_copy(b) for b in range(blocks)])
    wait_all(copies)
    low_all = lanes_of(768) < 64

    def row_block(b, carry):
        full_copy(b).wait()
        rows = pl.ds(pl.multiple_of(b * BACKWARD_ROWS, 32), BACKWARD_ROWS)
        total = None
        for s in range(6):
            both = pairs[s, 1]
            keys = jnp.where(low_all, both, jnp.zeros_like(both))
            values = jnp.where(low_all, jnp.zeros_like(both), both)
            asked = pairs[s, 0, rows, :]
            inverse = full_ref[rows, 768 + s : 769 + s]
            center = full_ref[rows, 832 + s : 833 + s]
            probs = jnp.exp2(dot_nt(asked, keys) * SCALE + full_ref[rows, 0:768]) * inverse
            score_grad = probs * (dot_nt(asked, values) - center)
            total = score_grad if total is None else total + score_grad
        pack_rows(total, grad_ref, b * (BACKWARD_ROWS // 48), BACKWARD_ROWS // 48)
        grad_copy(b).start()
        return carry

    def grad_copy(b):
        part = pl.ds(b * (BACKWARD_ROWS // 48), BACKWARD_ROWS // 48)
        return pltpu.make_async_copy(grad_ref.at[part], grad_hbm.at[part], out_sems.at[b])

    lax.fori_loop(0, blocks, row_block, 0)
    wait_all([grad_copy(b) for b in range(blocks)])


def pair_grad_kernel(in_hbm, w_ref, out_hbm, scr, in_ref, out_ref, in_sems, out_sems):
    copies = start_all([pltpu.make_async_copy(in_hbm.at[n], in_ref.at[n], in_sems.at[n]) for n in range(8)])
    total = None
    for n in range(8):
        copies[n].wait()
        part = in_ref[n].astype(F32)
        total = part if total is None else total + part
    scr[...] = total.reshape(640, 128)
    weight = w_ref[...]

    def group(positions, places):
        grad = jnp.concatenate([scr[pl.ds(p, 16, stride=40), :] for p in positions], axis=1)
        high = grad.astype(BF16)
        rest = grad - high.astype(F32)
        middle = rest.astype(BF16)
        least = (rest - middle.astype(F32)).astype(BF16)
        rows = dot_tn(jnp.concatenate([high, middle, least], axis=0), weight)
        for n, spots in enumerate(places):
            at = 128 * n
            for row, start, size in spots:
                out_ref[row, pl.ds(start, size), :] = rows[at : at + size]
                at += size

    par, par2 = UPDATE_PAR, THIN_PAR

    def wide(i, carry):
        group([par * i + n for n in range(par)], [wide_places(par * i + n) for n in range(par)])
        return carry

    def thin(i, carry):
        group([24 + par2 * i + n for n in range(par2)], [thin_places(par2 * i + n) for n in range(par2)])
        return carry

    lax.fori_loop(0, 24 // par, wide, 0)
    out_copies = [
        pltpu.make_async_copy(out_ref.at[:, pl.ds(c, n)], out_hbm.at[:, pl.ds(c, n)], out_sems.at[k])
        for k, (c, n) in enumerate(((0, 64), (64, 32)))
    ]
    out_copies[0].start()
    lax.fori_loop(0, 16 // par2, thin, 0)
    out_copies[1].start()
    wait_all(out_copies)


def column_order(value, axis):
    shape = value.shape
    split = value.reshape(shape[:axis] + (8, 96) + shape[axis + 1 :])
    wide = lax.slice_in_dim(split, 0, 64, axis=axis + 1).reshape(shape[:axis] + (512,) + shape[axis + 1 :])
    thin = lax.slice_in_dim(split, 64, 96, axis=axis + 1).reshape(shape[:axis] + (256,) + shape[axis + 1 :])
    return jnp.concatenate([wide, thin], axis=axis)


def memory(space):
    return pl.BlockSpec(memory_space=space)


VMEM, SMEM, HBM = memory(pltpu.VMEM), memory(pltpu.SMEM), memory(pltpu.HBM)
TILE = (48, 96, 128)
PACKED = (16, 8, 40, 128)


def shape(dims, dtype=BF16):
    return jax.ShapeDtypeStruct(dims, dtype)


def dma(count):
    return pltpu.SemaphoreType.DMA((count,))


def run_project(*args):
    return call(
        project_kernel,
        (shape((128, 72, 128)), shape((4608, 128))),
        args,
        [
            pltpu.VMEM((128 * 72, 128), F32),
            pltpu.VMEM((4608, 128), BF16),
            pltpu.VMEM((4608, 128), BF16),
            pltpu.VMEM((4, 128, 128), BF16),
            pltpu.VMEM((128, 72, 128), BF16),
            pltpu.SMEM((768,), jnp.int32),
            dma(9),
            dma(5),
            dma(17),
        ],
        "project",
        flops=2 * 512 * 128 * 6144,
        nbytes=5_000_000,
        spaces=[HBM, VMEM] + [HBM] * 5,
        out_specs=(HBM, HBM),
    )


def run_tokens(samples, *args):
    part = shape((samples, 2, 768, 128))
    token_block = pl.BlockSpec((1, 768, 768), lambda s: (s, 0, 0))
    part_block = pl.BlockSpec((1, 2, 768, 128), lambda s: (s, 0, 0, 0))
    return call(
        token_kernel,
        (part, part),
        args,
        [pltpu.VMEM((768, 384), BF16), pltpu.VMEM((128, 768), BF16), pltpu.VMEM((768, 768), BF16)],
        "tokens",
        flops=2 * 2304 * 768 * 512,
        nbytes=12_000_000,
        spaces=[token_block, token_block] + [VMEM] * 5 + [SMEM],
        grid=(samples,),
        out_specs=(part_block, part_block),
    )


def run_product(*args):
    return call(
        product_kernel,
        shape(PACKED),
        args,
        [
            pltpu.VMEM((16, 8, 72, 128), BF16),
            pltpu.VMEM(PACKED, BF16),
            pltpu.VMEM((768, 768), BF16),
            pltpu.VMEM((768, 768), BF16),
            dma(2),
            dma(4),
        ],
        "product",
        flops=2 * 768**3,
        nbytes=4_000_000,
        spaces=[HBM],
        out_specs=HBM,
        mib=50,
    )


def run_update(*args):
    return call(
        update_kernel,
        (shape(TILE, F32), shape((8, 16, 40, 128))),
        args,
        [
            pltpu.VMEM((128 * 40, 128), F32),
            pltpu.VMEM((16 * 40, 128), F32),
            pltpu.VMEM((128, 40, 128), BF16),
            pltpu.VMEM(TILE, BF16),
            pltpu.VMEM(TILE, F32),
            pltpu.VMEM(TILE, F32),
            pltpu.VMEM((16, 40, 128), BF16),
            dma(4),
            dma(2),
            dma(10),
        ],
        "update",
        flops=2 * 128 * 128 * 5120,
        nbytes=9_000_000,
        spaces=[HBM, HBM, HBM] + [VMEM] * 4,
        out_specs=(HBM, HBM),
        mib=52,
    )


def run_forward(*args):
    return call(
        forward_kernel,
        (shape((16, 3, 48, 128)), shape((768, 896), F32)),
        args,
        [
            pltpu.VMEM((6, 2, 768, 128), BF16),
            pltpu.VMEM(PACKED, BF16),
            pltpu.VMEM((16, 3, 48, 128), BF16),
            pltpu.VMEM((768, 896), F32),
            dma(2),
            dma(2),
            dma(4),
        ],
        "forward",
        flops=6 * 4 * 768 * 768 * 128,
        nbytes=12_000_000,
        spaces=[HBM, HBM, HBM, VMEM, VMEM, SMEM, SMEM],
        out_specs=(HBM, HBM),
        mib=51,
    )


def run_backward(*args):
    return call(
        backward_kernel,
        shape(PACKED),
        args,
        [
            pltpu.VMEM((6, 2, 768, 128), BF16),
            pltpu.VMEM((768, 896), F32),
            pltpu.VMEM(PACKED, BF16),
            dma(2),
            dma(768 // BACKWARD_ROWS),
            dma(768 // BACKWARD_ROWS),
        ],
        "backward",
        flops=6 * 4 * 768 * 768 * 128,
        nbytes=12_000_000,
        spaces=[HBM] * 3,
        out_specs=HBM,
    )


def run_pair_grad(*args):
    return call(
        pair_grad_kernel,
        shape(TILE, F32),
        args,
        [
            pltpu.VMEM((16 * 40, 128), F32),
            pltpu.VMEM((8, 16, 40, 128), BF16),
            pltpu.VMEM(TILE, F32),
            dma(8),
            dma(2),
        ],
        "pair_grad",
        flops=2 * 48 * 128 * 5120,
        nbytes=4_000_000,
        spaces=[HBM, VMEM],
        out_specs=HBM,
        mib=52,
    )


def run_transition(*args):
    return call(
        transition_kernel,
        shape((3, 96, 768), F32),
        args,
        [
            pltpu.VMEM((16, 3, 48, 128), BF16),
            pltpu.VMEM((16, 64, 768), BF16),
            pltpu.VMEM((3, 96, 768), BF16),
            pltpu.VMEM((768, 1536), BF16),
            pltpu.VMEM((768, 1536), BF16),
            pltpu.VMEM((1536, 768), BF16),
            pltpu.VMEM((288, 1024), BF16),
            pltpu.VMEM((3, 96, 768), F32),
            dma(5),
            dma(16),
            dma(1),
        ],
        "transition",
        flops=2 * 288 * 768 * (1024 + 3 * 1536),
        nbytes=12_000_000,
        spaces=[HBM] * 3 + [SMEM, HBM, VMEM] + [HBM] * 3,
        out_specs=HBM,
        mib=51,
    )


def exchange(value, axes):
    return lax.all_to_all(value, axes, 0, 0, tiled=True)


SWAP = [(0, 1), (1, 0)]


def gather_ring(half):
    ring = [half] + [lax.ppermute(half, "z", [(i, (i - k) % 4) for i in range(4)]) for k in range(1, 4)]
    return jnp.stack(ring)


def body(
    pair_state,
    pair_mask,
    chain_ids,
    tokens,
    grad_attn,
    norm_pair,
    proj_left,
    gate_left,
    proj_right,
    gate_right,
    gate_out,
    norm_tri,
    tri_out,
    norm_bias,
    bias_proj,
    chain_weight,
    norm_tokens,
    w_query,
    w_key,
    w_value,
    w_out,
    norm_ff,
    ff_gate,
    ff_up,
    ff_down,
):
    tile_rows, tile_cols, channels = pair_state.shape
    tile_size = tile_rows * tile_cols
    row_start = lax.axis_index(ROWS) * tile_rows
    col_index = lax.axis_index(COLS)
    col_start = col_index * tile_cols
    pair_flat = pair_state.reshape(tile_size, channels)

    core_index = lax.axis_index("core")
    place = jnp.stack(
        [row_start, col_start, core_index, 2 * col_index + core_index, lax.axis_index("xh"), lax.axis_index("z")]
    ).astype(jnp.int32)

    sides, normed = run_project(
        pair_flat, norm_pair, proj_left, proj_right, gate_left, gate_right, pair_mask
    )
    sides_in = exchange(sides, ALL)

    samples, seq_len, model_width = tokens.shape
    keep, send = run_tokens(
        samples, tokens, grad_attn, norm_tokens.astype(F32)[None], w_query, w_key, w_value, w_out, place[2:3]
    )
    keep, send, w_out_late = lax.optimization_barrier((keep, send, w_out))
    ring = gather_ring(lax.dynamic_slice_in_dim(w_out_late, core_index * HD, HD, 0))
    sides_in, keep, send, ring = lax.optimization_barrier((sides_in, keep, send, ring))
    recv = lax.ppermute(send, "core", SWAP)
    products = run_product(sides_in.reshape(16, 8, 72, 128))
    tri_in = exchange(products.reshape(128, 40, 128), ALL)
    share_len = seq_len // 8
    token_share = lax.dynamic_slice_in_dim(tokens, col_index * share_len, share_len, 1)
    gate = jax.nn.sigmoid(matmul(normed, gate_out)).reshape(pair_state.shape)
    heads_first = jnp.transpose(bias_proj.T.reshape(8, 2, 128), (1, 0, 2)).reshape(16, 128)
    tri_gain = jnp.broadcast_to(norm_tri.astype(F32)[:, None], (128, 128))
    bias_gain = norm_bias.astype(F32)[None]
    ff_gain = norm_ff.astype(F32)[None]
    triple = jnp.concatenate([heads_first] * 3, axis=0)
    chain_row, chain_col = chain_ids[:, None], column_order(chain_ids[None], 1)
    (
        tri_in, recv, token_share, gate, heads_first, tri_gain, bias_gain, ff_gain, triple, chain_row, chain_col
    ) = lax.optimization_barrier(
        (
            tri_in, recv, token_share, gate, heads_first, tri_gain, bias_gain, ff_gain, triple, chain_row, chain_col
        )
    )

    pair_out, bias = run_update(
        tri_in,
        pair_state,
        gate,
        tri_out,
        tri_gain,
        bias_gain,
        heads_first,
    )
    bias_in = exchange(bias.reshape(128, 40, 128), ALL).reshape(PACKED)

    bias_in, ring = lax.optimization_barrier((bias_in, ring))
    rings = jnp.concatenate([ring, lax.ppermute(ring, "xh", SWAP)], axis=0)

    mixed, full_bias = run_forward(
        bias_in, keep, recv, chain_row, chain_col, place, chain_weight
    )
    mixed, rings = lax.optimization_barrier((mixed, rings))
    far_rings = lax.ppermute(rings, "core", SWAP)
    mixed_in = exchange(mixed, ("core",) + COLS)
    bias_grad = run_backward(full_bias, keep, recv)
    grad_in = exchange(bias_grad.reshape(128, 40, 128), ALL).reshape(8, 16, 40, 128)

    refined = run_transition(
        mixed_in, rings, far_rings, place, token_share, ff_gain, ff_gate, ff_up, ff_down
    )

    pair_grad = run_pair_grad(grad_in, triple)
    return (pair_out, refined, pair_grad)


def solution(mesh):
    fine = Mesh(mesh.devices.reshape(2, 4, 2, 2, 4), ALL)
    pair = P(ROWS, COLS, None)
    sample_rows = P(ROWS, None, None)
    return jax.shard_map(
        body,
        mesh=fine,
        in_specs=(pair, P(), P(), sample_rows, sample_rows)
        + (P(),) * 12
        + (P(None, COLS),) * 3
        + (P(COLS, None),)
        + (P(),) * 4,
        out_specs=(pair, pair, pair),
        check_vma=False,
    )
```

```python
import functools
import jax
import jax.numpy as jnp
from jax import lax
from jax.experimental import pallas as pl
from jax.experimental.pallas import tpu as pltpu
from jax.sharding import Mesh, PartitionSpec as P

HD = 48
F32 = jnp.float32
BF16 = jnp.bfloat16
ROWS = ("grp", "y", "core")
COLS = ("xh", "z")
ALL = ROWS + COLS
LOG2E = 1.4426950408889634
SCALE = HD ** (-0.5) * LOG2E
FORWARD_ROWS = 768
UPDATE_PAR = 12
THIN_PAR = 16
BACKWARD_ROWS = 384


def layer_norm(value_rows, gain_vec):
    middle = value_rows - jnp.mean(value_rows, axis=-1, keepdims=True)
    spread = jnp.mean(middle * middle, axis=-1, keepdims=True)
    return middle * lax.rsqrt(spread + 1e-05) * gain_vec.astype(F32)


def matmul(left_side, right_side):
    return jnp.dot(left_side, right_side, preferred_element_type=F32)


def dot_nt(a, b):
    return lax.dot_general(a, b, (((1,), (1,)), ((), ())), preferred_element_type=F32)


def dot_tn(a, b):
    return lax.dot_general(a, b, (((0,), (0,)), ((), ())), preferred_element_type=F32)


def lanes_of(rows):
    return lax.broadcasted_iota(jnp.int32, (rows, 128), 1)


def roll(value, shift):
    shift = shift % 128
    return value if shift == 0 else pltpu.roll(value, shift, 1)


def call(kernel, outs, args, scratch, name, flops=0, nbytes=0, spaces=None, grid=None, out_specs=None, mib=60):
    vmem = pl.BlockSpec(memory_space=pltpu.VMEM)
    return pl.pallas_call(
        kernel,
        out_shape=outs,
        in_specs=spaces or [vmem] * len(args),
        out_specs=out_specs or jax.tree.map(lambda _: vmem, outs),
        scratch_shapes=scratch,
        compiler_params=pltpu.CompilerParams(vmem_limit_bytes=int(mib * 1024 * 1024)),
        cost_estimate=pl.CostEstimate(flops=flops, bytes_accessed=nbytes, transcendentals=0),
        name=name,
        **({} if grid is None else {"grid": grid}),
    )(*args)


def start_all(copies):
    for copy in copies:
        copy.start()
    return copies


def wait_all(copies):
    for copy in copies:
        copy.wait()


def project_kernel(
    pair_hbm, gain_ref, pl_hbm, pr_hbm, gl_hbm, gr_hbm, mask_hbm, out_hbm, normed_hbm,
    scr, pair_ref, normed_ref, w_ref, out_ref, mask_ref, pair_sems, w_sems, out_sems,
):
    blocks = [pl.ds(2304 * (n % 2) + 576 * (n // 2), 576) for n in range(8)]
    pair_copies = start_all(
        [pltpu.make_async_copy(pair_hbm.at[b], pair_ref.at[b], pair_sems.at[n]) for n, b in enumerate(blocks)]
    )
    w_copies = start_all(
        [
            pltpu.make_async_copy(src, w_ref.at[n], w_sems.at[n])
            for n, src in enumerate((pl_hbm, pr_hbm, gl_hbm, gr_hbm))
        ]
        + [pltpu.make_async_copy(mask_hbm, mask_ref, w_sems.at[4])]
    )
    gain = gain_ref[...].astype(F32).reshape(1, 128)
    normed_copies = []

    def norm_block(n):
        block = blocks[n]
        pair_copies[n].wait()
        normed_ref[block, :] = layer_norm(pair_ref[block, :].astype(F32), gain).astype(BF16)
        copy = pltpu.make_async_copy(normed_ref.at[block], normed_hbm.at[block], out_sems.at[n])
        copy.start()
        normed_copies.append(copy)

    norm_block(0)
    norm_block(1)
    wait_all(w_copies)
    lane = lanes_of(1)
    row_start = lax.axis_index(ROWS) * 48
    col_start = lax.axis_index(COLS) * 96
    wide_cols = jnp.zeros((1, 128), F32)
    thin_cols = jnp.zeros((1, 128), F32)
    for k in range(64):
        wide_cols = jnp.where(lane % 64 == k, mask_ref[col_start + k].astype(F32), wide_cols)
    for k in range(32):
        thin_cols = jnp.where(lane % 32 == k, mask_ref[col_start + 64 + k].astype(F32), thin_cols)
    low = lanes_of(128) < 64
    weights = jnp.concatenate([w_ref[n].astype(F32).T.astype(BF16) for n in range(4)], axis=0)

    def rows_at(i, start, size):
        return normed_ref[pl.ds(pl.multiple_of(i * 96 + start, 32), size), :]

    def one(i):
        wide = [rows_at(i, 0, 64), rows_at(i + 24, 0, 64)]
        thin = [rows_at(i, 64, 32), rows_at(i + 24, 64, 32)]
        y = dot_nt(weights, jnp.concatenate(wide + thin + thin, axis=0))
        first = mask_ref[row_start + i].astype(F32)
        second = mask_ref[row_start + i + 24].astype(F32)
        wide_mask = jnp.where(lane < 64, first, second) * wide_cols
        thin_mask = jnp.where(lane % 64 < 32, first, second) * thin_cols
        left = y[0:128, 0:128] * jax.nn.sigmoid(y[256:384, 0:128])
        right = y[128:256, 0:128] * jax.nn.sigmoid(y[384:512, 0:128])
        both_p = jnp.where(low, y[0:128, 128:256], y[128:256, 128:256])
        both_g = jnp.where(low, y[256:384, 128:256], y[384:512, 128:256])
        scr[pl.ds(i, 128, stride=72), :] = left * wide_mask
        scr[pl.ds(i + 24, 128, stride=72), :] = right * wide_mask
        scr[pl.ds(i + 48, 128, stride=72), :] = both_p * jax.nn.sigmoid(both_g) * thin_mask

    for m in range(4):
        if m < 3:
            norm_block(2 * m + 2)
            norm_block(2 * m + 3)
        for k in range(6):
            one(6 * m + k)
    out_copies = []
    for n in range(8):
        part = scr[1152 * n : 1152 * n + 1152, :].reshape(16, 72, 128)
        out_ref[16 * n : 16 * n + 16] = part.astype(BF16)
        copy = pltpu.make_async_copy(
            out_ref.at[pl.ds(16 * n, 16)], out_hbm.at[pl.ds(16 * n, 16)], out_sems.at[9 + n]
        )
        copy.start()
        out_copies.append(copy)
    wait_all(normed_copies + out_copies)


def token_kernel(
    tokens_ref, grad_ref, gain_ref, wq_ref, wk_ref, wv_ref, wo_ref, core_ref, keep_ref, send_ref, w_scr, wo_scr, norm_scr
):
    even = core_ref[0] == 0

    @pl.when(pl.program_id(0) == 0)
    def _():
        gap = jnp.zeros((768, 16), F32)
        for n, ref in enumerate((wq_ref, wk_ref, wv_ref)):
            w = ref[...].astype(F32)
            w = jnp.concatenate([w[:, 0:48], gap, w[:, 48:96], gap], axis=1)
            w_scr[:, 128 * n : 128 * n + 128] = jnp.where(even, w, roll(w, 64)).astype(BF16)
        first, second = wo_ref[0:48, :], wo_ref[48:96, :]
        wo_scr[0:48, :] = jnp.where(even, first, second)
        wo_scr[64:112, :] = jnp.where(even, second, first)
        wo_scr[48:64, :] = jnp.zeros((16, 768), BF16)
        wo_scr[112:128, :] = jnp.zeros((16, 768), BF16)

    gain = gain_ref[...]

    def norm_block(block, carry):
        rows = pl.ds(pl.multiple_of(block * 96, 32), 96)
        norm_scr[rows, :] = layer_norm(tokens_ref[0, rows, :].astype(F32), gain).astype(BF16)
        return carry

    lax.fori_loop(0, 8, norm_block, 0)
    low = lanes_of(768) < 64
    query = matmul(norm_scr[...], w_scr[:, 0:128])
    grads = dot_nt(grad_ref[0], wo_scr[...])
    keep_ref[0, 0] = jnp.where(low, query, roll(grads, 64)).astype(BF16)
    send_ref[0, 0] = jnp.where(low, roll(query, 64), grads).astype(BF16)
    key = matmul(norm_scr[...], w_scr[:, 128:256])
    value = matmul(norm_scr[...], w_scr[:, 256:384])
    for ref, full in (
        (keep_ref, jnp.where(low, key, roll(value, 64))),
        (send_ref, jnp.where(low, roll(key, 64), value)),
    ):
        full = full.astype(BF16)
        for q in range(8):
            ref[0, 1, 64 * q : 64 * q + 64] = full[96 * q : 96 * q + 64]
            ref[0, 1, 512 + 32 * q : 544 + 32 * q] = full[96 * q + 64 : 96 * q + 96]


def unpack_wide(first, second, low):
    top = jnp.where(low, first, roll(second, 64))
    bottom = jnp.where(low, roll(first, 64), second)
    return top, bottom


def product_kernel(in_hbm, out_hbm, in_ref, out_ref, l_scr, r_scr, in_sems, out_sems):
    copies = start_all(
        [
            pltpu.make_async_copy(
                in_hbm.at[:, pl.ds(4 * u, 4)], in_ref.at[:, pl.ds(4 * u, 4)], in_sems.at[u]
            )
            for u in range(2)
        ]
    )
    lane = lanes_of(384)
    low = lane < 64

    def put(dst, column, full):
        full = full.reshape(768, 128).astype(BF16)
        if dst is l_scr:
            dst[:, column : column + 128] = full
        else:
            for q in range(8):
                dst[64 * q : 64 * q + 64, column : column + 128] = full[96 * q : 96 * q + 64]
                dst[512 + 32 * q : 544 + 32 * q, column : column + 128] = full[96 * q + 64 : 96 * q + 96]

    def stack(halves):
        return jnp.concatenate([h.reshape(16, 24, 128) for h in halves], axis=1)

    def part(value, start):
        return value[:, start : start + 24].reshape(384, 128)

    for u in range(2):
        copies[u].wait()
        blocks = [in_ref[:, 4 * u + v].astype(F32) for v in range(4)]
        for p in range(2):
            for dst, start in ((l_scr, 0), (r_scr, 24)):
                halves = unpack_wide(part(blocks[2 * p], start), part(blocks[2 * p + 1], start), low)
                put(dst, (2 * u + p) * 128, stack(halves))
        thin = [part(b, 48) for b in blocks]
        for dst, base in ((l_scr, 0), (r_scr, 2)):
            halves = []
            for a in range(2):
                parts = [roll(thin[v], 32 * (v - base - a)) for v in range(4)]
                lower = jnp.where(lane < 32, parts[0], parts[1])
                upper = jnp.where(lane < 96, parts[2], parts[3])
                halves.append(jnp.where(low, lower, upper))
            put(dst, 512 + u * 128, stack(halves))
    out_copies = []
    for b in range(4):
        product = dot_nt(l_scr[192 * b : 192 * b + 192, :], r_scr[...])
        pack_rows(product, out_ref, 4 * b, 4)
        copy = pltpu.make_async_copy(
            out_ref.at[pl.ds(4 * b, 4)], out_hbm.at[pl.ds(4 * b, 4)], out_sems.at[b]
        )
        copy.start()
        out_copies.append(copy)
    wait_all(out_copies)


def pack_rows(full, out_ref, first, count):
    low = lanes_of(count * 24) < 64
    lane = lanes_of(count * 16)
    for q in range(8):
        tile = full[:, 128 * (q // 2) : 128 * (q // 2) + 128].reshape(count, 48, 128)
        top = tile[:, 0:24].reshape(count * 24, 128)
        bottom = tile[:, 24:48].reshape(count * 24, 128)
        if q % 2 == 0:
            wide = jnp.where(low, top, roll(bottom, 64))
        else:
            wide = jnp.where(low, roll(top, 64), bottom)
        tile = full[:, 512 + 128 * (q // 4) : 640 + 128 * (q // 4)].reshape(count, 48, 128)
        thin = [
            roll(tile[:, 16 * m : 16 * m + 16].reshape(count * 16, 128), 32 * (m - q % 4))
            for m in range(3)
        ]
        thin = jnp.where(lane < 32, thin[0], jnp.where(lane < 64, thin[1], thin[2]))
        piece = jnp.concatenate(
            [wide.reshape(count, 24, 128), thin.reshape(count, 16, 128)], axis=1
        )
        out_ref[pl.ds(first, count), q] = piece.astype(BF16)


def transition_kernel(
    mixed_hbm, ring_hbm, far_hbm, place_ref, token_hbm, gain_ref, gate_hbm, up_hbm, down_hbm, out_hbm,
    mixed_ref, wo_ref, token_ref, gate_ref, up_ref, down_ref, x_ref, out_ref, sems, wo_sems, out_sems,
):
    pairs = ((mixed_hbm, mixed_ref), (token_hbm, token_ref), (gate_hbm, gate_ref), (up_hbm, up_ref), (down_hbm, down_ref))
    wo_copies = []
    for far, src in ((0, ring_hbm), (1, far_hbm)):
        for n in range(8):
            core = lax.rem(place_ref[2] + far, 2)
            high = lax.rem(place_ref[4] + n // 4, 2)
            block = core * 8 + high * 4 + lax.rem(place_ref[5] + n, 4)
            wo_copies.append(
                pltpu.make_async_copy(src.at[n], wo_ref.at[block, pl.ds(0, 48)], wo_sems.at[8 * far + n])
            )
    start_all(wo_copies)
    copies = start_all([pltpu.make_async_copy(src, dst, sems.at[n]) for n, (src, dst) in enumerate(pairs)])
    wo_ref[:, 48:64, :] = jnp.zeros((16, 16, 768), BF16)
    copies[0].wait()
    low = lanes_of(144) < 64
    for n in range(8):
        first = mixed_ref[2 * n].reshape(144, 128).astype(F32)
        second = mixed_ref[2 * n + 1].reshape(144, 128).astype(F32)
        top, bottom = unpack_wide(first, second, low)
        x_ref[0:144, 128 * n : 128 * n + 128] = top.astype(BF16)
        x_ref[144:288, 128 * n : 128 * n + 128] = bottom.astype(BF16)
    wait_all(wo_copies)
    attn = matmul(x_ref[...], wo_ref[...].reshape(1024, 768))
    copies[1].wait()
    token = jnp.concatenate([token_ref[s, 48 * half : 48 * half + 48] for half in range(2) for s in range(3)], axis=0)
    state = token.astype(F32) + attn
    fed = layer_norm(state, gain_ref[...]).astype(BF16)
    wait_all(copies[2:])
    refined = state
    for n in range(3):
        cols = slice(512 * n, 512 * n + 512)
        hidden = jax.nn.silu(matmul(fed, gate_ref[:, cols])) * matmul(fed, up_ref[:, cols])
        refined = refined + matmul(hidden.astype(BF16), down_ref[cols, :])
    for half in range(2):
        for s in range(3):
            at = 144 * half + 48 * s
            out_ref[s, 48 * half : 48 * half + 48] = refined[at : at + 48]
    copy = pltpu.make_async_copy(out_ref, out_hbm, out_sems.at[0])
    copy.start()
    copy.wait()


def wide_places(i):
    return [(i, 0, 64), (i + 24, 0, 64)]


def thin_places(i):
    return [(i + 16 * m, 64, 32) for m in range(3)]


def update_kernel(
    t_hbm, pair_hbm, gate_hbm, w_ref, tri_gain_ref, bias_gain_ref, bp_ref, out_hbm, bias_hbm,
    scr, b_scr, t_ref, pair_ref, gate_ref, out_ref, bias_ref, t_sems, sems, out_sems,
):
    t_copies = start_all(
        [
            pltpu.make_async_copy(t_hbm.at[pl.ds(32 * n, 32)], t_ref.at[pl.ds(32 * n, 32)], t_sems.at[n])
            for n in range(4)
        ]
    )
    copies = start_all(
        [
            pltpu.make_async_copy(pair_hbm, pair_ref, sems.at[0]),
            pltpu.make_async_copy(gate_hbm, gate_ref, sems.at[1]),
        ]
    )
    for n in range(4):
        t_copies[n].wait()
        scr[1280 * n : 1280 * n + 1280, :] = t_ref[32 * n : 32 * n + 32].astype(F32).reshape(1280, 128)
    wait_all(copies)
    weight = w_ref[...]
    tri_gain = tri_gain_ref[...]
    bias_gain = bias_gain_ref[...]
    bias_proj = bp_ref[...]

    def group(positions, places):
        normed = []
        for position in positions:
            tri = scr[pl.ds(position, 128, stride=40), :]
            middle = tri - jnp.mean(tri, axis=0, keepdims=True)
            spread_of = jnp.mean(middle * middle, axis=0, keepdims=True)
            normed.append((middle * lax.rsqrt(spread_of + 1e-05) * tri_gain).astype(BF16))
        update = dot_tn(jnp.concatenate(normed, axis=1), weight)
        fed = []
        for n, spots in enumerate(places):
            at = 128 * n
            for row, start, size in spots:
                cols = pl.ds(start, size)
                new = pair_ref[row, cols, :].astype(F32) + gate_ref[row, cols, :] * update[at : at + size]
                out_ref[row, cols, :] = new
                fed.append(layer_norm(new, bias_gain).astype(BF16))
                at += size
            if len(spots) == 3:
                fed.append(fed[-1])
        bias = dot_nt(bias_proj, jnp.concatenate(fed, axis=0))
        for n, position in enumerate(positions):
            b_scr[pl.ds(position, 16, stride=40), :] = bias[:, 128 * n : 128 * n + 128]

    par, par2 = UPDATE_PAR, THIN_PAR

    def wide(i, carry):
        group([par * i + n for n in range(par)], [wide_places(par * i + n) for n in range(par)])
        return carry

    def thin(i, carry):
        group([24 + par2 * i + n for n in range(par2)], [thin_places(par2 * i + n) for n in range(par2)])
        return carry

    lax.fori_loop(0, 24 // par, wide, 0)
    out_copies = [
        pltpu.make_async_copy(out_ref.at[:, pl.ds(c, n)], out_hbm.at[:, pl.ds(c, n)], out_sems.at[8 + k])
        for k, (c, n) in enumerate(((0, 64), (64, 32)))
    ]
    out_copies[0].start()
    lax.fori_loop(0, 16 // par2, thin, 0)
    out_copies[1].start()
    bias_ref[...] = b_scr[...].reshape(16, 40, 128).astype(BF16)
    out_copies += start_all(
        [pltpu.make_async_copy(bias_ref, bias_hbm.at[n], out_sems.at[n]) for n in range(8)]
    )
    wait_all(out_copies)


def unpack_bias(bias_ref, copies, put):
    low = lanes_of(384) < 64
    lane = lanes_of(256)
    for u in range(2):
        copies[u].wait()
        blocks = [bias_ref[:, 4 * u + v].astype(F32) for v in range(4)]
        for p in range(2):
            halves = unpack_wide(
                blocks[2 * p][:, 0:24].reshape(384, 128),
                blocks[2 * p + 1][:, 0:24].reshape(384, 128),
                low,
            )
            put((2 * u + p) * 128, jnp.concatenate([h.reshape(16, 24, 128) for h in halves], axis=1))
        thin = [b[:, 24:40].reshape(256, 128) for b in blocks]
        thirds = []
        for m in range(3):
            parts = [roll(thin[v], 32 * (v - m)) for v in range(4)]
            lower = jnp.where(lane < 32, parts[0], parts[1])
            upper = jnp.where(lane < 96, parts[2], parts[3])
            thirds.append(jnp.where(lane < 64, lower, upper).reshape(16, 16, 128))
        put(512 + u * 128, jnp.concatenate(thirds, axis=1))


def pair_copies(keep_hbm, recv_hbm, pairs, sems):
    return start_all(
        [
            pltpu.make_async_copy(src, pairs.at[pl.ds(3 * n, 3)], sems.at[n])
            for n, src in enumerate((keep_hbm, recv_hbm))
        ]
    )


def forward_kernel(
    bias_hbm, keep_hbm, recv_hbm, chain_row_ref, chain_col_ref, place_ref, weight_ref,
    mixed_hbm, full_hbm, pairs, bias_ref, mixed_ref, full_ref, sems, in_sems, out_sems,
):
    bias_copies = start_all(
        [
            pltpu.make_async_copy(
                bias_hbm.at[:, pl.ds(4 * u, 4)], bias_ref.at[:, pl.ds(4 * u, 4)], in_sems.at[u]
            )
            for u in range(2)
        ]
    )
    copies = pair_copies(keep_hbm, recv_hbm, pairs, sems)
    core = place_ref[2]
    head_weight = weight_ref[place_ref[3]] * LOG2E

    def put(column, full):
        same = chain_row_ref[...] == chain_col_ref[:, column : column + 128]
        full_ref[:, column : column + 128] = full.reshape(768, 128) * LOG2E + jnp.where(
            same, head_weight, 0.0
        )

    unpack_bias(bias_ref, bias_copies, put)
    stats = slice(768, 896)
    full_copy = pltpu.make_async_copy(full_ref.at[:, 0:768], full_hbm.at[:, 0:768], out_sems.at[0])
    full_copy.start()
    full_ref[:, stats] = jnp.zeros((768, 128), F32)
    wait_all(copies)
    low_all = lanes_of(768) < 64
    lane = lanes_of(FORWARD_ROWS)
    low = lane < 64
    thin_low = lanes_of(48) < 64
    blocks = 768 // FORWARD_ROWS
    shares = FORWARD_ROWS // 96

    def block(s, b, owner, slot):
        both = pairs[s, 1]
        keys = jnp.where(low_all, both, jnp.zeros_like(both))
        rows = pl.ds(pl.multiple_of(b * FORWARD_ROWS, 32), FORWARD_ROWS)
        asked = pairs[s, 0, rows, :]
        weights = jnp.exp2(dot_nt(asked, keys) * SCALE + full_ref[rows, 0:768])
        inverse = 1.0 / jnp.sum(weights, axis=-1, keepdims=True)
        mixed = matmul((weights * inverse).astype(BF16), both)
        center = jnp.sum(jnp.where(low, 0.0, asked.astype(F32) * mixed), axis=-1, keepdims=True)
        full_ref[rows, stats] = jnp.where(
            lane == s, inverse, jnp.where(lane == s + 64, center, full_ref[rows, stats])
        )
        for n in range(shares):
            mixed_ref[owner * 8 + b * shares + n, slot] = jnp.where(
                thin_low, roll(mixed[96 * n : 96 * n + 48], 64), mixed[96 * n + 48 : 96 * n + 96]
            ).astype(BF16)

    def step(i, carry):
        half = i // blocks
        owner = jnp.where(half == 0, core, 1 - core)
        for n in range(3):
            block(3 * half + n, i % blocks, owner, n)
        return carry

    def mixed_copy(owner, sem):
        part = pl.ds(owner * 8, 8)
        return pltpu.make_async_copy(mixed_ref.at[part], mixed_hbm.at[part], out_sems.at[sem])

    lax.fori_loop(0, blocks, step, 0)
    mixed_copy(core, 1).start()
    lax.fori_loop(blocks, 2 * blocks, step, 0)
    mixed_copy(1 - core, 2).start()
    stats_copy = pltpu.make_async_copy(full_ref.at[:, stats], full_hbm.at[:, stats], out_sems.at[3])
    stats_copy.start()
    mixed_copy(core, 1).wait()
    mixed_copy(1 - core, 2).wait()
    full_copy.wait()
    stats_copy.wait()


def backward_kernel(full_hbm, keep_hbm, recv_hbm, grad_hbm, pairs, full_ref, grad_ref, sems, in_sems, out_sems):
    copies = pair_copies(keep_hbm, recv_hbm, pairs, sems)
    blocks = 768 // BACKWARD_ROWS

    def full_copy(b):
        rows = pl.ds(pl.multiple_of(b * BACKWARD_ROWS, 32), BACKWARD_ROWS)
        return pltpu.make_async_copy(full_hbm.at[rows], full_ref.at[rows], in_sems.at[b])

    start_all([full_copy(b) for b in range(blocks)])
    wait_all(copies)
    low_all = lanes_of(768) < 64

    def row_block(b, carry):
        full_copy(b).wait()
        rows = pl.ds(pl.multiple_of(b * BACKWARD_ROWS, 32), BACKWARD_ROWS)
        total = None
        for s in range(6):
            both = pairs[s, 1]
            keys = jnp.where(low_all, both, jnp.zeros_like(both))
            values = jnp.where(low_all, jnp.zeros_like(both), both)
            asked = pairs[s, 0, rows, :]
            inverse = full_ref[rows, 768 + s : 769 + s]
            center = full_ref[rows, 832 + s : 833 + s]
            probs = jnp.exp2(dot_nt(asked, keys) * SCALE + full_ref[rows, 0:768]) * inverse
            score_grad = probs * (dot_nt(asked, values) - center)
            total = score_grad if total is None else total + score_grad
        pack_rows(total, grad_ref, b * (BACKWARD_ROWS // 48), BACKWARD_ROWS // 48)
        grad_copy(b).start()
        return carry

    def grad_copy(b):
        part = pl.ds(b * (BACKWARD_ROWS // 48), BACKWARD_ROWS // 48)
        return pltpu.make_async_copy(grad_ref.at[part], grad_hbm.at[part], out_sems.at[b])

    lax.fori_loop(0, blocks, row_block, 0)
    wait_all([grad_copy(b) for b in range(blocks)])


def pair_grad_kernel(in_hbm, w_ref, out_hbm, scr, in_ref, out_ref, in_sems, out_sems):
    copies = start_all([pltpu.make_async_copy(in_hbm.at[n], in_ref.at[n], in_sems.at[n]) for n in range(8)])
    total = None
    for n in range(8):
        copies[n].wait()
        part = in_ref[n].astype(F32)
        total = part if total is None else total + part
    scr[...] = total.reshape(640, 128)
    weight = w_ref[...]

    def group(positions, places):
        grad = jnp.concatenate([scr[pl.ds(p, 16, stride=40), :] for p in positions], axis=1)
        high = grad.astype(BF16)
        rest = grad - high.astype(F32)
        middle = rest.astype(BF16)
        least = (rest - middle.astype(F32)).astype(BF16)
        rows = dot_tn(jnp.concatenate([high, middle, least], axis=0), weight)
        for n, spots in enumerate(places):
            at = 128 * n
            for row, start, size in spots:
                out_ref[row, pl.ds(start, size), :] = rows[at : at + size]
                at += size

    par, par2 = UPDATE_PAR, THIN_PAR

    def wide(i, carry):
        group([par * i + n for n in range(par)], [wide_places(par * i + n) for n in range(par)])
        return carry

    def thin(i, carry):
        group([24 + par2 * i + n for n in range(par2)], [thin_places(par2 * i + n) for n in range(par2)])
        return carry

    lax.fori_loop(0, 24 // par, wide, 0)
    out_copies = [
        pltpu.make_async_copy(out_ref.at[:, pl.ds(c, n)], out_hbm.at[:, pl.ds(c, n)], out_sems.at[k])
        for k, (c, n) in enumerate(((0, 64), (64, 32)))
    ]
    out_copies[0].start()
    lax.fori_loop(0, 16 // par2, thin, 0)
    out_copies[1].start()
    wait_all(out_copies)


def column_order(value, axis):
    shape = value.shape
    split = value.reshape(shape[:axis] + (8, 96) + shape[axis + 1 :])
    wide = lax.slice_in_dim(split, 0, 64, axis=axis + 1).reshape(shape[:axis] + (512,) + shape[axis + 1 :])
    thin = lax.slice_in_dim(split, 64, 96, axis=axis + 1).reshape(shape[:axis] + (256,) + shape[axis + 1 :])
    return jnp.concatenate([wide, thin], axis=axis)


def memory(space):
    return pl.BlockSpec(memory_space=space)


VMEM, SMEM, HBM = memory(pltpu.VMEM), memory(pltpu.SMEM), memory(pltpu.HBM)
TILE = (48, 96, 128)
PACKED = (16, 8, 40, 128)


def shape(dims, dtype=BF16):
    return jax.ShapeDtypeStruct(dims, dtype)


def dma(count):
    return pltpu.SemaphoreType.DMA((count,))


def run_project(*args):
    return call(
        project_kernel,
        (shape((128, 72, 128)), shape((4608, 128))),
        args,
        [
            pltpu.VMEM((128 * 72, 128), F32),
            pltpu.VMEM((4608, 128), BF16),
            pltpu.VMEM((4608, 128), BF16),
            pltpu.VMEM((4, 128, 128), BF16),
            pltpu.VMEM((128, 72, 128), BF16),
            pltpu.SMEM((768,), jnp.int32),
            dma(9),
            dma(5),
            dma(17),
        ],
        "project",
        flops=2 * 512 * 128 * 6144,
        nbytes=5_000_000,
        spaces=[HBM, VMEM] + [HBM] * 5,
        out_specs=(HBM, HBM),
    )


def run_tokens(samples, *args):
    part = shape((samples, 2, 768, 128))
    token_block = pl.BlockSpec((1, 768, 768), lambda s: (s, 0, 0))
    part_block = pl.BlockSpec((1, 2, 768, 128), lambda s: (s, 0, 0, 0))
    return call(
        token_kernel,
        (part, part),
        args,
        [pltpu.VMEM((768, 384), BF16), pltpu.VMEM((128, 768), BF16), pltpu.VMEM((768, 768), BF16)],
        "tokens",
        flops=2 * 2304 * 768 * 512,
        nbytes=12_000_000,
        spaces=[token_block, token_block] + [VMEM] * 5 + [SMEM],
        grid=(samples,),
        out_specs=(part_block, part_block),
    )


def run_product(*args):
    return call(
        product_kernel,
        shape(PACKED),
        args,
        [
            pltpu.VMEM((16, 8, 72, 128), BF16),
            pltpu.VMEM(PACKED, BF16),
            pltpu.VMEM((768, 768), BF16),
            pltpu.VMEM((768, 768), BF16),
            dma(2),
            dma(4),
        ],
        "product",
        flops=2 * 768**3,
        nbytes=4_000_000,
        spaces=[HBM],
        out_specs=HBM,
        mib=50,
    )


def run_update(*args):
    return call(
        update_kernel,
        (shape(TILE, F32), shape((8, 16, 40, 128))),
        args,
        [
            pltpu.VMEM((128 * 40, 128), F32),
            pltpu.VMEM((16 * 40, 128), F32),
            pltpu.VMEM((128, 40, 128), BF16),
            pltpu.VMEM(TILE, BF16),
            pltpu.VMEM(TILE, F32),
            pltpu.VMEM(TILE, F32),
            pltpu.VMEM((16, 40, 128), BF16),
            dma(4),
            dma(2),
            dma(10),
        ],
        "update",
        flops=2 * 128 * 128 * 5120,
        nbytes=9_000_000,
        spaces=[HBM, HBM, HBM] + [VMEM] * 4,
        out_specs=(HBM, HBM),
        mib=52,
    )


def run_forward(*args):
    return call(
        forward_kernel,
        (shape((16, 3, 48, 128)), shape((768, 896), F32)),
        args,
        [
            pltpu.VMEM((6, 2, 768, 128), BF16),
            pltpu.VMEM(PACKED, BF16),
            pltpu.VMEM((16, 3, 48, 128), BF16),
            pltpu.VMEM((768, 896), F32),
            dma(2),
            dma(2),
            dma(4),
        ],
        "forward",
        flops=6 * 4 * 768 * 768 * 128,
        nbytes=12_000_000,
        spaces=[HBM, HBM, HBM, VMEM, VMEM, SMEM, SMEM],
        out_specs=(HBM, HBM),
        mib=51,
    )


def run_backward(*args):
    return call(
        backward_kernel,
        shape(PACKED),
        args,
        [
            pltpu.VMEM((6, 2, 768, 128), BF16),
            pltpu.VMEM((768, 896), F32),
            pltpu.VMEM(PACKED, BF16),
            dma(2),
            dma(768 // BACKWARD_ROWS),
            dma(768 // BACKWARD_ROWS),
        ],
        "backward",
        flops=6 * 4 * 768 * 768 * 128,
        nbytes=12_000_000,
        spaces=[HBM] * 3,
        out_specs=HBM,
    )


def run_pair_grad(*args):
    return call(
        pair_grad_kernel,
        shape(TILE, F32),
        args,
        [
            pltpu.VMEM((16 * 40, 128), F32),
            pltpu.VMEM((8, 16, 40, 128), BF16),
            pltpu.VMEM(TILE, F32),
            dma(8),
            dma(2),
        ],
        "pair_grad",
        flops=2 * 48 * 128 * 5120,
        nbytes=4_000_000,
        spaces=[HBM, VMEM],
        out_specs=HBM,
        mib=52,
    )


def run_transition(*args):
    return call(
        transition_kernel,
        shape((3, 96, 768), F32),
        args,
        [
            pltpu.VMEM((16, 3, 48, 128), BF16),
            pltpu.VMEM((16, 64, 768), BF16),
            pltpu.VMEM((3, 96, 768), BF16),
            pltpu.VMEM((768, 1536), BF16),
            pltpu.VMEM((768, 1536), BF16),
            pltpu.VMEM((1536, 768), BF16),
            pltpu.VMEM((288, 1024), BF16),
            pltpu.VMEM((3, 96, 768), F32),
            dma(5),
            dma(16),
            dma(1),
        ],
        "transition",
        flops=2 * 288 * 768 * (1024 + 3 * 1536),
        nbytes=12_000_000,
        spaces=[HBM] * 3 + [SMEM, HBM, VMEM] + [HBM] * 3,
        out_specs=HBM,
        mib=51,
    )


def exchange(value, axes):
    return lax.all_to_all(value, axes, 0, 0, tiled=True)


SWAP = [(0, 1), (1, 0)]


def gather_ring(half):
    ring = [half] + [lax.ppermute(half, "z", [(i, (i - k) % 4) for i in range(4)]) for k in range(1, 4)]
    return jnp.stack(ring)


def body(
    pair_state,
    pair_mask,
    chain_ids,
    tokens,
    grad_attn,
    norm_pair,
    proj_left,
    gate_left,
    proj_right,
    gate_right,
    gate_out,
    norm_tri,
    tri_out,
    norm_bias,
    bias_proj,
    chain_weight,
    norm_tokens,
    w_query,
    w_key,
    w_value,
    w_out,
    norm_ff,
    ff_gate,
    ff_up,
    ff_down,
):
    tile_rows, tile_cols, channels = pair_state.shape
    tile_size = tile_rows * tile_cols
    row_start = lax.axis_index(ROWS) * tile_rows
    col_index = lax.axis_index(COLS)
    col_start = col_index * tile_cols
    pair_flat = pair_state.reshape(tile_size, channels)

    core_index = lax.axis_index("core")
    place = jnp.stack(
        [row_start, col_start, core_index, 2 * col_index + core_index, lax.axis_index("xh"), lax.axis_index("z")]
    ).astype(jnp.int32)

    sides, normed = run_project(
        pair_flat, norm_pair, proj_left, proj_right, gate_left, gate_right, pair_mask
    )
    sides_in = exchange(sides, ALL)

    samples, seq_len, model_width = tokens.shape
    keep, send = run_tokens(
        samples, tokens, grad_attn, norm_tokens.astype(F32)[None], w_query, w_key, w_value, w_out, place[2:3]
    )
    normed, w_out_late = lax.optimization_barrier((normed, w_out))
    ring = gather_ring(lax.dynamic_slice_in_dim(w_out_late, core_index * HD, HD, 0))
    sides_in, keep, send, ring = lax.optimization_barrier((sides_in, keep, send, ring))
    recv = lax.ppermute(send, "core", SWAP)
    products = run_product(sides_in.reshape(16, 8, 72, 128))
    tri_in = exchange(products.reshape(128, 40, 128), ALL)
    share_len = seq_len // 8
    token_share = lax.dynamic_slice_in_dim(tokens, col_index * share_len, share_len, 1)
    gate = jax.nn.sigmoid(matmul(normed, gate_out)).reshape(pair_state.shape)
    heads_first = jnp.transpose(bias_proj.T.reshape(8, 2, 128), (1, 0, 2)).reshape(16, 128)
    tri_gain = jnp.broadcast_to(norm_tri.astype(F32)[:, None], (128, 128))
    bias_gain = norm_bias.astype(F32)[None]
    ff_gain = norm_ff.astype(F32)[None]
    triple = jnp.concatenate([heads_first] * 3, axis=0)
    chain_row, chain_col = chain_ids[:, None], column_order(chain_ids[None], 1)
    (
        tri_in, recv, token_share, gate, heads_first, tri_gain, bias_gain, ff_gain, triple, chain_row, chain_col
    ) = lax.optimization_barrier(
        (
            tri_in, recv, token_share, gate, heads_first, tri_gain, bias_gain, ff_gain, triple, chain_row, chain_col
        )
    )

    pair_out, bias = run_update(
        tri_in,
        pair_state,
        gate,
        tri_out,
        tri_gain,
        bias_gain,
        heads_first,
    )
    bias_in = exchange(bias.reshape(128, 40, 128), ALL).reshape(PACKED)

    bias_in, ring = lax.optimization_barrier((bias_in, ring))
    rings = jnp.concatenate([ring, lax.ppermute(ring, "xh", SWAP)], axis=0)

    mixed, full_bias = run_forward(
        bias_in, keep, recv, chain_row, chain_col, place, chain_weight
    )
    mixed, rings = lax.optimization_barrier((mixed, rings))
    far_rings = lax.ppermute(rings, "core", SWAP)
    mixed_in = exchange(mixed, ("core",) + COLS)
    bias_grad = run_backward(full_bias, keep, recv)
    grad_in = exchange(bias_grad.reshape(128, 40, 128), ALL).reshape(8, 16, 40, 128)

    refined = run_transition(
        mixed_in, rings, far_rings, place, token_share, ff_gain, ff_gate, ff_up, ff_down
    )

    pair_grad = run_pair_grad(grad_in, triple)
    return (pair_out, refined, pair_grad)


def solution(mesh):
    fine = Mesh(mesh.devices.reshape(2, 4, 2, 2, 4), ALL)
    pair = P(ROWS, COLS, None)
    sample_rows = P(ROWS, None, None)
    return jax.shard_map(
        body,
        mesh=fine,
        in_specs=(pair, P(), P(), sample_rows, sample_rows)
        + (P(),) * 12
        + (P(None, COLS),) * 3
        + (P(COLS, None),)
        + (P(),) * 4,
        out_specs=(pair, pair, pair),
        check_vma=False,
    )
```
